32 devices in a mesh: dp: 8 (over z, y), section: 4 (over x, core).
Axes of the slice: x: 2, y: 2, z: 4, core: 2. Of those that a mesh axis runs over, the one named last changes fastest.
Arguments:
- hidden_in: bfloat16 [4096, 768], P('dp'), may hold values from -6 to 6
- out_grad: float32 [4096, 768], P('dp'), may hold values from -6 to 6
- seq_counts: int32 [8, 2], P('dp'), may hold values from 1 to 2, as said below
- segment_ids: int32 [32, 128], P('dp'), may hold values from 0 to 3, never falling along the last dimension, each value on 1 to 64 neighbouring positions
- proj: bfloat16 [4, 768, 3072], P('section'), may hold values from -8 to 8
- proj_master: float32 [4, 768, 3072], P('section', 'dp'), may hold values from -8 to 8
- proj_m: float32 [4, 768, 3072], P('section', 'dp'), may hold values from -5 to 5
- proj_v: float32 [4, 768, 3072], P('section', 'dp'), may hold values from 0.01 to 10
- down: bfloat16 [2, 3072, 768], P(None, 'section'), may hold values from -0.109375 to 0.109375
- down_master: float32 [2, 3072, 768], P(None, 'section', 'dp'), may hold values from -0.109375 to 0.109375
- down_m: float32 [2, 3072, 768], P(None, 'section', 'dp'), may hold values from -5 to 5
- down_v: float32 [2, 3072, 768], P(None, 'section', 'dp'), may hold values from 0.01 to 10
- vectors: float32 [2, 12, 768], replicated, may hold values from -1 to 1.5
- vec_m: float32 [2, 12, 768], replicated, may hold values from -5 to 5
- vec_v: float32 [2, 12, 768], replicated, may hold values from 0.01 to 10
Outputs:
- section_out: bfloat16 [4, 4096, 768], P('section', 'dp')
- section_in_grad: float32 [4, 4096, 768], P('section', 'dp')
- proj_grad: float32 [4, 768, 3072], P('section', 'dp')
- proj_master_new: float32 [4, 768, 3072], P('section', 'dp')
- proj_m_new: float32 [4, 768, 3072], P('section', 'dp')
- proj_v_new: float32 [4, 768, 3072], P('section', 'dp')
- proj_copy: bfloat16 [4, 768, 3072], P('section')
- down_grad: float32 [2, 3072, 768], P(None, 'section', 'dp')
- down_master_new: float32 [2, 3072, 768], P(None, 'section', 'dp')
- down_m_new: float32 [2, 3072, 768], P(None, 'section', 'dp')
- down_v_new: float32 [2, 3072, 768], P(None, 'section', 'dp')
- down_copy: bfloat16 [2, 3072, 768], P(None, 'section')
- vec_grad: float32 [2, 12, 768], replicated
- vec_m_new: float32 [2, 12, 768], replicated
- vec_v_new: float32 [2, 12, 768], replicated
The draws below stay inside these ranges and needn't reach their ends.
Inputs may be any that keep to these rules, and one draw needn't show every extreme that they name: The first seq_counts[g, b] slots of micro-batch b of group g are live; some micro-batch of some group is full. `segment_ids`: document numbers never fall along a sequence; each document has 1 to 64 tokens.
All inputs are finite; a program needn't handle non-finite values.
Results may differ from the reference program's by a relative error of at most 0.02.
Values may be sent and summed in bfloat16 or wider, within the bound.
No kernel may reach another device: no remote copies, remote signals or barrier semaphores. Data moves between devices by JAX's collectives and lax.ppermute only.
A program may use at most 1.875 GiB of HBM per device.

```python
import math
import jax
import jax.numpy as jnp
import numpy as np
from jax import lax

D = 768
HEADS = 12
FF = 3072
LEN = 128
MB = 2
CAP = 2
GROUPS = 8
SECTIONS = 4
SEQS = 32
TOKENS = 4096


def matrix_law(key):
    shape = (SECTIONS, D, 4 * D)
    base = jnp.clip(jax.random.normal(key, shape, jnp.float32), -5.0, 5.0) * D ** (-0.5)
    section_ids = lax.broadcasted_iota(jnp.int32, shape, 0)
    columns = lax.broadcasted_iota(jnp.int32, shape, 2)
    widened = (section_ids % 2 == 0) & (columns >= 3 * D)
    return jnp.where(widened, base * 8.0, base)


def draw_proj(key, part):
    key = jax.random.fold_in(key, 11)
    return matrix_law(key).astype(jnp.bfloat16)


def draw_proj_master(key, part):
    key = jax.random.fold_in(key, 12)
    shape = (SECTIONS, D, 4 * D)
    return jnp.clip(jax.random.normal(key, shape, jnp.float32), -5.0, 5.0) * (0.3 * D ** (-0.5))


def draw_vectors(key, part):
    key = jax.random.fold_in(key, 13)
    shape = (2, 12, D)
    noise = jnp.clip(jax.random.normal(key, shape, jnp.float32), -5.0, 5.0)
    row_ids = lax.broadcasted_iota(jnp.int32, shape, 1)
    gain_rows = (row_ids == 3) | (row_ids == 10)
    return jnp.where(gain_rows, 1.0 + 0.1 * noise, 0.2 * noise)


def draw_seq_counts(key, part):
    key = jax.random.fold_in(key, 14)
    count_key, pick_key = jax.random.split(key)
    counts_drawn = jax.random.randint(count_key, (GROUPS, MB), 1, CAP + 1)
    picked = jax.random.randint(pick_key, (), 0, GROUPS * MB)
    spots = lax.broadcasted_iota(jnp.int32, (GROUPS, MB), 0) * MB + lax.broadcasted_iota(jnp.int32, (GROUPS, MB), 1)
    return jnp.where(spots == picked, CAP, counts_drawn).astype(jnp.int32)


def block_levels(stream_key, shape, pieces, least, high):
    loudness = 1.0
    for axis_at, blocks in pieces:
        steps = jax.random.uniform(jax.random.fold_in(jax.random.fold_in(stream_key, 6), axis_at), (blocks,), jnp.float32, least / len(pieces), high / len(pieces))
        loudness = loudness * jnp.repeat(jnp.exp(steps), shape[axis_at] // blocks).reshape((-1,) + (1,) * (len(shape) - 1 - axis_at))
    return loudness


def length_profile(count, total, most, skew):
    weights = [(1 << 20) // math.isqrt(standing ** skew) + 1 for standing in range(2, count + 1)]
    spare, holding = total - most - (count - 1), [1] * (count - 1)
    while spare > 0:
        candidates = [i for i in range(count - 1) if holding[i] < most]
        whole, budget = sum([weights[i] for i in candidates]), spare
        for i in candidates:
            extra = min(most - holding[i], max(1, budget * weights[i] // whole), spare)
            holding[i] = holding[i] + extra
            spare = spare - extra
    return np.array([most] + holding)


def ragged(rng, amount, total, reach, slope):
    if amount == 2:
        one = jax.random.randint(rng, (), max(1, total - reach), min(reach, total - 1) + 1)
        return jnp.stack([one, total - one])
    tallies = jnp.asarray(length_profile(amount, total, reach, slope), jnp.int32)
    couples = (amount - 1) // 2
    source_of, receiver = tallies[1:1 + 2 * couples:2], tallies[2:2 + 2 * couples:2]
    slack = jnp.minimum(source_of - 1, reach - receiver)
    passed = jax.random.randint(jax.random.fold_in(rng, 1), (couples,), 0, 1 << 20) % (slack + 1)
    tallies = tallies.at[1:1 + 2 * couples:2].set(source_of - passed).at[2:2 + 2 * couples:2].set(receiver + passed)
    return tallies[jax.random.permutation(jax.random.fold_in(rng, 2), amount)]


def scatter_about(own_key, dims, spread, most, cuts=(), kind=jnp.bfloat16):
    entries = spread * jax.random.normal(own_key, dims, jnp.float32)
    if cuts:
        entries = entries * block_levels(own_key, dims, cuts, -0.22, 0.18)
    return jnp.clip(entries, -most, most).astype(kind)


def setup_inputs(seed: int = 0) -> dict:
    splits = jax.random.split(jax.random.key(seed), 16)
    hidden_in = scatter_about(splits[0], (TOKENS, D), 1.0, 6.0, ((0, 8),))
    out_grad = scatter_about(splits[1], (TOKENS, D), 1.0, 6.0, ((0, 8),), jnp.float32)
    seq_counts = draw_seq_counts(jax.random.fold_in(splits[15], 71), 0)
    segment_ids = jax.vmap(lambda own: jnp.searchsorted(jnp.cumsum(ragged(own, 4, LEN, LEN // 2, 0)), jnp.arange(LEN), side="right"))(jax.random.split(splits[3], SEQS)).reshape((SEQS, LEN)).astype(jnp.int32)
    proj = draw_proj(jax.random.fold_in(splits[15], 71), 0)
    proj_master = draw_proj_master(jax.random.fold_in(splits[15], 71), 0)
    proj_m = scatter_about(splits[6], (SECTIONS, D, FF), 1.0, 5.0, ((0, 4), (1, 8)), jnp.float32)
    proj_v = jnp.clip(jnp.exp(math.log(10.0) - 6.9077553 * jax.random.uniform(splits[7], (SECTIONS, D, FF), jnp.float32) ** block_levels(splits[7], (SECTIONS, D, FF), ((0, 4), (1, 8)), -0.2, 0.2)), 0.01, 10.0)
    down = scatter_about(splits[8], (2, FF, D), FF ** -0.5, 0.109375, ((1, 4),))
    down_master = scatter_about(splits[9], (2, FF, D), FF ** -0.5, 0.109375, ((1, 4), (2, 8)), jnp.float32)
    down_m = scatter_about(splits[10], (2, FF, D), 1.0, 5.0, ((1, 4), (2, 8)), jnp.float32)
    down_v = jnp.clip(jnp.exp(math.log(10.0) - 6.9077553 * jax.random.uniform(splits[11], (2, FF, D), jnp.float32) ** block_levels(splits[11], (2, FF, D), ((1, 4), (2, 8)), -0.2, 0.2)), 0.01, 10.0)
    vectors = draw_vectors(jax.random.fold_in(splits[15], 71), 0)
    vec_m = scatter_about(splits[13], (2, 12, D), 1.0, 5.0, (), jnp.float32)
    vec_v = jnp.clip(jnp.exp(jax.random.uniform(splits[14], (2, 12, D), jnp.float32, math.log(0.01), math.log(10.0))), 0.01, 10.0)
    return {"hidden_in": hidden_in, "out_grad": out_grad, "seq_counts": seq_counts, "segment_ids": segment_ids, "proj": proj, "proj_master": proj_master, "proj_m": proj_m, "proj_v": proj_v, "down": down, "down_master": down_master, "down_m": down_m, "down_v": down_v, "vectors": vectors, "vec_m": vec_m, "vec_v": vec_v}


highest = lax.Precision.HIGHEST
norm_eps = 1e-05
beta_one = 0.9
beta_two = 0.98
adam_eps = 1e-06
learn_rate = 0.001
weight_decay = 0.01
adam_step = 100.0

@jax.custom_vjp
def low(v):
    return lax.optimization_barrier(v.astype(jnp.bfloat16)).astype(jnp.float32)

@jax.custom_vjp
def low_back(v):
    return v

def low_keep(v):
    return (low(v), None)

def low_pass(kept, grad):
    return (grad,)

def back_keep(v):
    return (v, None)

def back_low(kept, grad):
    return (low(grad),)
low.defvjp(low_keep, low_pass)
low_back.defvjp(back_keep, back_low)

def norm_apply(residual_sum, gain, shift):
    centered = residual_sum - lax.optimization_barrier(jnp.mean(residual_sum, -1, keepdims=True))
    scale_inv = lax.rsqrt(lax.optimization_barrier(jnp.mean(centered * centered, -1, keepdims=True)) + norm_eps)
    return centered * scale_inv * gain + shift

def attend(hidden, documents, matrices, vector_rows):
    seq_count, seq_len, model_width = hidden.shape
    head_size = model_width // HEADS
    score_scale = head_size ** (-0.5)
    flat_rows = hidden.reshape(-1, model_width)
    joined_bias = jnp.concatenate([vector_rows[0], jnp.zeros_like(vector_rows[0]), vector_rows[1]])
    joined_proj = low(low_back(jnp.dot(flat_rows, matrices[:, :3 * model_width], precision=highest) + joined_bias))
    packed = joined_proj.reshape(seq_count, seq_len, 3, HEADS, head_size)
    queries = packed[:, :, 0]
    keys_part = packed[:, :, 1]
    values = packed[:, :, 2]
    scores = low_back(jnp.einsum('sqhd,skhd->shqk', queries, keys_part, precision=highest) * score_scale)
    same_doc = (documents[:, :, None] == documents[:, None, :])[:, None]
    scores = jnp.where(same_doc, scores, -1e+30)
    exponent = jnp.exp(scores - lax.optimization_barrier(jnp.max(scores, -1, keepdims=True)))
    attn_probs = exponent / lax.optimization_barrier(jnp.sum(exponent, -1, keepdims=True))
    probs_low = low(attn_probs)
    context = jnp.einsum('shqk,skhd->sqhd', probs_low, values, precision=highest).reshape(-1, model_width)
    context = low(low_back(context))
    branch_out = low_back(jnp.dot(context, matrices[:, 3 * model_width:], precision=highest) + vector_rows[2])
    return norm_apply(flat_rows + branch_out, vector_rows[3], vector_rows[4]).reshape(hidden.shape)

def feed(hidden, matrices, down_layer, vector_rows):
    model_width = hidden.shape[-1]
    flat_rows = hidden.reshape(-1, model_width)
    pre_act = low_back(jnp.dot(flat_rows, matrices, precision=highest) + vector_rows[5:9].reshape(-1))
    gelu_low = low(jax.nn.gelu(pre_act, approximate=False))
    branch_out = low_back(jnp.dot(gelu_low, down_layer, precision=highest) + vector_rows[9])
    return norm_apply(flat_rows + branch_out, vector_rows[10], vector_rows[11]).reshape(hidden.shape)

def chain(parameters, block_inputs, block_docs, block_live, block_shifts):
    proj_full, down_full, vector_all = parameters
    hidden = block_inputs + block_shifts[0]
    collected = []
    for section_index in range(SECTIONS):
        layer_index = section_index // 2
        if section_index % 2 == 0:
            result = attend(hidden, block_docs, proj_full[section_index], vector_all[layer_index])
        else:
            result = feed(hidden, proj_full[section_index], down_full[layer_index], vector_all[layer_index])
        result = result * block_live[:, None, None]
        collected.append(result)
        if section_index + 1 < SECTIONS:
            hidden = low(low_back(result)) + block_shifts[section_index + 1]
    return jnp.stack(collected)

def adam_apply(weight_now, first_moment, second_moment, gradient, decay_rate):
    first_new = beta_one * first_moment + (1.0 - beta_one) * gradient
    second_new = beta_two * second_moment + (1.0 - beta_two) * gradient * gradient
    update = first_new / (1.0 - beta_one ** adam_step) / (jnp.sqrt(second_new / (1.0 - beta_two ** adam_step)) + adam_eps)
    return (weight_now - learn_rate * (update + decay_rate * weight_now), first_new, second_new)

def reference(hidden_in, out_grad, seq_counts, segment_ids, proj, proj_master, proj_m, proj_v, down, down_master, down_m, down_v, vectors, vec_m, vec_v):
    block_seqs = MB * CAP
    inputs = hidden_in.astype(jnp.float32).reshape(GROUPS, block_seqs, LEN, D)
    cotangent = out_grad.reshape(GROUPS, block_seqs, LEN, D)
    documents = segment_ids.reshape(GROUPS, block_seqs, LEN)
    slot_ids = jnp.arange(block_seqs, dtype=jnp.int32) % CAP
    live_rows = (slot_ids[None, :] < jnp.repeat(seq_counts, CAP, axis=1)).astype(jnp.float32)
    parameters = (proj.astype(jnp.float32), down.astype(jnp.float32), vectors)
    input_shifts = jnp.zeros((GROUPS, SECTIONS, block_seqs, LEN, D), jnp.float32)

    def forward(parameters, input_shifts):

        def group_block(block_item):
            return chain(parameters, *block_item)
        return lax.map(jax.checkpoint(group_block), (inputs, documents, live_rows, input_shifts))
    section_outputs, pull_back = jax.vjp(forward, parameters, input_shifts)
    seed_grad = jnp.zeros_like(section_outputs).at[:, SECTIONS - 1].set(cotangent)
    grad_params, grad_inputs = pull_back(seed_grad)
    grad_proj, grad_down, grad_vectors = grad_params

    def arrange(grid):
        return jnp.swapaxes(grid, 0, 1).reshape(SECTIONS, GROUPS * block_seqs * LEN, D)
    section_out = arrange(section_outputs).astype(jnp.bfloat16)
    section_in_grad = arrange(grad_inputs)
    proj_grad = grad_proj / GROUPS
    down_grad = grad_down / GROUPS
    vec_grad = grad_vectors / GROUPS
    proj_new, proj_m_new, proj_v_new = adam_apply(proj_master, proj_m, proj_v, proj_grad, weight_decay)
    down_new, down_m_new, down_v_new = adam_apply(down_master, down_m, down_v, down_grad, weight_decay)
    vec_moments = adam_apply(vectors, vec_m, vec_v, vec_grad, 0.0)
    return (section_out, section_in_grad, proj_grad, proj_new, proj_m_new, proj_v_new, proj_new.astype(jnp.bfloat16), down_grad, down_new, down_m_new, down_v_new, down_new.astype(jnp.bfloat16), vec_grad, vec_moments[1], vec_moments[2])
```

```python
import functools
import math

import jax
import jax.numpy as jnp
from jax import lax
from jax.experimental import pallas as pl
from jax.experimental.pallas import tpu as pltpu
from jax.sharding import PartitionSpec as P

HEADS = 12
HEAD_PAIRS = HEADS // 2

norm_eps = 1e-05
beta_one = 0.9
beta_two = 0.98
adam_eps = 1e-06
learn_rate = 0.001
weight_decay = 0.01
adam_step = 100.0

VMEM_LIMIT = 56 * 1024 * 1024
low = jnp.bfloat16
full = jnp.float32

vmem = pl.BlockSpec(memory_space=pltpu.VMEM)
smem = pl.BlockSpec(memory_space=pltpu.SMEM)
anywhere = pl.BlockSpec(memory_space=pl.ANY)


def dot(a, b):
    return lax.dot_general(a, b, (((1,), (0,)), ((), ())), preferred_element_type=full)


def dot_right(a, b):
    return lax.dot_general(a, b, (((1,), (1,)), ((), ())), preferred_element_type=full)


def dot_left(a, b):
    return lax.dot_general(a, b, (((0,), (0,)), ((), ())), preferred_element_type=full)


def row_mean(z):
    return jnp.mean(z, -1, keepdims=True)


def norm_rows(z):
    centered = z - row_mean(z)
    inv = lax.rsqrt(row_mean(centered * centered) + norm_eps)
    return centered * inv, inv


def norm_rows_back(upstream, normed, inv, gain):
    scaled = upstream * gain
    return inv * (scaled - row_mean(scaled) - normed * row_mean(scaled * normed))


def live_rows(rows, live_count, seq_len):
    return lax.broadcasted_iota(jnp.int32, (rows, 1), 0) < live_count * seq_len


def column_sum(block):
    return jnp.sum(block, 0, keepdims=True)


def call(kernel, outs, ins, specs, scratch=(), flops=0, moved=0):
    return pl.pallas_call(
        kernel,
        out_shape=outs,
        in_specs=specs,
        out_specs=jax.tree.map(lambda _: vmem, outs),
        scratch_shapes=list(scratch),
        compiler_params=pltpu.CompilerParams(vmem_limit_bytes=VMEM_LIMIT),
        cost_estimate=pl.CostEstimate(flops=flops, bytes_accessed=moved, transcendentals=0),
    )(*ins)


def pair_masks(seq_len):
    first = lax.broadcasted_iota(jnp.int32, (seq_len, 128), 1) < 64
    return first


def spread_pair(block, first):
    zero = jnp.zeros_like(block)
    return jnp.concatenate([jnp.where(first, block, zero), jnp.where(first, zero, block)], 0)


def pair_probs(q, keys_two, same_doc, scale, seq_len):
    scores = dot_right(q, keys_two) * scale
    parts = []
    for half in range(2):
        part = jnp.where(same_doc, scores[:, half * seq_len : (half + 1) * seq_len], -1e30)
        exponent = jnp.exp(part - jnp.max(part, -1, keepdims=True))
        parts.append(exponent / jnp.sum(exponent, -1, keepdims=True))
    return parts


def pick_weights(core, own_hbm, other_hbm, attn_buf, feed_buf, sems):
    if attn_buf is not None:
        @pl.when(core == 0)
        def _():
            pltpu.make_async_copy(own_hbm, attn_buf, sems.at[0]).start()

        @pl.when(core != 0)
        def _():
            pltpu.make_async_copy(other_hbm, attn_buf, sems.at[0]).start()

    if feed_buf is not None:
        @pl.when(core == 0)
        def _():
            pltpu.make_async_copy(other_hbm, feed_buf, sems.at[1]).start()

        @pl.when(core != 0)
        def _():
            pltpu.make_async_copy(own_hbm, feed_buf, sems.at[1]).start()


def forward_first(
    scal, h_ref, doc_row, doc_col, vec, own_hbm, other_hbm,
    qkv_ref, ctx_ref, n_ref, r_ref, h_next, act_ref, slope_ref,
    attn_buf, feed_buf, sems,
):
    rows, width = h_ref.shape
    seq_len = doc_row.shape[1]
    seqs = rows // seq_len
    scale = (width // HEADS) ** (-0.5)
    pick_weights(scal[0], own_hbm, other_hbm, attn_buf, feed_buf, sems)
    hidden = h_ref[...]
    pltpu.make_async_copy(own_hbm, attn_buf, sems.at[0]).wait()
    for part in range(3):
        cols = slice(part * width, (part + 1) * width)
        block = dot(hidden, attn_buf[:, cols])
        if part == 0:
            block = block + vec[0:1, :]
        if part == 2:
            block = block + vec[1:2, :]
        qkv_ref[:, cols] = block.astype(low)
    first = pair_masks(seq_len)
    for s in range(seqs):
        at = slice(s * seq_len, (s + 1) * seq_len)
        same_doc = doc_col[at, :] == doc_row[s : s + 1, :]
        for p in range(HEAD_PAIRS):
            q = qkv_ref[at, p * 128 : (p + 1) * 128]
            keys_two = spread_pair(qkv_ref[at, width + p * 128 : width + (p + 1) * 128], first)
            values_two = spread_pair(
                qkv_ref[at, 2 * width + p * 128 : 2 * width + (p + 1) * 128], first
            )
            probs = pair_probs(q, keys_two, same_doc, scale, seq_len)
            probs_low = jnp.concatenate([x.astype(low) for x in probs], 1)
            ctx_ref[at, p * 128 : (p + 1) * 128] = dot(probs_low, values_two).astype(low)
    z = hidden.astype(full) + (dot(ctx_ref[...], attn_buf[:, 3 * width :]) + vec[2:3, :])
    normed, inv = norm_rows(z)
    n_ref[...] = normed
    r_ref[...] = inv
    live = live_rows(rows, scal[2], seq_len)
    nxt = jnp.where(live, normed * vec[3:4, :] + vec[4:5, :], 0.0).astype(low)
    h_next[...] = nxt
    pltpu.make_async_copy(own_hbm, feed_buf, sems.at[1]).wait()
    for k in range(4):
        pre = dot(nxt, feed_buf[:, k * width : (k + 1) * width]) + vec[5 + k : 6 + k, :]
        half_cdf = 0.5 * (1.0 + lax.erf(pre * (1.0 / math.sqrt(2.0))))
        act_ref[k] = (pre * half_cdf).astype(low)
        slope_ref[k] = (
            half_cdf + pre * jnp.exp(-0.5 * pre * pre) * (1.0 / math.sqrt(2.0 * math.pi))
        ).astype(slope_ref.dtype)


def forward_second(scal, h_ref, act_ref, vec, d0, d1, d2, d3, h_next, n_ref, r_ref, *, seq_len):
    rows, width = h_ref.shape
    section = scal[1]
    total = h_ref[...].astype(full) + vec[9:10, :]
    for m, block in enumerate((d0, d1, d2, d3)):
        total = total + dot(act_ref[section ^ m], block[...])
    normed, inv = norm_rows(total)
    n_ref[...] = normed
    r_ref[...] = inv
    live = live_rows(rows, scal[2], seq_len)
    h_next[...] = jnp.where(live, normed * vec[10:11, :] + vec[11:12, :], 0.0).astype(low)


def backward_second(
    scal, e_ref, n_ref, r_ref, slope_ref, vec, d0, d1, d2, d3, own_hbm, other_hbm,
    db_ref, dpre_ref, dh_ref, sums, feed_buf, sems, *, seq_len,
):
    rows, width = n_ref.shape
    section = scal[1]
    pick_weights(scal[0], own_hbm, other_hbm, None, feed_buf, sems)
    upstream = jnp.where(live_rows(rows, scal[2], seq_len), e_ref[...], 0.0)
    normed = n_ref[...]
    dz = norm_rows_back(upstream, normed, r_ref[...], vec[10:11, :])
    db = dz.astype(low)
    db_ref[...] = db
    sums[4:5, :] = column_sum(db.astype(full))
    sums[5:6, :] = column_sum(upstream * normed)
    sums[6:7, :] = column_sum(upstream)
    sums[7:8, :] = jnp.zeros((1, width), full)
    for m, block in enumerate((d0, d1, d2, d3)):
        at = section ^ m
        dact = dot_right(db, block[...])
        dpre = (dact * slope_ref[at].astype(full)).astype(low)
        dpre_ref[at] = dpre
    total = dz
    pltpu.make_async_copy(own_hbm, feed_buf, sems.at[1]).wait()
    for k in range(4):
        dpre = dpre_ref[k]
        sums[k : k + 1, :] = column_sum(dpre.astype(full))
        total = total + dot_right(dpre, feed_buf[:, k * width : (k + 1) * width])
    dh_ref[...] = total


def backward_first(
    scal, e_ref, n_ref, r_ref, qkv_ref, doc_row, doc_col, vec, own_hbm, other_hbm,
    dqkvd_ref, dh_ref, sums, attn_buf, dctx_buf, sems,
):
    rows, width = n_ref.shape
    seq_len = doc_row.shape[1]
    seqs = rows // seq_len
    scale = (width // HEADS) ** (-0.5)
    pick_weights(scal[0], own_hbm, other_hbm, attn_buf, None, sems)
    upstream = e_ref[...].astype(low).astype(full)
    upstream = jnp.where(live_rows(rows, scal[2], seq_len), upstream, 0.0)
    normed = n_ref[...]
    dz = norm_rows_back(upstream, normed, r_ref[...], vec[3:4, :])
    da = dz.astype(low)
    dqkvd_ref[3] = da
    sums[2:3, :] = column_sum(da.astype(full))
    sums[3:4, :] = column_sum(upstream * normed)
    sums[4:5, :] = column_sum(upstream)
    sums[5:8, :] = jnp.zeros((3, width), full)
    pltpu.make_async_copy(own_hbm, attn_buf, sems.at[0]).wait()
    dctx_buf[...] = dot_right(da, attn_buf[:, 3 * width :]).astype(low)
    first = pair_masks(seq_len)
    for s in range(seqs):
        at = slice(s * seq_len, (s + 1) * seq_len)
        same_doc = doc_col[at, :] == doc_row[s : s + 1, :]
        for p in range(HEAD_PAIRS):
            here = slice(p * 128, (p + 1) * 128)
            q = qkv_ref[at, here]
            keys_two = spread_pair(qkv_ref[at, width + p * 128 : width + (p + 1) * 128], first)
            values_two = spread_pair(
                qkv_ref[at, 2 * width + p * 128 : 2 * width + (p + 1) * 128], first
            )
            dctx = dctx_buf[at, here]
            probs = pair_probs(q, keys_two, same_doc, scale, seq_len)
            probs_low = jnp.concatenate([x.astype(low) for x in probs], 1)
            dv_two = dot_left(probs_low, dctx)
            dqkvd_ref[2, at, here] = jnp.where(
                first, dv_two[:seq_len, :], dv_two[seq_len:, :]
            ).astype(low)
            dprobs = dot_right(dctx, values_two)
            dscores = []
            for half in range(2):
                part = dprobs[:, half * seq_len : (half + 1) * seq_len]
                inner = jnp.sum(probs[half] * part, -1, keepdims=True)
                dscores.append((probs[half] * (part - inner)).astype(low))
            dscores = jnp.concatenate(dscores, 1)
            dqkvd_ref[0, at, here] = (dot(dscores, keys_two) * scale).astype(low)
            dk_two = dot_left(dscores, q)
            dqkvd_ref[1, at, here] = (
                jnp.where(first, dk_two[:seq_len, :], dk_two[seq_len:, :]) * scale
            ).astype(low)
    total = dz
    for k in range(3):
        block = dqkvd_ref[k]
        if k != 1:
            sums[k // 2 : k // 2 + 1, :] = column_sum(block.astype(full))
        total = total + dot_right(block, attn_buf[:, k * width : (k + 1) * width])
    dh_ref[...] = total


def down_gradient(act_own, act_other, db_own, db_other, out):
    for t in range(2):
        out[t] = (
            dot_left(db_own[...], act_own[t]) + dot_left(db_other[...], act_other[t])
        ).astype(low)


def weight_gradient(left_own, left_other, right_own, right_other, out):
    out[...] = (
        dot_left(left_own[...], right_own[...]) + dot_left(left_other[...], right_other[...])
    ).astype(low)


def swap(block, axis, mask):
    return lax.ppermute(block, axis, [(i, i ^ mask) for i in range(lax.axis_size(axis))])


def adam_apply(weight_now, first_moment, second_moment, gradient, decay_rate):
    first_new = beta_one * first_moment + (1.0 - beta_one) * gradient
    second_new = beta_two * second_moment + (1.0 - beta_two) * gradient * gradient
    update = (
        first_new
        / (1.0 - beta_one**adam_step)
        / (jnp.sqrt(second_new / (1.0 - beta_two**adam_step)) + adam_eps)
    )
    return (weight_now - learn_rate * (update + decay_rate * weight_now), first_new, second_new)


def masks_of(count):
    return [1 << b for b in range(count.bit_length() - 1)]


def pick(block, at):
    return lax.dynamic_index_in_dim(block, at, 1, keepdims=False)


class Exchange:
    def __init__(self):
        self.count = lax.axis_size("dp")
        self.index = lax.axis_index("dp")
        self.masks = masks_of(self.count)
        self.token = None
        self.state = {}
        self.results = {}

    def bit(self, mask):
        return (self.index // mask) % 2

    def begin(self, name, partial, finish):
        rows, cols = partial.shape
        blocks = partial.reshape(self.count // 2, 2, rows // self.count, cols)
        bit = self.bit(self.masks[0])
        got = swap(pick(blocks, 1 - bit), "dp", self.masks[0])
        self.state[name] = (0, pick(blocks, bit), got, finish)

    def order(self, *arrays):
        if self.token is None:
            self.token = jnp.zeros((8, 128), full)
        *arrays, self.token = lax.optimization_barrier((*arrays, self.token))
        return arrays

    def advance(self, name):
        stage, keep, got, finish = self.state[name]
        steps = len(self.masks)
        keep, got = self.order(keep, got)
        if stage < steps:
            total = keep.astype(full) + got.astype(full)
            if stage < steps - 1:
                total = total.astype(low)
                blocks = total.reshape(total.shape[0] // 2, 2, *total.shape[1:])
                bit = self.bit(self.masks[stage + 1])
                keep, send = self.order(pick(blocks, bit), pick(blocks, 1 - bit))
                got = swap(send, "dp", self.masks[stage + 1])
            else:
                (keep,) = self.order(finish(total[0])[None])
                got = swap(keep, "dp", self.masks[-1])
        else:
            bit = self.bit(self.masks[2 * steps - 1 - stage])
            both = jnp.where(bit == 0, jnp.stack([keep, got], 1), jnp.stack([got, keep], 1))
            keep = both.reshape(-1, *keep.shape[1:])
            (keep,) = self.order(keep)
            if stage == 2 * steps - 1:
                self.results[name] = keep.reshape(-1, keep.shape[-1])
            else:
                got = swap(keep, "dp", self.masks[2 * steps - 2 - stage])
        self.state[name] = (stage + 1, keep, got, finish)


def shards(
    hidden_in, out_grad, seq_counts, segment_ids, proj, proj_master, proj_m, proj_v,
    down, down_master, down_m, down_v, vectors, vec_m, vec_v,
):
    group_count = lax.axis_size("dp")
    section = lax.axis_index("section")
    core, layer = section % 2, section // 2
    width = hidden_in.shape[1]
    seq_len = segment_ids.shape[1]
    slots = segment_ids.shape[0] // 2
    rows = slots * seq_len
    wide = proj.shape[2]
    at_first = layer == 0

    def shape(dims, kind):
        return jax.ShapeDtypeStruct(dims, kind)

    own_w = proj[0]
    other_w = swap(own_w, "section", 1)
    d0 = lax.dynamic_index_in_dim(down, layer, 0, keepdims=False)
    d2 = swap(lax.dynamic_index_in_dim(down, 1 - layer, 0, keepdims=False), "section", 2)
    d1 = swap(d0, "section", 1)
    d3 = swap(d2, "section", 1)
    downs = (d0, d1, d2, d3)
    vec = lax.dynamic_index_in_dim(vectors, layer, 0, keepdims=False)

    own_in = lax.dynamic_slice_in_dim(hidden_in, core * rows, rows, 0)
    own_cot = lax.dynamic_slice_in_dim(out_grad, core * rows, rows, 0)
    docs = lax.dynamic_slice_in_dim(segment_ids, core * slots, slots, 0)
    doc_col = docs.reshape(rows, 1)
    live_count = lax.dynamic_index_in_dim(seq_counts[0], core, 0, keepdims=False)
    scal = jnp.stack([core, section, live_count]).astype(jnp.int32)

    weight_sems = pltpu.SemaphoreType.DMA((2,))
    weight_buf = pltpu.VMEM((width, wide), low)
    flops_one = 2 * rows * width * wide

    def run_first(hidden):
        return call(
            forward_first,
            [
                shape((rows, 3 * width), low), shape((rows, width), low),
                shape((rows, width), full), shape((rows, 1), full), shape((rows, width), low),
                shape((4, rows, width), low), shape((4, rows, width), low),
            ],
            (scal, hidden, docs, doc_col, vec, own_w, other_w),
            [smem, vmem, vmem, vmem, vmem, anywhere, anywhere],
            (weight_buf, weight_buf, weight_sems),
            flops=2 * flops_one, moved=15 << 20,
        )

    def run_second(hidden, act):
        return call(
            functools.partial(forward_second, seq_len=seq_len),
            [shape((rows, width), low), shape((rows, width), full), shape((rows, 1), full)],
            (scal, hidden, act, vec, *downs),
            [smem] + [vmem] * 7,
            flops=flops_one, moved=8 << 20,
        )

    def hop(block, towards):
        route = [(0, 2), (1, 3)] if towards else [(2, 0), (3, 1)]
        return lax.ppermute(block, "section", route)

    first = run_first(own_in)
    h_two = run_second(first[4], first[5])[0]
    layer_in = jnp.where(at_first, own_in, hop(h_two, True))
    qkv, ctx, n_one, r_one, h_one, act, slope = run_first(layer_in)
    h_two, n_two, r_two = run_second(h_one, act)

    def by_core(at_zero, at_one):
        return jnp.where(core == 0, at_zero, at_one)

    kept_left = (by_core(layer_in, h_one), by_core(ctx, h_one), by_core(h_one, h_two))
    sent_left = jnp.stack(
        [by_core(h_one, layer_in), by_core(h_one, ctx), by_core(h_two, h_one)]
    )
    got_left = swap(sent_left, "section", 1)
    act_pairs = act.reshape(2, 2, rows, width)
    act_kept = pick(act_pairs, core)
    act_got = swap(pick(act_pairs, 1 - core), "section", 1)

    def run_back_second(upstream):
        return call(
            functools.partial(backward_second, seq_len=seq_len),
            [
                shape((rows, width), low), shape((4, rows, width), low),
                shape((rows, width), full), shape((8, width), full),
            ],
            (scal, upstream, n_two, r_two, slope, vec, *downs, own_w, other_w),
            [smem] + [vmem] * 9 + [anywhere] * 2,
            (weight_buf, weight_sems),
            flops=2 * flops_one, moved=16 << 20,
        )

    def run_back_first(upstream):
        return call(
            backward_first,
            [shape((4, rows, width), low), shape((rows, width), full), shape((8, width), full)],
            (scal, upstream, n_one, r_one, qkv, docs, doc_col, vec, own_w, other_w),
            [smem] + [vmem] * 7 + [anywhere] * 2,
            (weight_buf, pltpu.VMEM((rows, width), low), weight_sems),
            flops=2 * flops_one, moved=10 << 20,
        )

    def run_down(db):
        return call(
            down_gradient,
            shape((2, width, width), low),
            (act_kept, act_got, db, swap(db, "section", 1)),
            [vmem] * 4,
            flops=2 * flops_one, moved=6 << 20,
        )

    db, dpre, dh_two, sums_two = run_back_second(own_cot)
    dqkvd, dh_one, sums_one = run_back_first(dh_two)
    early_down = run_down(db)
    early = jnp.where(at_first, hop(early_down[0], False), early_down[1])

    upstream = jnp.where(at_first, hop(dh_one.astype(low), False).astype(full), own_cot)
    db, dpre, dh_two, sums_two = run_back_second(upstream)
    late_down = run_down(db)
    late = jnp.where(at_first, late_down[0], hop(late_down[1], True))
    dqkvd, dh_one, sums_one = run_back_first(dh_two)

    kept_right = by_core(dqkvd, dpre)
    got_right = swap(by_core(dpre, dqkvd), "section", 1)
    kept_grad = by_core(dh_one, dh_two)
    got_grad = swap(by_core(dh_two, dh_one), "section", 1)

    moments = {}

    def finish_proj(k):
        cols = slice(k * width, (k + 1) * width)

        def finish(total):
            grad = total / group_count
            new = adam_apply(
                proj_master[0, :, cols], proj_m[0, :, cols], proj_v[0, :, cols], grad, weight_decay
            )
            moments["proj", k] = (grad, *new)
            return new[0].astype(low)

        return finish

    def finish_down(at):
        def finish(total):
            grad = total.T / group_count
            new = adam_apply(down_master[at], down_m[at], down_v[at], grad, weight_decay)
            moments["down", at] = (grad, *new)
            return new[0].astype(low).T

        return finish

    exchange = Exchange()
    stages = 2 * len(exchange.masks)
    exchange.begin("early", early, finish_down(1))
    for _ in range(stages):
        exchange.advance("early")
    names = []
    for k in range(4):
        lhs = 0 if k < 3 else 1
        partial = call(
            weight_gradient,
            shape((width, width), low),
            (kept_left[lhs], got_left[lhs], kept_right[k], got_right[k]),
            [vmem] * 4,
            flops=flops_one // 2, moved=4 << 20,
        )
        exchange.begin(k, partial, finish_proj(k))
        names.append(k)
    exchange.begin("late", late, finish_down(0))
    names.append("late")
    plan = []
    for place, name in enumerate(names):
        at = 13.0 * (place + 1)
        for stage in range(stages - 1):
            plan.append((at, place, name))
            at += 10.5
        plan.append((max(at, 13.0 * (len(names) + place)) + 13.0, place, name))
    for _, _, name in sorted(plan, key=lambda item: item[:2]):
        exchange.advance(name)

    sums = jnp.concatenate([sums_one[:5], sums_two[:7]], 0)
    sums = sums + swap(sums, "section", 1)
    for mask in masks_of(group_count):
        sums = sums + swap(sums, "dp", mask)
    other_sums = swap(sums, "section", 2)
    vec_grad = jnp.where(
        at_first, jnp.stack([sums, other_sums]), jnp.stack([other_sums, sums])
    ) / group_count
    vec_moments = adam_apply(vectors, vec_m, vec_v, vec_grad, 0.0)

    def in_order(kept, got):
        return by_core(jnp.concatenate([kept, got], 0), jnp.concatenate([got, kept], 0))[None]

    proj_parts = [
        jnp.concatenate([moments["proj", k][i] for k in range(4)], 1)[None] for i in range(4)
    ]
    down_parts = [jnp.stack([moments["down", at][i] for at in range(2)]) for i in range(4)]
    proj_copy = jnp.concatenate([exchange.results[k] for k in range(4)], 1)[None]
    down_copy = jnp.stack([exchange.results["late"].T, exchange.results["early"].T])
    return (
        in_order(kept_left[2], got_left[2]),
        in_order(kept_grad, got_grad),
        *proj_parts,
        proj_copy,
        *down_parts,
        down_copy,
        vec_grad,
        vec_moments[1],
        vec_moments[2],
    )


def solution(mesh):
    shared = P("section", "dp", None)
    split = P(None, "section", "dp")
    placed = (
        P("dp", None), P("dp", None), P("dp", None), P("dp", None),
        P("section", None, None), shared, shared, shared,
        P(None, "section", None), split, split, split, P(), P(), P(),
    )
    return jax.shard_map(
        shards,
        mesh=mesh,
        in_specs=placed,
        out_specs=(
            shared, shared, shared, shared, shared, shared,
            P("section", None, None), split, split, split, split,
            P(None, "section", None), P(), P(), P(),
        ),
        check_vma=False,
    )
```

```python
import functools
import math

import jax
import jax.numpy as jnp
from jax import lax
from jax.experimental import pallas as pl
from jax.experimental.pallas import tpu as pltpu
from jax.sharding import PartitionSpec as P

HEADS = 12
HEAD_PAIRS = HEADS // 2

norm_eps = 1e-05
beta_one = 0.9
beta_two = 0.98
adam_eps = 1e-06
learn_rate = 0.001
weight_decay = 0.01
adam_step = 100.0

low = jnp.bfloat16
full = jnp.float32

vmem = pl.BlockSpec(memory_space=pltpu.VMEM)
smem = pl.BlockSpec(memory_space=pltpu.SMEM)
anywhere = pl.BlockSpec(memory_space=pl.ANY)
hbm = pl.BlockSpec(memory_space=pltpu.HBM)


def dot(a, b):
    return lax.dot_general(a, b, (((1,), (0,)), ((), ())), preferred_element_type=full)


def dot_right(a, b):
    return lax.dot_general(a, b, (((1,), (1,)), ((), ())), preferred_element_type=full)


def dot_left(a, b):
    return lax.dot_general(a, b, (((0,), (0,)), ((), ())), preferred_element_type=full)


def row_mean(z):
    return jnp.mean(z, -1, keepdims=True)


def norm_rows(z):
    centered = z - row_mean(z)
    inv = lax.rsqrt(row_mean(centered * centered) + norm_eps)
    return centered * inv, inv


def norm_rows_back(upstream, normed, inv, gain):
    scaled = upstream * gain
    return inv * (scaled - row_mean(scaled) - normed * row_mean(scaled * normed))


def live_rows(rows, live_count, seq_len):
    return lax.broadcasted_iota(jnp.int32, (rows, 1), 0) < live_count * seq_len


def column_sum(block):
    return jnp.sum(block, 0, keepdims=True)


def call(kernel, outs, ins, specs, scratch=(), grid=(), out_specs=None, limit=12, cost=0, aliases=None):
    return pl.pallas_call(
        kernel,
        grid=grid,
        out_shape=outs,
        in_specs=specs,
        out_specs=out_specs or jax.tree.map(lambda _: vmem, outs),
        scratch_shapes=list(scratch),
        input_output_aliases=aliases or {},
        compiler_params=pltpu.CompilerParams(vmem_limit_bytes=limit << 20),
        cost_estimate=pl.CostEstimate(flops=cost * 10**9, bytes_accessed=0, transcendentals=0),
    )(*ins)


def pair_masks(seq_len):
    first = lax.broadcasted_iota(jnp.int32, (seq_len, 128), 1) < 64
    return first


def spread_pair(block, first):
    zero = jnp.zeros_like(block)
    return jnp.concatenate([jnp.where(first, block, zero), jnp.where(first, zero, block)], 0)


def pair_probs(q, keys_two, same_doc, scale, seq_len):
    scores = dot_right(q, keys_two) * scale
    parts = []
    for half in range(2):
        part = jnp.where(same_doc, scores[:, half * seq_len : (half + 1) * seq_len], -1e30)
        exponent = jnp.exp(part - jnp.max(part, -1, keepdims=True))
        parts.append(exponent / jnp.sum(exponent, -1, keepdims=True))
    return parts


class Blocks:
    def __init__(self, *refs):
        self.refs = refs

    def __call__(self, k):
        if len(self.refs) > 1:
            return self.refs[k][...]
        (ref,) = self.refs
        width = ref.shape[1] // 4
        return ref[:, k * width : (k + 1) * width]


def attend_forward(
    hidden, doc_row, doc_col, vec, attn, live, qkv_ref, ctx_ref, n_ref, r_ref, h_next
):
    rows, width = hidden.shape
    seq_len = doc_row.shape[1]
    scale = (width // HEADS) ** (-0.5)
    for part in range(3):
        block = dot(hidden, attn(part))
        if part == 0:
            block = block + vec[0:1, :]
        if part == 2:
            block = block + vec[1:2, :]
        qkv_ref[:, part * width : (part + 1) * width] = block.astype(low)
    first = pair_masks(seq_len)
    for s in range(rows // seq_len):
        at = slice(s * seq_len, (s + 1) * seq_len)
        same_doc = doc_col[at, :] == doc_row[s : s + 1, :]
        for p in range(HEAD_PAIRS):
            q, k, v = (
                qkv_ref[at, part * width + p * 128 : part * width + (p + 1) * 128]
                for part in range(3)
            )
            probs = pair_probs(q, spread_pair(k, first), same_doc, scale, seq_len)
            probs_low = jnp.concatenate([x.astype(low) for x in probs], 1)
            ctx_ref[at, p * 128 : (p + 1) * 128] = dot(probs_low, spread_pair(v, first)).astype(low)
    z = hidden.astype(full) + (dot(ctx_ref[...], attn(3)) + vec[2:3, :])
    normed, inv = norm_rows(z)
    n_ref[...] = normed
    r_ref[...] = jnp.broadcast_to(inv, r_ref.shape)
    h_next[...] = jnp.where(live, normed * vec[3:4, :] + vec[4:5, :], 0.0).astype(low)


def feed_up(h_ref, vec, feed, act_ref, slope_ref):
    hidden = h_ref[...]
    for k in range(4):
        pre = dot(hidden, feed(k)) + vec[5 + k : 6 + k, :]
        half_cdf = 0.5 * (1.0 + lax.erf(pre * (1.0 / math.sqrt(2.0))))
        act_ref[k] = (pre * half_cdf).astype(low)
        slope_ref[k] = (
            half_cdf + pre * jnp.exp(-0.5 * pre * pre) * (1.0 / math.sqrt(2.0 * math.pi))
        ).astype(slope_ref.dtype)


def feed_down(h_ref, act_ref, section, vec, downs, live, h_next, n_ref, r_ref):
    total = h_ref[...].astype(full) + vec[9:10, :]
    for m in range(4):
        total = total + dot(act_ref[section ^ m], downs(m))
    normed, inv = norm_rows(total)
    n_ref[...] = normed
    r_ref[...] = jnp.broadcast_to(inv, r_ref.shape)
    h_next[...] = jnp.where(live, normed * vec[10:11, :] + vec[11:12, :], 0.0).astype(low)


def feed_back(
    upstream, n_ref, r_ref, slope_ref, section, vec, downs, feed, db_ref, dpre_ref, sums, loads=()
):
    width = n_ref.shape[1]
    normed = n_ref[...]
    dz = norm_rows_back(upstream, normed, r_ref[:, :1], vec[10:11, :])
    db = dz.astype(low)
    if db_ref is not None:
        db_ref[...] = db
        sums[4:5, :] = column_sum(db.astype(full))
        sums[5:6, :] = column_sum(upstream * normed)
        sums[6:7, :] = column_sum(upstream)
        sums[7:8, :] = jnp.zeros((1, width), full)
    for m in range(4):
        at = section ^ m
        dact = dot_right(db, downs(m))
        if m == 0 and loads:
            loads[0].wait()
        dpre_ref[at] = (dact * slope_ref[at].astype(full)).astype(low)
    total = dz
    if loads:
        loads[1].wait()
    for k in range(4):
        dpre = dpre_ref[k]
        if db_ref is not None:
            sums[k : k + 1, :] = column_sum(dpre.astype(full))
        total = total + dot_right(dpre, feed(k))
    return total


def attend_back(
    upstream, n_ref, r_ref, qkv_ref, doc_row, doc_col, vec, attn, dqkvd_ref, dctx_buf, sums
):
    rows, width = n_ref.shape
    seq_len = doc_row.shape[1]
    scale = (width // HEADS) ** (-0.5)
    normed = n_ref[...]
    dz = norm_rows_back(upstream, normed, r_ref[:, :1], vec[3:4, :])
    da = dz.astype(low)
    dqkvd_ref[3] = da
    if sums is not None:
        sums[2:3, :] = column_sum(da.astype(full))
        sums[3:4, :] = column_sum(upstream * normed)
        sums[4:5, :] = column_sum(upstream)
        sums[5:8, :] = jnp.zeros((3, width), full)
    dctx_buf[...] = dot_right(da, attn(3)).astype(low)
    first = pair_masks(seq_len)
    for s in range(rows // seq_len):
        at = slice(s * seq_len, (s + 1) * seq_len)
        same_doc = doc_col[at, :] == doc_row[s : s + 1, :]
        for p in range(HEAD_PAIRS):
            here = slice(p * 128, (p + 1) * 128)
            q, k, v = (
                qkv_ref[at, part * width + p * 128 : part * width + (p + 1) * 128]
                for part in range(3)
            )
            keys_two = spread_pair(k, first)
            dctx = dctx_buf[at, here]
            probs = pair_probs(q, keys_two, same_doc, scale, seq_len)
            probs_low = jnp.concatenate([x.astype(low) for x in probs], 1)
            dv_two = dot_left(probs_low, dctx)
            dqkvd_ref[2, at, here] = jnp.where(
                first, dv_two[:seq_len, :], dv_two[seq_len:, :]
            ).astype(low)
            dprobs = dot_right(dctx, spread_pair(v, first))
            dscores = []
            for half in range(2):
                part = dprobs[:, half * seq_len : (half + 1) * seq_len]
                inner = jnp.sum(probs[half] * part, -1, keepdims=True)
                dscores.append((probs[half] * (part - inner)).astype(low))
            dscores = jnp.concatenate(dscores, 1)
            dqkvd_ref[0, at, here] = (dot(dscores, keys_two) * scale).astype(low)
            dk_two = dot_left(dscores, q)
            dqkvd_ref[1, at, here] = (
                jnp.where(first, dk_two[:seq_len, :], dk_two[seq_len:, :]) * scale
            ).astype(low)
    total = dz
    for k in range(3):
        block = dqkvd_ref[k]
        if sums is not None and k != 1:
            sums[k // 2 : k // 2 + 1, :] = column_sum(block.astype(full))
        total = total + dot_right(block, attn(k))
    return total


class Stores:
    def __init__(self, targets, sources, sems):
        self.copies = [
            pltpu.make_async_copy(source, target, sems.at[at])
            for at, (target, source) in enumerate(zip(targets, sources))
        ]

    def __call__(self, which):
        for at in which:
            self.copies[at].start()

    def wait(self):
        for copy in self.copies:
            copy.wait()


def first_kernel(
    scal, h_ref, doc_row, doc_col, vec, attn_ref, feed_ref,
    *refs,
):
    store = Stores(refs[:7], refs[7:14], refs[14])
    qkv_ref, ctx_ref, n_ref, r_ref, h_next, act_ref, slope_ref = refs[7:14]
    live = live_rows(h_ref.shape[0], scal[2], doc_row.shape[1])
    attend_forward(
        h_ref[...], doc_row, doc_col, vec, Blocks(attn_ref), live, qkv_ref, ctx_ref, n_ref, r_ref,
        h_next,
    )
    store(range(5))
    feed_up(h_next, vec, Blocks(feed_ref), act_ref, slope_ref)
    store((5, 6))
    store.wait()


def second_kernel(
    scal, h_ref, act_ref, vec, d0, d1, d2, d3, *refs, seq_len
):
    store = Stores(refs[:3], refs[3:6], refs[6])
    live = live_rows(h_ref.shape[0], scal[2], seq_len)
    feed_down(h_ref, act_ref, scal[1], vec, Blocks(d0, d1, d2, d3), live, *refs[3:6])
    store(range(3))
    store.wait()


def turn_kernel(
    scal, h_ref, e_ref, doc_row, doc_col, vec, attn_ref, feed_ref, d0, d1, d2, d3, *refs
):
    low_ref, bufs = refs[20], refs[21:31]
    dpre_buf, dqkvd_buf, dctx_buf, out_sems = refs[31:]
    qkv_ref, ctx_ref, n_one, r_one, h_one, act_ref, slope_ref, h_two, n_two, r_two = bufs
    rows, seq_len = h_ref.shape[0], doc_row.shape[1]

    @pl.when(scal[1] >= 2)
    def _():
        store = Stores(refs[10:20], bufs, out_sems)
        attn, feed, downs = Blocks(attn_ref), Blocks(feed_ref), Blocks(d0, d1, d2, d3)
        live = live_rows(rows, scal[2], seq_len)
        attend_forward(
            h_ref[...], doc_row, doc_col, vec, attn, live, qkv_ref, ctx_ref, n_one, r_one, h_one
        )
        store(range(5))
        feed_up(h_one, vec, feed, act_ref, slope_ref)
        store((5, 6))
        feed_down(h_one, act_ref, scal[1], vec, downs, live, h_two, n_two, r_two)
        store((7, 8, 9))
        upstream = jnp.where(live, e_ref[...], 0.0)
        total = feed_back(
            upstream, n_two, r_two, slope_ref, scal[1], vec, downs, feed, None, dpre_buf, None
        )
        upstream = jnp.where(live, total.astype(low).astype(full), 0.0)
        total = attend_back(
            upstream, n_one, r_one, qkv_ref, doc_row, doc_col, vec, attn, dqkvd_buf, dctx_buf, None
        )
        low_ref[...] = total.astype(low)
        store.wait()


def back_second_kernel(
    scal, low_ref, e_ref, n_ref, r_ref, vec, d0, d1, d2, d3, slope_hbm, feed_hbm,
    db_ref, dpre_ref, dh_ref, sums, slope_ref, feed_ref, sems, *, seq_len,
):
    loads = Stores((slope_ref, feed_ref), (slope_hbm, feed_hbm), sems)
    loads((0, 1))
    upstream = jnp.where(scal[1] < 2, low_ref[...].astype(full), e_ref[...])
    upstream = jnp.where(live_rows(n_ref.shape[0], scal[2], seq_len), upstream, 0.0)
    dh_ref[...] = feed_back(
        upstream, n_ref, r_ref, slope_ref, scal[1], vec, Blocks(d0, d1, d2, d3), Blocks(feed_ref),
        db_ref, dpre_ref, sums, loads.copies,
    )


def back_first_kernel(
    scal, e_ref, n_ref, r_ref, qkv_ref, doc_row, doc_col, vec, dpre_ref, attn_ref,
    kept_ref, sent_ref, dh_ref, sums, dctx_buf, dqkvd_ref,
):
    live = live_rows(n_ref.shape[0], scal[2], doc_row.shape[1])
    upstream = jnp.where(live, e_ref[...].astype(low).astype(full), 0.0)
    dh_ref[...] = attend_back(
        upstream, n_ref, r_ref, qkv_ref, doc_row, doc_col, vec, Blocks(attn_ref), dqkvd_ref,
        dctx_buf, sums,
    )

    @pl.when(scal[0] == 0)
    def _():
        kept_ref[...] = dqkvd_ref[...]
        sent_ref[...] = dpre_ref[...]

    @pl.when(scal[0] != 0)
    def _():
        kept_ref[...] = dpre_ref[...]
        sent_ref[...] = dqkvd_ref[...]


def split_blocks(total, keep, send, bit, stride):
    half, share, cols = keep.shape
    blocks = total.reshape(2 * half, share, cols)
    for i in range(half):
        base = (i // stride) * 2 * stride + i % stride

        @pl.when(bit == 0)
        def _():
            keep[i] = blocks[base].astype(low)
            send[i] = blocks[base + stride].astype(low)

        @pl.when(bit != 0)
        def _():
            keep[i] = blocks[base + stride].astype(low)
            send[i] = blocks[base].astype(low)


def down_gradient(
    bits, act_own, act_other, db_own, db_other, keep, send, far, *, stride, place, here
):
    t = bits[here]
    total = dot_left(db_own[...], act_own[1 - t]) + dot_left(db_other[...], act_other[1 - t])
    far[...] = total.reshape(far.shape).astype(low)
    total = dot_left(db_own[...], act_own[t]) + dot_left(db_other[...], act_other[t])
    split_blocks(total, keep, send, bits[place], stride)


def weight_gradient(
    bits, left_own, left_other, right_own, right_other, keep, send, *, stride, place
):
    total = dot_left(left_own[...], right_own[...]) + dot_left(left_other[...], right_other[...])
    split_blocks(total, keep, send, bits[place], stride)


def adam_apply(weight_now, first_moment, second_moment, gradient, decay_rate):
    first_new = beta_one * first_moment + (1.0 - beta_one) * gradient
    second_new = beta_two * second_moment + (1.0 - beta_two) * gradient * gradient
    update = (
        first_new
        / (1.0 - beta_one**adam_step)
        / (jnp.sqrt(second_new / (1.0 - beta_two**adam_step)) + adam_eps)
    )
    return (weight_now - learn_rate * (update + decay_rate * weight_now), first_new, second_new)


def swap(block, axis, mask):
    return lax.ppermute(block, axis, [(i, i ^ mask) for i in range(lax.axis_size(axis))])


def masks_of(count):
    return [1 << b for b in range(count.bit_length() - 1)]


def pick(block, at):
    return lax.dynamic_index_in_dim(block, at, 1, keepdims=False)


def struct(dims, kind):
    return jax.ShapeDtypeStruct(dims, kind)


class Order:
    def __init__(self, masks):
        self.masks = masks
        left = sorted(masks)
        self.strides = []
        for mask in masks:
            self.strides.append(1 << left.index(mask))
            left.remove(mask)


def take(blocks, bit, stride):
    rest = blocks.shape[1:]
    blocks = blocks.reshape(-1, 2, stride, *rest)
    return lax.dynamic_index_in_dim(blocks, bit, 1, keepdims=False).reshape(-1, *rest)


def weave(own, got, bit, stride):
    rest = own.shape[1:]
    own, got = own.reshape(-1, 1, stride, *rest), got.reshape(-1, 1, stride, *rest)
    both = jnp.where(
        bit == 0, jnp.concatenate([own, got], 1), jnp.concatenate([got, own], 1)
    )
    return both.reshape(-1, *rest)


def shards(
    hidden_in, out_grad, seq_counts, segment_ids, proj, proj_master, proj_m, proj_v,
    down, down_master, down_m, down_v, vectors, vec_m, vec_v,
):
    group_count = lax.axis_size("dp")
    section = lax.axis_index("section")
    core, layer = section % 2, section // 2
    width = hidden_in.shape[1]
    seq_len = segment_ids.shape[1]
    slots = segment_ids.shape[0] // 2
    rows = slots * seq_len
    wide = proj.shape[2]
    at_first = layer == 0

    own_w = proj[0]
    other_w = swap(own_w, "section", 1)
    d0 = lax.dynamic_index_in_dim(down, layer, 0, keepdims=False)
    d2 = swap(lax.dynamic_index_in_dim(down, 1 - layer, 0, keepdims=False), "section", 2)
    d1 = swap(d0, "section", 1)
    vec = lax.dynamic_index_in_dim(vectors, layer, 0, keepdims=False)

    own_in = lax.dynamic_slice_in_dim(hidden_in, core * rows, rows, 0)
    own_cot = lax.dynamic_slice_in_dim(out_grad, core * rows, rows, 0)
    docs = lax.dynamic_slice_in_dim(segment_ids, core * slots, slots, 0)
    doc_col = docs.reshape(rows, 1)
    live_count = lax.dynamic_index_in_dim(seq_counts[0], core, 0, keepdims=False)
    scal = jnp.stack([core, section, live_count]).astype(jnp.int32)

    def by_core(at_zero, at_one):
        return jnp.where(core == 0, at_zero, at_one)

    attn_w, feed_w = by_core(own_w, other_w), by_core(other_w, own_w)
    rows_low, rows_full = struct((rows, width), low), struct((rows, width), full)
    blocks, inverse = struct((4, rows, width), low), struct((rows, 128), full)
    residuals = [
        struct((rows, 3 * width), low), rows_low, rows_full, inverse, rows_low, blocks, blocks,
        rows_low, rows_full, inverse,
    ]

    kept_out = [pltpu.HBM(x.shape, x.dtype) for x in residuals]

    def scratch(shape):
        return pltpu.VMEM(shape.shape, shape.dtype)

    def hop(block, towards):
        route = [(0, 2), (1, 3)] if towards else [(2, 0), (3, 1)]
        return lax.ppermute(block, "section", route)

    first = call(
        first_kernel, kept_out[:7], (scal, own_in, docs, doc_col, vec, attn_w, feed_w),
        [smem] + [vmem] * 6, [*map(scratch, residuals[:7]), pltpu.SemaphoreType.DMA((7,))],
        out_specs=[hbm] * 7, limit=24, cost=6,
    )
    d2, _ = lax.optimization_barrier((d2, first[4]))
    downs = (d0, d1, d2, swap(d2, "section", 1))
    second = call(
        functools.partial(second_kernel, seq_len=seq_len),
        kept_out[7:], (scal, first[4], first[5], vec, *downs),
        [smem] + [vmem] * 7, [*map(scratch, residuals[7:]), pltpu.SemaphoreType.DMA((3,))],
        out_specs=[hbm] * 3, limit=16, cost=4,
    )
    arrived = hop(second[0], True)
    layer_in = jnp.where(at_first, own_in, arrived)
    ins = (scal, arrived, own_cot, docs, doc_col, vec, attn_w, feed_w, *downs, *first, *second)
    *kept, back_low = call(
        turn_kernel, [*kept_out, rows_low], ins,
        [smem] + [vmem] * 11 + [hbm] * 10,
        [
            *map(scratch, (*residuals, blocks, blocks, rows_low)),
            pltpu.SemaphoreType.DMA((10,)),
        ],
        out_specs=[hbm] * 10 + [vmem], limit=36, cost=25,
        aliases={len(ins) - 10 + i: i for i in range(10)},
    )
    qkv, ctx, n_one, r_one, h_one, act, slope, h_two, n_two, r_two = kept

    kept_left = (by_core(layer_in, h_one), by_core(ctx, h_one), by_core(h_one, h_two))
    sent_left = jnp.stack(
        [by_core(h_one, layer_in), by_core(h_one, ctx), by_core(h_two, h_one)]
    )
    got_left = swap(sent_left, "section", 1)
    act_pairs = act.reshape(2, 2, rows, width)
    act_kept = pick(act_pairs, core)
    act_got = swap(pick(act_pairs, 1 - core), "section", 1)

    masks = masks_of(group_count)
    index = lax.axis_index("dp")
    share = width // group_count
    half = group_count // 2
    bits = jnp.stack([(index // mask) % 2 for mask in masks] + [layer]).astype(jnp.int32)
    scatter = Order(masks)
    gathers = {name: Order(masks) for name in ("near", 0, 1, 2, 3)}
    gathers["far"] = Order(masks[1:] + masks[:1])
    last = len(masks) - 1
    part = struct((half, share, width), low)

    def bit(mask):
        return (index // mask) % 2

    token = [jnp.zeros((8, 128), full)]

    def tie(*arrays):
        *arrays, token[0] = lax.optimization_barrier((*arrays, token[0]))
        return arrays if len(arrays) > 1 else arrays[0]

    db, dpre, dh_two, sums_two = call(
        functools.partial(back_second_kernel, seq_len=seq_len),
        [rows_low, blocks, rows_full, struct((8, width), full)],
        (
            scal, hop(back_low, False), own_cot, n_two, r_two, vec, *downs, slope, feed_w,
        ),
        [smem] + [vmem] * 9 + [hbm] * 2,
        (scratch(blocks), pltpu.VMEM((width, wide), low), pltpu.SemaphoreType.DMA((2,))),
        limit=24, cost=6,
    )
    keep, send, far = call(
        functools.partial(
            down_gradient, stride=scatter.strides[0], place=0, here=len(masks)
        ),
        [part, part, struct((group_count, share, width), low)],
        (bits, act_kept, act_got, db, swap(db, "section", 1)),
        [smem] + [vmem] * 4, cost=4,
    )
    terms = {"near": [keep]}
    dh_two, send, far = lax.optimization_barrier((dh_two, send, far))
    got = {"near": swap(send, "dp", masks[0])}
    kept_right, sent_right, dh_one, sums_one = call(
        back_first_kernel,
        [blocks, blocks, rows_full, struct((8, width), full)],
        (scal, dh_two, n_one, r_one, qkv, docs, doc_col, vec, dpre, attn_w),
        [smem] + [vmem] * 9,
        (scratch(rows_low), scratch(blocks)), limit=16, cost=9,
    )
    got_right = [swap(sent_right[k], "section", 1) for k in range(4)]
    kept_grad = by_core(dh_one, dh_two)
    got_grad = swap(by_core(dh_two, dh_one), "section", 1)
    proj_copy = [jnp.zeros((1, width, wide), low)]
    updated, down_copies = {}, {}

    def begin(k):
        flight.append(k)
        if k == "far":
            blocks = tie(far)
            terms[k] = [take(blocks, bit(masks[0]), scatter.strides[0])]
            send = take(blocks, 1 - bit(masks[0]), scatter.strides[0])
            got[k] = swap(tie(send), "dp", masks[0])
            return
        lhs = 0 if k < 3 else 1
        keep, send = call(
            functools.partial(weight_gradient, stride=scatter.strides[0], place=0),
            [part, part],
            (bits, kept_left[lhs], got_left, kept_right, tie(got_right[k])),
            [
                smem, vmem, pl.BlockSpec((None, rows, width), lambda _: (lhs, 0, 0)),
                pl.BlockSpec((None, rows, width), lambda _: (k, 0, 0)), vmem,
            ],
            grid=(1,),
        )
        terms[k] = [keep]
        got[k] = swap(tie(send), "dp", masks[0])

    def arrive(name, stage):
        terms[name].append(tie(got[name]))
        if stage:
            terms[name][:-1] = [
                take(x, bit(scatter.masks[stage]), scatter.strides[stage])
                for x in terms[name][:-1]
            ]

    def total_of(name):
        return sum(x.astype(full) for x in terms[name])[0]

    def scatter_step(stage):
        def step(name):
            arrive(name, stage)
            mask, stride = scatter.masks[stage + 1], scatter.strides[stage + 1]
            send = sum(take(x, 1 - bit(mask), stride).astype(full) for x in terms[name])
            got[name] = swap(tie(send.astype(low)), "dp", mask)

        return step

    def gather_start(name, payload):
        terms[name] = tie(payload)
        got[name] = swap(terms[name], "dp", gathers[name].masks[last])

    def down_step(name):
        arrive(name, last)
        grad = total_of(name) / group_count
        at = layer if name == "near" else 1 - layer
        held = [
            lax.dynamic_index_in_dim(jnp.swapaxes(x, 1, 2), at, 0, keepdims=False)
            for x in (down_master, down_m, down_v)
        ]
        new = adam_apply(*held, grad, weight_decay)
        updated[name] = (grad, *new)
        gather_start(name, new[0][None].astype(low))

    def proj_step(name):
        arrive(name, last)
        grad = total_of(name) / group_count
        cols = slice(name * width, (name + 1) * width)
        new = adam_apply(
            proj_master[0, :, cols], proj_m[0, :, cols], proj_v[0, :, cols], grad, weight_decay
        )
        updated[name] = (grad, *new)
        gather_start(name, new[0][None].astype(low))

    def woven(name, stage):
        mask, stride = gathers[name].masks[stage], gathers[name].strides[stage]
        return weave(terms[name], tie(got[name]), bit(mask), stride)

    def gather_step(stage):
        def step(name):
            terms[name] = tie(woven(name, stage))
            got[name] = swap(terms[name], "dp", gathers[name].masks[stage - 1])

        return step

    def copy_proj_step(name):
        block = tie(woven(name, 0)).reshape(1, width, width)
        proj_copy[0] = lax.dynamic_update_slice(proj_copy[0], block, (0, 0, name * width))

    def copy_down_step(name):
        down_copies[name] = tie(woven(name, 0).reshape(width, width).T)

    halvings = [scatter_step(stage) for stage in range(last)]
    doublings = [gather_step(stage) for stage in range(last, 0, -1)]
    todo = {
        name: halvings
        + [down_step if name in ("near", "far") else proj_step]
        + doublings
        + [copy_down_step if name in ("near", "far") else copy_proj_step]
        for name in gathers
    }
    flight = ["near"]

    def advance():
        name = flight.pop(0)
        todo[name].pop(0)(name)
        if todo[name]:
            flight.append(name)

    def by_layer(near, far):
        return jnp.where(at_first, jnp.stack([near, far]), jnp.stack([far, near]))

    sums = jnp.concatenate([sums_one[:5], sums_two[:7]], 0)
    sums = sums + swap(sums, "section", 1)
    vector_sums = [sums]

    def vector_step(mask):
        def step(name):
            vector_sums[0] = tie(vector_sums[0] + tie(got[name]))
            if mask:
                got[name] = swap(vector_sums[0], "dp", mask)
            else:
                got[name] = swap(vector_sums[0], "section", 2)

        return step

    def vector_last(name):
        updated[name] = by_layer(vector_sums[0], tie(got[name]))

    todo["vectors"] = [vector_step(mask) for mask in (*masks[1:], 0)] + [vector_last]
    begin(0)
    advance()
    far = swap(tie(far), "section", 2)
    for name in (1, 2, 3, "far"):
        begin(name)
        while flight[0] != name:
            advance()
    got["vectors"] = swap(tie(vector_sums[0]), "dp", masks[0])
    flight.append("vectors")
    while flight:
        advance()

    vec_grad = updated["vectors"] / group_count
    vec_moments = adam_apply(vectors, vec_m, vec_v, vec_grad, 0.0)

    def in_order(kept, got):
        return by_core(jnp.concatenate([kept, got], 0), jnp.concatenate([got, kept], 0))[None]

    return (
        in_order(kept_left[2], got_left[2]),
        in_order(kept_grad, got_grad),
        *[jnp.concatenate([updated[k][i] for k in range(4)], 1)[None] for i in range(4)],
        proj_copy[0],
        *[
            jnp.swapaxes(by_layer(updated["near"][i], updated["far"][i]), 1, 2) for i in range(4)
        ],
        by_layer(down_copies["near"], down_copies["far"]),
        vec_grad,
        vec_moments[1],
        vec_moments[2],
    )


def solution(mesh):
    shared = P("section", "dp", None)
    split = P(None, "section", "dp")
    placed = (
        P("dp", None), P("dp", None), P("dp", None), P("dp", None),
        P("section", None, None), shared, shared, shared,
        P(None, "section", None), split, split, split, P(), P(), P(),
    )
    return jax.shard_map(
        shards,
        mesh=mesh,
        in_specs=placed,
        out_specs=(
            shared, shared, shared, shared, shared, shared,
            P("section", None, None), split, split, split, split,
            P(None, "section", None), P(), P(), P(),
        ),
        check_vma=False,
    )
```

```python
import functools
import math

import jax
import jax.numpy as jnp
from jax import lax
from jax.experimental import pallas as pl
from jax.experimental.pallas import tpu as pltpu
from jax.sharding import PartitionSpec as P

HEADS = 12
HEAD_PAIRS = HEADS // 2

norm_eps = 1e-05
beta_one = 0.9
beta_two = 0.98
adam_eps = 1e-06
learn_rate = 0.001
weight_decay = 0.01
adam_step = 100.0

low = jnp.bfloat16
full = jnp.float32

vmem = pl.BlockSpec(memory_space=pltpu.VMEM)
smem = pl.BlockSpec(memory_space=pltpu.SMEM)
anywhere = pl.BlockSpec(memory_space=pl.ANY)
hbm = pl.BlockSpec(memory_space=pltpu.HBM)


def dot(a, b):
    return lax.dot_general(a, b, (((1,), (0,)), ((), ())), preferred_element_type=full)


def dot_right(a, b):
    return lax.dot_general(a, b, (((1,), (1,)), ((), ())), preferred_element_type=full)


def dot_left(a, b):
    return lax.dot_general(a, b, (((0,), (0,)), ((), ())), preferred_element_type=full)


def row_mean(z):
    return jnp.mean(z, -1, keepdims=True)


def norm_rows(z):
    centered = z - row_mean(z)
    inv = lax.rsqrt(row_mean(centered * centered) + norm_eps)
    return centered * inv, inv


def norm_rows_back(upstream, normed, inv, gain):
    scaled = upstream * gain
    return inv * (scaled - row_mean(scaled) - normed * row_mean(scaled * normed))


def live_rows(rows, live_count, seq_len):
    return lax.broadcasted_iota(jnp.int32, (rows, 1), 0) < live_count * seq_len


def column_sum(block):
    return jnp.sum(block, 0, keepdims=True)


def call(kernel, outs, ins, specs, scratch=(), grid=(), out_specs=None, limit=12, cost=0, aliases=None):
    return pl.pallas_call(
        kernel,
        grid=grid,
        out_shape=outs,
        in_specs=specs,
        out_specs=out_specs or jax.tree.map(lambda _: vmem, outs),
        scratch_shapes=list(scratch),
        input_output_aliases=aliases or {},
        compiler_params=pltpu.CompilerParams(vmem_limit_bytes=limit << 20),
        cost_estimate=pl.CostEstimate(flops=cost * 10**9, bytes_accessed=0, transcendentals=0),
    )(*ins)


def pair_masks(seq_len):
    first = lax.broadcasted_iota(jnp.int32, (seq_len, 128), 1) < 64
    return first


def spread_pair(block, first):
    zero = jnp.zeros_like(block)
    return jnp.concatenate([jnp.where(first, block, zero), jnp.where(first, zero, block)], 0)


def pair_probs(q, keys_two, same_doc, scale, seq_len):
    scores = dot_right(q, keys_two) * scale
    parts = []
    for half in range(2):
        part = jnp.where(same_doc, scores[:, half * seq_len : (half + 1) * seq_len], -1e30)
        exponent = jnp.exp(part - jnp.max(part, -1, keepdims=True))
        parts.append(exponent / jnp.sum(exponent, -1, keepdims=True))
    return parts


class Blocks:
    def __init__(self, *refs):
        self.refs = refs

    def __call__(self, k):
        if len(self.refs) > 1:
            return self.refs[k][...]
        (ref,) = self.refs
        width = ref.shape[1] // 4
        return ref[:, k * width : (k + 1) * width]


def attend_forward(
    hidden, doc_row, doc_col, vec, attn, live, qkv_ref, ctx_ref, n_ref, r_ref, h_next
):
    rows, width = hidden.shape
    seq_len = doc_row.shape[1]
    scale = (width // HEADS) ** (-0.5)
    for part in range(3):
        block = dot(hidden, attn(part))
        if part == 0:
            block = block + vec[0:1, :]
        if part == 2:
            block = block + vec[1:2, :]
        qkv_ref[:, part * width : (part + 1) * width] = block.astype(low)
    first = pair_masks(seq_len)
    for s in range(rows // seq_len):
        at = slice(s * seq_len, (s + 1) * seq_len)
        same_doc = doc_col[at, :] == doc_row[s : s + 1, :]
        for p in range(HEAD_PAIRS):
            q, k, v = (
                qkv_ref[at, part * width + p * 128 : part * width + (p + 1) * 128]
                for part in range(3)
            )
            probs = pair_probs(q, spread_pair(k, first), same_doc, scale, seq_len)
            probs_low = jnp.concatenate([x.astype(low) for x in probs], 1)
            ctx_ref[at, p * 128 : (p + 1) * 128] = dot(probs_low, spread_pair(v, first)).astype(low)
    z = hidden.astype(full) + (dot(ctx_ref[...], attn(3)) + vec[2:3, :])
    normed, inv = norm_rows(z)
    n_ref[...] = normed
    r_ref[...] = jnp.broadcast_to(inv, r_ref.shape)
    h_next[...] = jnp.where(live, normed * vec[3:4, :] + vec[4:5, :], 0.0).astype(low)


def feed_up(h_ref, vec, feed, act_ref, slope_ref):
    hidden = h_ref[...]
    for k in range(4):
        pre = dot(hidden, feed(k)) + vec[5 + k : 6 + k, :]
        half_cdf = 0.5 * (1.0 + lax.erf(pre * (1.0 / math.sqrt(2.0))))
        act_ref[k] = (pre * half_cdf).astype(low)
        slope_ref[k] = (
            half_cdf + pre * jnp.exp(-0.5 * pre * pre) * (1.0 / math.sqrt(2.0 * math.pi))
        ).astype(slope_ref.dtype)


def feed_down(h_ref, act_ref, section, vec, downs, live, h_next, n_ref, r_ref):
    total = h_ref[...].astype(full) + vec[9:10, :]
    for m in range(4):
        total = total + dot(act_ref[section ^ m], downs(m))
    finish_second(total, vec, live, h_next, n_ref, r_ref)


def finish_second(total, vec, live, h_next, n_ref, r_ref):
    normed, inv = norm_rows(total)
    n_ref[...] = normed
    r_ref[...] = jnp.broadcast_to(inv, r_ref.shape)
    h_next[...] = jnp.where(live, normed * vec[10:11, :] + vec[11:12, :], 0.0).astype(low)


def feed_back(
    upstream, n_ref, r_ref, slope_ref, section, vec, downs, feed, db_ref, dpre_ref, sums, loads=()
):
    width = n_ref.shape[1]
    normed = n_ref[...]
    dz = norm_rows_back(upstream, normed, r_ref[:, :1], vec[10:11, :])
    db = dz.astype(low)
    if db_ref is not None:
        db_ref[...] = db
        sums[4:5, :] = column_sum(db.astype(full))
        sums[5:6, :] = column_sum(upstream * normed)
        sums[6:7, :] = column_sum(upstream)
        sums[7:8, :] = jnp.zeros((1, width), full)
    for m in range(4):
        at = section ^ m
        if loads:
            loads[m].wait()
        dact = dot_right(db, downs(m))
        if m == 0 and loads:
            loads[4].wait()
        dpre_ref[at] = (dact * slope_ref[at].astype(full)).astype(low)
    total = dz
    if loads:
        loads[5].wait()
    for k in range(4):
        dpre = dpre_ref[k]
        if db_ref is not None:
            sums[k : k + 1, :] = column_sum(dpre.astype(full))
        total = total + dot_right(dpre, feed(k))
    return total


def attend_back(
    upstream, n_ref, r_ref, qkv_ref, doc_row, doc_col, vec, attn, dqkvd_ref, dctx_buf, sums,
    loads=(),
):
    rows, width = n_ref.shape
    seq_len = doc_row.shape[1]
    scale = (width // HEADS) ** (-0.5)
    normed = n_ref[...]
    dz = norm_rows_back(upstream, normed, r_ref[:, :1], vec[3:4, :])
    da = dz.astype(low)
    dqkvd_ref[3] = da
    if sums is not None:
        sums[2:3, :] = column_sum(da.astype(full))
        sums[3:4, :] = column_sum(upstream * normed)
        sums[4:5, :] = column_sum(upstream)
        sums[5:8, :] = jnp.zeros((3, width), full)
    if loads:
        loads[0].wait()
    dctx_buf[...] = dot_right(da, attn(3)).astype(low)
    if loads:
        loads[1].wait()
    first = pair_masks(seq_len)
    for s in range(rows // seq_len):
        at = slice(s * seq_len, (s + 1) * seq_len)
        same_doc = doc_col[at, :] == doc_row[s : s + 1, :]
        for p in range(HEAD_PAIRS):
            here = slice(p * 128, (p + 1) * 128)
            q, k, v = (
                qkv_ref[at, part * width + p * 128 : part * width + (p + 1) * 128]
                for part in range(3)
            )
            keys_two = spread_pair(k, first)
            dctx = dctx_buf[at, here]
            probs = pair_probs(q, keys_two, same_doc, scale, seq_len)
            probs_low = jnp.concatenate([x.astype(low) for x in probs], 1)
            dv_two = dot_left(probs_low, dctx)
            dqkvd_ref[2, at, here] = jnp.where(
                first, dv_two[:seq_len, :], dv_two[seq_len:, :]
            ).astype(low)
            dprobs = dot_right(dctx, spread_pair(v, first))
            dscores = []
            for half in range(2):
                part = dprobs[:, half * seq_len : (half + 1) * seq_len]
                inner = jnp.sum(probs[half] * part, -1, keepdims=True)
                dscores.append((probs[half] * (part - inner)).astype(low))
            dscores = jnp.concatenate(dscores, 1)
            dqkvd_ref[0, at, here] = (dot(dscores, keys_two) * scale).astype(low)
            dk_two = dot_left(dscores, q)
            dqkvd_ref[1, at, here] = (
                jnp.where(first, dk_two[:seq_len, :], dk_two[seq_len:, :]) * scale
            ).astype(low)
    total = dz
    if loads:
        loads[2].wait()
    for k in range(3):
        block = dqkvd_ref[k]
        if sums is not None and k != 1:
            sums[k // 2 : k // 2 + 1, :] = column_sum(block.astype(full))
        total = total + dot_right(block, attn(k))
    return total


class Stores:
    def __init__(self, targets, sources, sems):
        self.copies = [
            pltpu.make_async_copy(source, target, sems.at[at])
            for at, (target, source) in enumerate(zip(targets, sources))
        ]

    def __call__(self, which):
        for at in which:
            self.copies[at].start()

    def wait(self):
        for copy in self.copies:
            copy.wait()


def first_kernel(
    scal, h_ref, doc_row, doc_col, vec, attn_ref, feed_ref,
    *refs,
):
    store = Stores(refs[:7], refs[7:14], refs[14])
    qkv_ref, ctx_ref, n_ref, r_ref, h_next, act_ref, slope_ref = refs[7:14]
    live = live_rows(h_ref.shape[0], scal[2], doc_row.shape[1])
    attend_forward(
        h_ref[...], doc_row, doc_col, vec, Blocks(attn_ref), live, qkv_ref, ctx_ref, n_ref, r_ref,
        h_next,
    )
    store(range(5))
    feed_up(h_next, vec, Blocks(feed_ref), act_ref, slope_ref)
    store((5, 6))
    store.wait()


def near_down_kernel(scal, h_ref, act_ref, vec, d0, d1, total):
    total[...] = h_ref[...].astype(full) + vec[9:10, :] + (
        dot(act_ref[scal[1]], d0[...]) + dot(act_ref[scal[1] ^ 1], d1[...])
    )


def second_kernel(scal, total_ref, act_ref, vec, d2, d3, *refs, seq_len):
    store = Stores(refs[:3], refs[3:6], refs[6])
    rows = total_ref.shape[0]
    total = total_ref[...] + (
        dot(act_ref[scal[1] ^ 2], d2[...]) + dot(act_ref[scal[1] ^ 3], d3[...])
    )
    finish_second(total, vec, live_rows(rows, scal[2], seq_len), *refs[3:6])
    store(range(3))
    store.wait()


def turn_kernel(
    scal, h_ref, e_ref, doc_row, doc_col, vec, attn_ref, feed_ref, d0, d1, d2, d3, *refs
):
    low_ref, bufs = refs[20], refs[21:31]
    dpre_buf, dqkvd_buf, dctx_buf, out_sems = refs[31:]
    qkv_ref, ctx_ref, n_one, r_one, h_one, act_ref, slope_ref, h_two, n_two, r_two = bufs
    rows, seq_len = h_ref.shape[0], doc_row.shape[1]

    @pl.when(scal[1] >= 2)
    def _():
        store = Stores(refs[10:20], bufs, out_sems)
        attn, feed, downs = Blocks(attn_ref), Blocks(feed_ref), Blocks(d0, d1, d2, d3)
        live = live_rows(rows, scal[2], seq_len)
        attend_forward(
            h_ref[...], doc_row, doc_col, vec, attn, live, qkv_ref, ctx_ref, n_one, r_one, h_one
        )
        store(range(5))
        feed_up(h_one, vec, feed, act_ref, slope_ref)
        store((5, 6))
        feed_down(h_one, act_ref, scal[1], vec, downs, live, h_two, n_two, r_two)
        store((7, 8, 9))
        upstream = jnp.where(live, e_ref[...], 0.0)
        total = feed_back(
            upstream, n_two, r_two, slope_ref, scal[1], vec, downs, feed, None, dpre_buf, None
        )
        upstream = jnp.where(live, total.astype(low).astype(full), 0.0)
        total = attend_back(
            upstream, n_one, r_one, qkv_ref, doc_row, doc_col, vec, attn, dqkvd_buf, dctx_buf, None
        )
        low_ref[...] = total.astype(low)
        store.wait()


def back_second_kernel(
    scal, low_ref, vec, *refs, seq_len,
):
    sources, (db_ref, dpre_ref, dh_ref, sums) = refs[:9], refs[9:13]
    targets, sems = refs[13:22], refs[22]
    n_ref, r_ref, e_ref, d0, slope_ref, d1, d2, d3, feed_ref = targets
    loads = Stores(targets, sources, sems)
    loads(range(9))
    for at in range(3):
        loads.copies[at].wait()
    waits = [loads.copies[at] for at in (3, 5, 6, 7, 4, 8)]
    upstream = jnp.where(scal[1] < 2, low_ref[...].astype(full), e_ref[...])
    upstream = jnp.where(live_rows(n_ref.shape[0], scal[2], seq_len), upstream, 0.0)
    dh_ref[...] = feed_back(
        upstream, n_ref, r_ref, slope_ref, scal[1], vec, Blocks(d0, d1, d2, d3), Blocks(feed_ref),
        db_ref, dpre_ref, sums, waits,
    )


def back_first_kernel(scal, e_ref, doc_row, doc_col, vec, *refs):
    *sources, attn_hbm = refs[:5]
    kept_ref, sent_ref, dh_ref, sums = refs[5:9]
    n_ref, r_ref, qkv_ref, dpre_ref, attn_ref, dctx_buf, dqkvd_ref, sems = refs[9:]
    width = n_ref.shape[1]
    out_cols, in_cols = pl.ds(3 * width, width), pl.ds(0, 3 * width)
    loads = Stores(
        (n_ref, r_ref, attn_ref.at[:, out_cols], qkv_ref, attn_ref.at[:, in_cols], dpre_ref),
        (*sources[:2], attn_hbm.at[:, out_cols], sources[2], attn_hbm.at[:, in_cols], sources[3]),
        sems,
    )
    loads(range(6))
    live = live_rows(n_ref.shape[0], scal[2], doc_row.shape[1])
    upstream = jnp.where(live, e_ref[...].astype(low).astype(full), 0.0)
    for at in range(2):
        loads.copies[at].wait()
    dh_ref[...] = attend_back(
        upstream, n_ref, r_ref, qkv_ref, doc_row, doc_col, vec, Blocks(attn_ref), dqkvd_ref,
        dctx_buf, sums, loads.copies[2:5],
    )
    loads.copies[5].wait()

    @pl.when(scal[0] == 0)
    def _():
        kept_ref[...] = dqkvd_ref[...]
        sent_ref[...] = dpre_ref[...]

    @pl.when(scal[0] != 0)
    def _():
        kept_ref[...] = dpre_ref[...]
        sent_ref[...] = dqkvd_ref[...]


def split_blocks(total, keep, send, bit, stride):
    half, share, cols = keep.shape
    blocks = total.reshape(2 * half, share, cols)
    for i in range(half):
        base = (i // stride) * 2 * stride + i % stride

        @pl.when(bit == 0)
        def _():
            keep[i] = blocks[base].astype(low)
            send[i] = blocks[base + stride].astype(low)

        @pl.when(bit != 0)
        def _():
            keep[i] = blocks[base + stride].astype(low)
            send[i] = blocks[base].astype(low)


def down_gradient(
    bits, act_own, act_other, db_own, db_other, keep, send, far, *, stride, place, here
):
    t = bits[here]
    total = dot_left(db_own[...], act_own[1 - t]) + dot_left(db_other[...], act_other[1 - t])
    far[...] = total.reshape(far.shape).astype(low)
    total = dot_left(db_own[...], act_own[t]) + dot_left(db_other[...], act_other[t])
    split_blocks(total, keep, send, bits[place], stride)


def weight_gradient(
    bits, left_own, left_other, right_own, right_other, keep, send, *, stride, place
):
    total = dot_left(left_own[...], right_own[...]) + dot_left(left_other[...], right_other[...])
    split_blocks(total, keep, send, bits[place], stride)


def adam_apply(weight_now, first_moment, second_moment, gradient, decay_rate):
    first_new = beta_one * first_moment + (1.0 - beta_one) * gradient
    second_new = beta_two * second_moment + (1.0 - beta_two) * gradient * gradient
    update = (
        first_new
        / (1.0 - beta_one**adam_step)
        / (jnp.sqrt(second_new / (1.0 - beta_two**adam_step)) + adam_eps)
    )
    return (weight_now - learn_rate * (update + decay_rate * weight_now), first_new, second_new)


def copy_columns(bits, keep, got, *refs, stride, place):
    out = refs[-1]
    bit = bits[place]
    for i in range(keep.shape[0]):
        base = (i // stride) * 2 * stride + i % stride
        out[base + bit * stride] = keep[i]
        out[base + (1 - bit) * stride] = got[i]


def copy_turned(bits, keep, got, *refs, stride, place, here, far):
    out, buf, turned, sem = refs[-4:]
    bit = bits[place]
    for i in range(keep.shape[0]):
        base = (i // stride) * 2 * stride + i % stride
        buf[base + bit * stride] = keep[i].astype(full)
        buf[base + (1 - bit) * stride] = got[i].astype(full)
    count, share, cols = buf.shape
    turned[...] = buf[...].reshape(count * share, cols).T.astype(low)
    copy = pltpu.make_async_copy(turned, out.at[bits[here] ^ far], sem)
    copy.start()
    copy.wait()


def swap(block, axis, mask):
    return lax.ppermute(block, axis, [(i, i ^ mask) for i in range(lax.axis_size(axis))])


def masks_of(count):
    return [1 << b for b in range(count.bit_length() - 1)]


def pick(block, at):
    return lax.dynamic_index_in_dim(block, at, 1, keepdims=False)


def struct(dims, kind):
    return jax.ShapeDtypeStruct(dims, kind)


class Order:
    def __init__(self, masks):
        self.masks = masks
        left = sorted(masks)
        self.strides = []
        for mask in masks:
            self.strides.append(1 << left.index(mask))
            left.remove(mask)


def take(blocks, bit, stride):
    rest = blocks.shape[1:]
    blocks = blocks.reshape(-1, 2, stride, *rest)
    return lax.dynamic_index_in_dim(blocks, bit, 1, keepdims=False).reshape(-1, *rest)


def weave(own, got, bit, stride):
    rest = own.shape[1:]
    own, got = own.reshape(-1, 1, stride, *rest), got.reshape(-1, 1, stride, *rest)
    both = jnp.where(
        bit == 0, jnp.concatenate([own, got], 1), jnp.concatenate([got, own], 1)
    )
    return both.reshape(-1, *rest)


def shards(
    hidden_in, out_grad, seq_counts, segment_ids, proj, proj_master, proj_m, proj_v,
    down, down_master, down_m, down_v, vectors, vec_m, vec_v,
):
    group_count = lax.axis_size("dp")
    section = lax.axis_index("section")
    core, layer = section % 2, section // 2
    width = hidden_in.shape[1]
    seq_len = segment_ids.shape[1]
    slots = segment_ids.shape[0] // 2
    rows = slots * seq_len
    wide = proj.shape[2]
    at_first = layer == 0

    own_w = proj[0]
    other_w = swap(own_w, "section", 1)
    crossing = lax.dynamic_index_in_dim(down, 1 - layer, 0, keepdims=False)
    crossing, whole_down = lax.optimization_barrier((crossing, down))
    d2 = swap(crossing, "section", 2)
    d0 = lax.dynamic_index_in_dim(whole_down, layer, 0, keepdims=False)
    d1 = swap(d0, "section", 1)
    vec = lax.dynamic_index_in_dim(vectors, layer, 0, keepdims=False)

    own_in = lax.dynamic_slice_in_dim(hidden_in, core * rows, rows, 0)
    own_cot = lax.dynamic_slice_in_dim(out_grad, core * rows, rows, 0)
    docs = lax.dynamic_slice_in_dim(segment_ids, core * slots, slots, 0)
    doc_col = docs.reshape(rows, 1)
    live_count = lax.dynamic_index_in_dim(seq_counts[0], core, 0, keepdims=False)
    scal = jnp.stack([core, section, live_count]).astype(jnp.int32)

    def by_core(at_zero, at_one):
        return jnp.where(core == 0, at_zero, at_one)

    attn_w, feed_w = by_core(own_w, other_w), by_core(other_w, own_w)
    rows_low, rows_full = struct((rows, width), low), struct((rows, width), full)
    blocks, inverse = struct((4, rows, width), low), struct((rows, 128), full)
    residuals = [
        struct((rows, 3 * width), low), rows_low, rows_full, inverse, rows_low, blocks, blocks,
        rows_low, rows_full, inverse,
    ]

    kept_out = [pltpu.HBM(x.shape, x.dtype) for x in residuals]

    def scratch(shape):
        return pltpu.VMEM(shape.shape, shape.dtype)

    def hop(block, towards):
        route = [(0, 2), (1, 3)] if towards else [(2, 0), (3, 1)]
        return lax.ppermute(block, "section", route)

    first = call(
        first_kernel, kept_out[:7], (scal, own_in, docs, doc_col, vec, attn_w, feed_w),
        [smem] + [vmem] * 6, [*map(scratch, residuals[:7]), pltpu.SemaphoreType.DMA((7,))],
        out_specs=[hbm] * 7, limit=24, cost=6,
    )
    own_part = call(
        near_down_kernel, rows_full, (scal, first[4], first[5], vec, d0, d1), [smem] + [vmem] * 5,
        limit=16, cost=2,
    )
    d2, own_part = lax.optimization_barrier((d2, own_part))
    downs = (d0, d1, d2, swap(d2, "section", 1))
    second = call(
        functools.partial(second_kernel, seq_len=seq_len),
        kept_out[7:], (scal, own_part, first[5], vec, *downs[2:]),
        [smem] + [vmem] * 5, [*map(scratch, residuals[7:]), pltpu.SemaphoreType.DMA((3,))],
        out_specs=[hbm] * 3, limit=16, cost=4,
    )
    arrived = hop(second[0], True)
    layer_in = jnp.where(at_first, own_in, arrived)
    ins = (scal, arrived, own_cot, docs, doc_col, vec, attn_w, feed_w, *downs, *first, *second)
    *kept, back_low = call(
        turn_kernel, [*kept_out, rows_low], ins,
        [smem] + [vmem] * 11 + [hbm] * 10,
        [
            *map(scratch, (*residuals, blocks, blocks, rows_low)),
            pltpu.SemaphoreType.DMA((10,)),
        ],
        out_specs=[hbm] * 10 + [vmem], limit=36, cost=25,
        aliases={len(ins) - 10 + i: i for i in range(10)},
    )
    qkv, ctx, n_one, r_one, h_one, act, slope, h_two, n_two, r_two = kept

    kept_left = (by_core(layer_in, h_one), by_core(ctx, h_one), by_core(h_one, h_two))
    sent_left = jnp.stack(
        [by_core(h_one, layer_in), by_core(h_one, ctx), by_core(h_two, h_one)]
    )
    got_left = swap(sent_left, "section", 1)
    act_pairs = act.reshape(2, 2, rows, width)
    act_kept = pick(act_pairs, core)
    act_got = swap(pick(act_pairs, 1 - core), "section", 1)

    masks = masks_of(group_count)
    index = lax.axis_index("dp")
    share = width // group_count
    half = group_count // 2
    bits = jnp.stack([(index // mask) % 2 for mask in masks] + [layer]).astype(jnp.int32)
    scatter = Order(masks)
    turned = masks[1:] + masks[:1]
    gathers = {
        name: Order(turned if name in (3,) else masks) for name in ("near", 0, 1, 2, 3, "far")
    }
    last = len(masks) - 1
    part = struct((half, share, width), low)

    def bit(mask):
        return (index // mask) % 2

    token = [jnp.zeros((8, 128), full)]

    def tie(*arrays):
        *arrays, token[0] = lax.optimization_barrier((*arrays, token[0]))
        return arrays if len(arrays) > 1 else arrays[0]

    db, dpre, dh_two, sums_two = call(
        functools.partial(back_second_kernel, seq_len=seq_len),
        [rows_low, blocks, rows_full, struct((8, width), full)],
        (
            scal, hop(back_low, False), vec, n_two, r_two, own_cot, downs[0], slope, *downs[1:],
            feed_w,
        ),
        [smem, vmem, vmem] + [hbm] * 9,
        (
            *map(scratch, (rows_full, inverse, rows_full, d0, blocks, d0, d0, d0, own_w)),
            pltpu.SemaphoreType.DMA((9,)),
        ),
        limit=58, cost=6,
    )
    keep, send, far = call(
        functools.partial(
            down_gradient, stride=scatter.strides[0], place=0, here=len(masks)
        ),
        [part, part, struct((group_count, share, width), low)],
        (bits, act_kept, act_got, db, swap(db, "section", 1)),
        [smem] + [vmem] * 4, cost=4,
    )
    terms = {"near": [keep]}
    dh_two, send, far = lax.optimization_barrier((dh_two, send, far))
    got = {"near": swap(send, "dp", masks[0])}
    kept_right, sent_right, dh_one, sums_one = call(
        back_first_kernel,
        [blocks, blocks, rows_full, struct((8, width), full)],
        (scal, dh_two, docs, doc_col, vec, n_one, r_one, qkv, dpre, attn_w),
        [smem] + [vmem] * 4 + [hbm] * 5,
        (
            *map(scratch, (rows_full, inverse, residuals[0], blocks, own_w, rows_low, blocks)),
            pltpu.SemaphoreType.DMA((6,)),
        ),
        limit=24, cost=9,
    )
    got_right = [swap(sent_right[k], "section", 1) for k in range(4)]
    kept_grad = by_core(dh_one, dh_two)
    got_grad = swap(by_core(dh_two, dh_one), "section", 1)
    proj_copy, down_copy, updated = [], [], {}

    def begin(k):
        flight.append(k)
        if k == "far":
            blocks = tie(far)
            terms[k] = [take(blocks, bit(masks[0]), scatter.strides[0])]
            send = take(blocks, 1 - bit(masks[0]), scatter.strides[0])
            got[k] = swap(tie(send), "dp", masks[0])
            return
        lhs = 0 if k < 3 else 1
        keep, send = call(
            functools.partial(weight_gradient, stride=scatter.strides[0], place=0),
            [part, part],
            (bits, kept_left[lhs], got_left, kept_right, tie(got_right[k])),
            [
                smem, vmem, pl.BlockSpec((None, rows, width), lambda _: (lhs, 0, 0)),
                pl.BlockSpec((None, rows, width), lambda _: (k, 0, 0)), vmem,
            ],
            grid=(1,),
        )
        terms[k] = [keep]
        got[k] = swap(tie(send), "dp", masks[0])

    def arrive(name, stage):
        terms[name].append(tie(got[name]))
        if stage:
            terms[name][:-1] = [
                take(x, bit(scatter.masks[stage]), scatter.strides[stage])
                for x in terms[name][:-1]
            ]

    def total_of(name):
        return sum(x.astype(full) for x in terms[name])[0]

    def scatter_step(stage):
        def step(name):
            arrive(name, stage)
            mask, stride = scatter.masks[stage + 1], scatter.strides[stage + 1]
            send = sum(take(x, 1 - bit(mask), stride).astype(full) for x in terms[name])
            got[name] = swap(tie(send.astype(low)), "dp", mask)

        return step

    def gather_start(name, payload):
        terms[name] = tie(payload)
        got[name] = swap(terms[name], "dp", gathers[name].masks[last])

    def down_step(name):
        arrive(name, last)
        grad = total_of(name) / group_count
        at = layer if name == "near" else 1 - layer
        held = [
            lax.dynamic_index_in_dim(jnp.swapaxes(x, 1, 2), at, 0, keepdims=False)
            for x in (down_master, down_m, down_v)
        ]
        new = adam_apply(*held, grad, weight_decay)
        updated[name] = (grad, *new)
        gather_start(name, new[0][None].astype(low))

    def proj_step(name):
        arrive(name, last)
        grad = total_of(name) / group_count
        cols = slice(name * width, (name + 1) * width)
        new = adam_apply(
            proj_master[0, :, cols], proj_m[0, :, cols], proj_v[0, :, cols], grad, weight_decay
        )
        updated[name] = (grad, *new)
        gather_start(name, new[0][None].astype(low))

    def woven(name, stage):
        mask, stride = gathers[name].masks[stage], gathers[name].strides[stage]
        return weave(terms[name], tie(got[name]), bit(mask), stride)

    def gather_step(stage):
        def step(name):
            terms[name] = tie(woven(name, stage))
            got[name] = swap(terms[name], "dp", gathers[name].masks[stage - 1])

        return step

    def copy_proj_step(name):
        ins, aliases = (bits, terms[name], tie(got[name])), {}
        if proj_copy:
            ins, aliases = (*ins, proj_copy.pop()), {3: 0}
        spec = pl.BlockSpec((group_count, share, width), lambda _: (0, 0, name))
        held = gathers[name]
        proj_copy.append(
            call(
                functools.partial(
                    copy_columns, stride=held.strides[0],
                    place=held.masks[0].bit_length() - 1,
                ),
                pltpu.HBM((group_count, share, wide), low), ins,
                [smem, vmem, vmem] + [anywhere] * len(aliases), out_specs=spec, aliases=aliases,
                grid=(1,),
            )
        )

    def copy_down_step(name):
        ins, aliases = (bits, terms[name], tie(got[name])), {}
        if down_copy:
            ins, aliases = (*ins, down_copy.pop()), {3: 0}
        held = gathers[name]
        down_copy.append(
            call(
                functools.partial(
                    copy_turned, stride=held.strides[0], place=held.masks[0].bit_length() - 1,
                    here=len(masks), far=int(name == "far"),
                ),
                pltpu.HBM((2, width, width), low), ins,
                [smem, vmem, vmem] + [anywhere] * len(aliases),
                (
                    pltpu.VMEM((group_count, share, width), full), pltpu.VMEM((width, width), low),
                    pltpu.SemaphoreType.DMA(()),
                ),
                out_specs=hbm, aliases=aliases,
            )
        )

    halvings = [scatter_step(stage) for stage in range(last)]
    doublings = [gather_step(stage) for stage in range(last, 0, -1)]
    todo = {
        name: halvings
        + [down_step if name in ("near", "far") else proj_step]
        + doublings
        + [copy_down_step if name in ("near", "far") else copy_proj_step]
        for name in gathers
    }
    flight = ["near"]

    def advance():
        name = flight.pop(0)
        todo[name].pop(0)(name)
        if todo[name]:
            flight.append(name)

    def by_layer(near, far):
        return jnp.where(at_first, jnp.stack([near, far]), jnp.stack([far, near]))

    sums = jnp.concatenate([sums_one[:5], sums_two[:7]], 0)
    sums = sums + swap(sums, "section", 1)
    vector_sums = [sums]

    def vector_step(mask):
        def step(name):
            vector_sums[0] = tie(vector_sums[0] + tie(got[name]))
            if mask:
                got[name] = swap(vector_sums[0], "dp", mask)
            else:
                got[name] = swap(vector_sums[0], "section", 2)

        return step

    def vector_last(name):
        updated[name] = by_layer(vector_sums[0], tie(got[name]))

    todo["vectors"] = [vector_step(mask) for mask in (*masks[1:], 0)] + [vector_last]
    begin(0)
    advance()
    far = swap(far, "section", 2)
    for name in (1, 2, 3, "far"):
        begin(name)
        if name == 1:
            got["vectors"] = swap(tie(vector_sums[0]), "dp", masks[0])
            flight.append("vectors")
        while flight[0] != name:
            advance()
    while flight:
        advance()

    vec_grad = updated["vectors"] / group_count
    vec_moments = adam_apply(vectors, vec_m, vec_v, vec_grad, 0.0)

    def in_order(kept, got):
        return by_core(jnp.concatenate([kept, got], 0), jnp.concatenate([got, kept], 0))[None]

    return (
        in_order(kept_left[2], got_left[2]),
        in_order(kept_grad, got_grad),
        *[jnp.concatenate([updated[k][i] for k in range(4)], 1)[None] for i in range(4)],
        proj_copy[0].reshape(1, width, wide),
        *[
            jnp.swapaxes(by_layer(updated["near"][i], updated["far"][i]), 1, 2) for i in range(4)
        ],
        down_copy[0],
        vec_grad,
        vec_moments[1],
        vec_moments[2],
    )


def solution(mesh):
    shared = P("section", "dp", None)
    split = P(None, "section", "dp")
    placed = (
        P("dp", None), P("dp", None), P("dp", None), P("dp", None),
        P("section", None, None), shared, shared, shared,
        P(None, "section", None), split, split, split, P(), P(), P(),
    )
    return jax.shard_map(
        shards,
        mesh=mesh,
        in_specs=placed,
        out_specs=(
            shared, shared, shared, shared, shared, shared,
            P("section", None, None), split, split, split, split,
            P(None, "section", None), P(), P(), P(),
        ),
        check_vma=False,
    )
```

```python
import functools
import math

import jax
import jax.numpy as jnp
from jax import lax
from jax.experimental import pallas as pl
from jax.experimental.pallas import tpu as pltpu
from jax.sharding import PartitionSpec as P

HEADS = 12
HEAD_PAIRS = HEADS // 2

norm_eps = 1e-05
beta_one = 0.9
beta_two = 0.98
adam_eps = 1e-06
learn_rate = 0.001
weight_decay = 0.01
adam_step = 100.0

low = jnp.bfloat16
full = jnp.float32

vmem = pl.BlockSpec(memory_space=pltpu.VMEM)
smem = pl.BlockSpec(memory_space=pltpu.SMEM)
anywhere = pl.BlockSpec(memory_space=pl.ANY)
hbm = pl.BlockSpec(memory_space=pltpu.HBM)


def dot(a, b):
    return lax.dot_general(a, b, (((1,), (0,)), ((), ())), preferred_element_type=full)


def dot_right(a, b):
    return lax.dot_general(a, b, (((1,), (1,)), ((), ())), preferred_element_type=full)


def dot_left(a, b):
    return lax.dot_general(a, b, (((0,), (0,)), ((), ())), preferred_element_type=full)


def row_mean(z):
    return jnp.mean(z, -1, keepdims=True)


def norm_rows(z):
    centered = z - row_mean(z)
    inv = lax.rsqrt(row_mean(centered * centered) + norm_eps)
    return centered * inv, inv


def norm_rows_back(upstream, normed, inv, gain):
    scaled = upstream * gain
    return inv * (scaled - row_mean(scaled) - normed * row_mean(scaled * normed))


def live_rows(rows, live_count, seq_len):
    return lax.broadcasted_iota(jnp.int32, (rows, 1), 0) < live_count * seq_len


def column_sum(block):
    return jnp.sum(block, 0, keepdims=True)


def call(kernel, outs, ins, specs, scratch=(), grid=(), out_specs=None, limit=12, cost=0, aliases=None):
    return pl.pallas_call(
        kernel,
        grid=grid,
        out_shape=outs,
        in_specs=specs,
        out_specs=out_specs or jax.tree.map(lambda _: vmem, outs),
        scratch_shapes=list(scratch),
        input_output_aliases=aliases or {},
        compiler_params=pltpu.CompilerParams(vmem_limit_bytes=limit << 20),
        cost_estimate=pl.CostEstimate(flops=cost * 10**9, bytes_accessed=0, transcendentals=0),
    )(*ins)


def pair_masks(seq_len):
    first = lax.broadcasted_iota(jnp.int32, (seq_len, 128), 1) < 64
    return first


def spread_pair(block, first):
    zero = jnp.zeros_like(block)
    return jnp.concatenate([jnp.where(first, block, zero), jnp.where(first, zero, block)], 0)


def pair_probs(q, keys_two, same_doc, scale, seq_len):
    scores = dot_right(q, keys_two) * scale
    parts = []
    for half in range(2):
        part = jnp.where(same_doc, scores[:, half * seq_len : (half + 1) * seq_len], -1e30)
        exponent = jnp.exp(part - jnp.max(part, -1, keepdims=True))
        parts.append(exponent / jnp.sum(exponent, -1, keepdims=True))
    return parts


class Blocks:
    def __init__(self, *refs):
        self.refs = refs

    def __call__(self, k):
        if len(self.refs) > 1:
            return self.refs[k][...]
        (ref,) = self.refs
        width = ref.shape[1] // 4
        return ref[:, k * width : (k + 1) * width]


def attend_forward(
    hidden, doc_row, doc_col, vec, attn, live, qkv_ref, ctx_ref, n_ref, r_ref, h_next,
    probs_ref=None,
):
    rows, width = hidden.shape
    seq_len = doc_row.shape[1]
    scale = (width // HEADS) ** (-0.5)
    for part in range(3):
        block = dot(hidden, attn(part))
        if part == 0:
            block = block + vec[0:1, :]
        if part == 2:
            block = block + vec[1:2, :]
        qkv_ref[:, part * width : (part + 1) * width] = block.astype(low)
    first = pair_masks(seq_len)
    for s in range(rows // seq_len):
        at = slice(s * seq_len, (s + 1) * seq_len)
        same_doc = doc_col[at, :] == doc_row[s : s + 1, :]
        for p in range(HEAD_PAIRS):
            q, k, v = (
                qkv_ref[at, part * width + p * 128 : part * width + (p + 1) * 128]
                for part in range(3)
            )
            probs = pair_probs(q, spread_pair(k, first), same_doc, scale, seq_len)
            if probs_ref is not None:
                probs_ref[s * HEAD_PAIRS + p] = jnp.concatenate(probs, 1)
            probs_low = jnp.concatenate([x.astype(low) for x in probs], 1)
            ctx_ref[at, p * 128 : (p + 1) * 128] = dot(probs_low, spread_pair(v, first)).astype(low)
    z = hidden.astype(full) + (dot(ctx_ref[...], attn(3)) + vec[2:3, :])
    normed, inv = norm_rows(z)
    n_ref[...] = normed
    r_ref[...] = jnp.broadcast_to(inv, r_ref.shape)
    h_next[...] = jnp.where(live, normed * vec[3:4, :] + vec[4:5, :], 0.0).astype(low)


def feed_up(h_ref, vec, feed, act_ref, slope_ref):
    hidden = h_ref[...]
    for k in range(4):
        pre = dot(hidden, feed(k)) + vec[5 + k : 6 + k, :]
        half_cdf = 0.5 * (1.0 + lax.erf(pre * (1.0 / math.sqrt(2.0))))
        act_ref[k] = (pre * half_cdf).astype(low)
        slope_ref[k] = (
            half_cdf + pre * jnp.exp(-0.5 * pre * pre) * (1.0 / math.sqrt(2.0 * math.pi))
        ).astype(slope_ref.dtype)


def feed_down(h_ref, act_ref, section, vec, downs, live, h_next, n_ref, r_ref):
    total = h_ref[...].astype(full) + vec[9:10, :]
    for m in range(4):
        total = total + dot(act_ref[section ^ m], downs(m))
    finish_second(total, vec, live, h_next, n_ref, r_ref)


def finish_second(total, vec, live, h_next, n_ref, r_ref):
    normed, inv = norm_rows(total)
    n_ref[...] = normed
    r_ref[...] = jnp.broadcast_to(inv, r_ref.shape)
    h_next[...] = jnp.where(live, normed * vec[10:11, :] + vec[11:12, :], 0.0).astype(low)


def feed_back(
    upstream, n_ref, r_ref, slope_ref, section, vec, downs, feed, db_ref, dpre_ref, sums, loads=()
):
    width = n_ref.shape[1]
    normed = n_ref[...]
    dz = norm_rows_back(upstream, normed, r_ref[:, :1], vec[10:11, :])
    db = dz.astype(low)
    if db_ref is not None:
        db_ref[...] = db
        sums[4:5, :] = column_sum(db.astype(full))
        sums[5:6, :] = column_sum(upstream * normed)
        sums[6:7, :] = column_sum(upstream)
        sums[7:8, :] = jnp.zeros((1, width), full)
    for m in range(4):
        at = section ^ m
        if loads:
            loads[m].wait()
        dact = dot_right(db, downs(m))
        if m == 0 and loads:
            loads[4].wait()
        dpre_ref[at] = (dact * slope_ref[at].astype(full)).astype(low)
    total = dz
    for k in range(4):
        if loads:
            loads[5 + k].wait()
        dpre = dpre_ref[k]
        if db_ref is not None:
            sums[k : k + 1, :] = column_sum(dpre.astype(full))
        total = total + dot_right(dpre, feed(k))
    return total


def attend_back(
    upstream, n_ref, r_ref, qkv_ref, doc_row, doc_col, vec, attn, dqkvd_ref, dctx_buf, sums,
    loads=(), probs_ref=None,
):
    rows, width = n_ref.shape
    seq_len = doc_row.shape[1]
    scale = (width // HEADS) ** (-0.5)
    normed = n_ref[...]
    dz = norm_rows_back(upstream, normed, r_ref[:, :1], vec[3:4, :])
    da = dz.astype(low)
    dqkvd_ref[3] = da
    if sums is not None:
        sums[2:3, :] = column_sum(da.astype(full))
        sums[3:4, :] = column_sum(upstream * normed)
        sums[4:5, :] = column_sum(upstream)
        sums[5:8, :] = jnp.zeros((3, width), full)
    if loads:
        loads[0].wait()
    dctx_buf[...] = dot_right(da, attn(3)).astype(low)
    if loads:
        loads[1].wait()
    first = pair_masks(seq_len)
    for s in range(rows // seq_len):
        at = slice(s * seq_len, (s + 1) * seq_len)
        same_doc = doc_col[at, :] == doc_row[s : s + 1, :]
        for p in range(HEAD_PAIRS):
            here = slice(p * 128, (p + 1) * 128)
            q, k, v = (
                qkv_ref[at, part * width + p * 128 : part * width + (p + 1) * 128]
                for part in range(3)
            )
            keys_two = spread_pair(k, first)
            dctx = dctx_buf[at, here]
            if probs_ref is None:
                probs = pair_probs(q, keys_two, same_doc, scale, seq_len)
            else:
                both = probs_ref[s * HEAD_PAIRS + p]
                probs = [both[:, :seq_len], both[:, seq_len:]]
            probs_low = jnp.concatenate([x.astype(low) for x in probs], 1)
            dv_two = dot_left(probs_low, dctx)
            dqkvd_ref[2, at, here] = jnp.where(
                first, dv_two[:seq_len, :], dv_two[seq_len:, :]
            ).astype(low)
            dprobs = dot_right(dctx, spread_pair(v, first))
            dscores = []
            for half in range(2):
                part = dprobs[:, half * seq_len : (half + 1) * seq_len]
                inner = jnp.sum(probs[half] * part, -1, keepdims=True)
                dscores.append((probs[half] * (part - inner)).astype(low))
            dscores = jnp.concatenate(dscores, 1)
            dqkvd_ref[0, at, here] = (dot(dscores, keys_two) * scale).astype(low)
            dk_two = dot_left(dscores, q)
            dqkvd_ref[1, at, here] = (
                jnp.where(first, dk_two[:seq_len, :], dk_two[seq_len:, :]) * scale
            ).astype(low)
    total = dz
    if loads:
        loads[2].wait()
    for k in range(3):
        block = dqkvd_ref[k]
        if sums is not None and k != 1:
            sums[k // 2 : k // 2 + 1, :] = column_sum(block.astype(full))
        total = total + dot_right(block, attn(k))
    return total


class Stores:
    def __init__(self, targets, sources, sems):
        self.copies = [
            pltpu.make_async_copy(source, target, sems.at[at])
            for at, (target, source) in enumerate(zip(targets, sources))
        ]

    def __call__(self, which):
        for at in which:
            self.copies[at].start()

    def wait(self):
        for copy in self.copies:
            copy.wait()


def first_kernel(
    scal, h_ref, doc_row, doc_col, vec, attn_ref, feed_ref,
    *refs,
):
    store = Stores(refs[:7], refs[7:14], refs[14])
    qkv_ref, ctx_ref, n_ref, r_ref, h_next, act_ref, slope_ref = refs[7:14]
    live = live_rows(h_ref.shape[0], scal[2], doc_row.shape[1])
    attend_forward(
        h_ref[...], doc_row, doc_col, vec, Blocks(attn_ref), live, qkv_ref, ctx_ref, n_ref, r_ref,
        h_next,
    )
    store(range(5))
    feed_up(h_next, vec, Blocks(feed_ref), act_ref, slope_ref)
    store((5, 6))
    store.wait()


def near_down_kernel(scal, h_ref, act_ref, vec, d0, d1, total):
    total[...] = h_ref[...].astype(full) + vec[9:10, :] + (
        dot(act_ref[scal[1]], d0[...]) + dot(act_ref[scal[1] ^ 1], d1[...])
    )


def next_down_kernel(scal, total_ref, act_ref, block, total):
    total[...] = total_ref[...] + dot(act_ref[scal[1] ^ 2], block[...])


def second_kernel(scal, total_ref, act_ref, vec, d3, *refs, seq_len):
    store = Stores(refs[:3], refs[3:6], refs[6])
    rows = total_ref.shape[0]
    total = total_ref[...] + dot(act_ref[scal[1] ^ 3], d3[...])
    finish_second(total, vec, live_rows(rows, scal[2], seq_len), *refs[3:6])
    store(range(3))
    store.wait()


def turn_kernel(
    scal, h_ref, e_ref, doc_row, doc_col, vec, attn_ref, feed_ref, d0, d1, d2, d3, *refs
):
    low_ref, bufs = refs[20], refs[21:31]
    dpre_buf, dqkvd_buf, dctx_buf, probs_buf, out_sems = refs[31:]
    qkv_ref, ctx_ref, n_one, r_one, h_one, act_ref, slope_ref, h_two, n_two, r_two = bufs
    rows, seq_len = h_ref.shape[0], doc_row.shape[1]

    @pl.when(scal[1] >= 2)
    def _():
        store = Stores(refs[10:20], bufs, out_sems)
        attn, feed, downs = Blocks(attn_ref), Blocks(feed_ref), Blocks(d0, d1, d2, d3)
        live = live_rows(rows, scal[2], seq_len)
        attend_forward(
            h_ref[...], doc_row, doc_col, vec, attn, live, qkv_ref, ctx_ref, n_one, r_one, h_one,
            probs_buf,
        )
        store(range(5))
        feed_up(h_one, vec, feed, act_ref, slope_ref)
        store((5, 6))
        feed_down(h_one, act_ref, scal[1], vec, downs, live, h_two, n_two, r_two)
        store((7, 8, 9))
        upstream = jnp.where(live, e_ref[...], 0.0)
        total = feed_back(
            upstream, n_two, r_two, slope_ref, scal[1], vec, downs, feed, None, dpre_buf, None
        )
        upstream = jnp.where(live, total.astype(low).astype(full), 0.0)
        total = attend_back(
            upstream, n_one, r_one, qkv_ref, doc_row, doc_col, vec, attn, dqkvd_buf, dctx_buf, None,
            probs_ref=probs_buf,
        )
        low_ref[...] = total.astype(low)
        store.wait()


def back_second_kernel(
    scal, low_ref, vec, *refs, seq_len,
):
    sources, (db_ref, dpre_ref, dh_ref, sums) = refs[:9], refs[9:13]
    targets, sems = refs[13:22], refs[22]
    n_ref, r_ref, e_ref, d0, slope_ref, d1, d2, d3, feed_ref = targets
    width = n_ref.shape[1]
    parts = [pl.ds(k * width, width) for k in range(4)]
    loads = Stores(
        (*targets[:8], *[feed_ref.at[:, part] for part in parts]),
        (*sources[:8], *[sources[8].at[:, part] for part in parts]),
        sems,
    )
    loads((0, 1))
    pl.when(scal[1] >= 2)(loads.copies[2].start)
    loads(range(3, 12))
    loads.copies[0].wait()
    loads.copies[1].wait()
    pl.when(scal[1] >= 2)(loads.copies[2].wait)
    waits = [loads.copies[at] for at in (3, 5, 6, 7, 4, 8, 9, 10, 11)]
    upstream = jnp.where(scal[1] < 2, low_ref[...].astype(full), e_ref[...])
    upstream = jnp.where(live_rows(n_ref.shape[0], scal[2], seq_len), upstream, 0.0)
    dh_ref[...] = feed_back(
        upstream, n_ref, r_ref, slope_ref, scal[1], vec, Blocks(d0, d1, d2, d3), Blocks(feed_ref),
        db_ref, dpre_ref, sums, waits,
    )


def back_first_kernel(scal, e_ref, doc_row, doc_col, vec, *refs):
    *sources, attn_hbm = refs[:5]
    kept_ref, sent_ref, dh_ref, sums = refs[5:9]
    n_ref, r_ref, qkv_ref, dpre_ref, attn_ref, dctx_buf, dqkvd_ref, sems = refs[9:]
    width = n_ref.shape[1]
    out_cols, in_cols = pl.ds(3 * width, width), pl.ds(0, 3 * width)
    loads = Stores(
        (n_ref, r_ref, attn_ref.at[:, out_cols], qkv_ref, attn_ref.at[:, in_cols], dpre_ref),
        (*sources[:2], attn_hbm.at[:, out_cols], sources[2], attn_hbm.at[:, in_cols], sources[3]),
        sems,
    )
    loads(range(6))
    live = live_rows(n_ref.shape[0], scal[2], doc_row.shape[1])
    upstream = jnp.where(live, e_ref[...].astype(low).astype(full), 0.0)
    for at in range(2):
        loads.copies[at].wait()
    dh_ref[...] = attend_back(
        upstream, n_ref, r_ref, qkv_ref, doc_row, doc_col, vec, Blocks(attn_ref), dqkvd_ref,
        dctx_buf, sums, loads.copies[2:5],
    )
    loads.copies[5].wait()

    @pl.when(scal[0] == 0)
    def _():
        kept_ref[...] = dqkvd_ref[...]
        sent_ref[...] = dpre_ref[...]

    @pl.when(scal[0] != 0)
    def _():
        kept_ref[...] = dpre_ref[...]
        sent_ref[...] = dqkvd_ref[...]


def split_blocks(total, keep, send, bit, stride):
    half, share, cols = keep.shape
    blocks = total.reshape(2 * half, share, cols)
    for i in range(half):
        base = (i // stride) * 2 * stride + i % stride

        @pl.when(bit == 0)
        def _():
            keep[i] = blocks[base].astype(low)
            send[i] = blocks[base + stride].astype(low)

        @pl.when(bit != 0)
        def _():
            keep[i] = blocks[base + stride].astype(low)
            send[i] = blocks[base].astype(low)


def down_gradient(
    bits, act_own, act_other, db_own, db_other, keep, send, far, *, stride, place, here
):
    t = bits[here]
    total = dot_left(db_own[...], act_own[1 - t]) + dot_left(db_other[...], act_other[1 - t])
    far[...] = total.reshape(far.shape).astype(low)
    total = dot_left(db_own[...], act_own[t]) + dot_left(db_other[...], act_other[t])
    split_blocks(total, keep, send, bits[place], stride)


def weight_gradient(
    bits, left_own, left_other, right_own, right_other, keep, send, *, stride, place
):
    total = dot_left(left_own[...], right_own[...]) + dot_left(left_other[...], right_other[...])
    split_blocks(total, keep, send, bits[place], stride)


def adam_apply(weight_now, first_moment, second_moment, gradient, decay_rate):
    first_new = beta_one * first_moment + (1.0 - beta_one) * gradient
    second_new = beta_two * second_moment + (1.0 - beta_two) * gradient * gradient
    update = (
        first_new
        / (1.0 - beta_one**adam_step)
        / (jnp.sqrt(second_new / (1.0 - beta_two**adam_step)) + adam_eps)
    )
    return (weight_now - learn_rate * (update + decay_rate * weight_now), first_new, second_new)


def copy_columns(bits, keep, got, *refs, stride, place):
    out = refs[-1]
    bit = bits[place]
    for i in range(keep.shape[0]):
        base = (i // stride) * 2 * stride + i % stride
        out[base + bit * stride] = keep[i]
        out[base + (1 - bit) * stride] = got[i]


def copy_turned(bits, keep, got, *refs, stride, place, here, far):
    out, buf, turned, sem = refs[-4:]
    bit = bits[place]
    for i in range(keep.shape[0]):
        base = (i // stride) * 2 * stride + i % stride
        buf[base + bit * stride] = keep[i].astype(full)
        buf[base + (1 - bit) * stride] = got[i].astype(full)
    count, share, cols = buf.shape
    turned[...] = buf[...].reshape(count * share, cols).T.astype(low)
    copy = pltpu.make_async_copy(turned, out.at[bits[here] ^ far], sem)
    copy.start()
    copy.wait()


def swap(block, axis, mask):
    return lax.ppermute(block, axis, [(i, i ^ mask) for i in range(lax.axis_size(axis))])


def masks_of(count):
    return [1 << b for b in range(count.bit_length() - 1)]


def pick(block, at):
    return lax.dynamic_index_in_dim(block, at, 1, keepdims=False)


def struct(dims, kind):
    return jax.ShapeDtypeStruct(dims, kind)


class Order:
    def __init__(self, masks):
        self.masks = masks
        left = sorted(masks)
        self.strides = []
        for mask in masks:
            self.strides.append(1 << left.index(mask))
            left.remove(mask)


def take(blocks, bit, stride):
    rest = blocks.shape[1:]
    blocks = blocks.reshape(-1, 2, stride, *rest)
    return lax.dynamic_index_in_dim(blocks, bit, 1, keepdims=False).reshape(-1, *rest)


def weave(own, got, bit, stride):
    rest = own.shape[1:]
    own, got = own.reshape(-1, 1, stride, *rest), got.reshape(-1, 1, stride, *rest)
    both = jnp.where(
        bit == 0, jnp.concatenate([own, got], 1), jnp.concatenate([got, own], 1)
    )
    return both.reshape(-1, *rest)


def shards(
    hidden_in, out_grad, seq_counts, segment_ids, proj, proj_master, proj_m, proj_v,
    down, down_master, down_m, down_v, vectors, vec_m, vec_v,
):
    group_count = lax.axis_size("dp")
    section = lax.axis_index("section")
    core, layer = section % 2, section // 2
    width = hidden_in.shape[1]
    seq_len = segment_ids.shape[1]
    slots = segment_ids.shape[0] // 2
    rows = slots * seq_len
    wide = proj.shape[2]
    at_first = layer == 0

    own_w = proj[0]
    other_w = swap(own_w, "section", 1)
    crossing = lax.dynamic_index_in_dim(down, 1 - layer, 0, keepdims=False)
    d2 = swap(crossing, "section", 2)
    whole_down, other_w = lax.optimization_barrier((down, other_w))
    d0 = lax.dynamic_index_in_dim(whole_down, layer, 0, keepdims=False)
    d1 = swap(d0, "section", 1)
    vec = lax.dynamic_index_in_dim(vectors, layer, 0, keepdims=False)

    own_in = lax.dynamic_slice_in_dim(hidden_in, core * rows, rows, 0)
    own_cot = lax.dynamic_slice_in_dim(out_grad, core * rows, rows, 0)
    docs = lax.dynamic_slice_in_dim(segment_ids, core * slots, slots, 0)
    doc_col = docs.reshape(rows, 1)
    live_count = lax.dynamic_index_in_dim(seq_counts[0], core, 0, keepdims=False)
    scal = jnp.stack([core, section, live_count]).astype(jnp.int32)

    def by_core(at_zero, at_one):
        return jnp.where(core == 0, at_zero, at_one)

    attn_w, feed_w = by_core(own_w, other_w), by_core(other_w, own_w)
    rows_low, rows_full = struct((rows, width), low), struct((rows, width), full)
    blocks, inverse = struct((4, rows, width), low), struct((rows, 128), full)
    residuals = [
        struct((rows, 3 * width), low), rows_low, rows_full, inverse, rows_low, blocks, blocks,
        rows_low, rows_full, inverse,
    ]

    kept_out = [pltpu.HBM(x.shape, x.dtype) for x in residuals]

    def scratch(shape):
        return pltpu.VMEM(shape.shape, shape.dtype)

    def hop(block, towards):
        route = [(0, 2), (1, 3)] if towards else [(2, 0), (3, 1)]
        return lax.ppermute(block, "section", route)

    first = call(
        first_kernel, kept_out[:7], (scal, own_in, docs, doc_col, vec, attn_w, feed_w),
        [smem] + [vmem] * 6, [*map(scratch, residuals[:7]), pltpu.SemaphoreType.DMA((7,))],
        out_specs=[hbm] * 7, limit=24, cost=6,
    )
    own_part = call(
        near_down_kernel, rows_full, (scal, first[4], first[5], vec, d0, d1), [smem] + [vmem] * 5,
        limit=16, cost=2,
    )
    d2, own_part = lax.optimization_barrier((d2, own_part))
    downs = (d0, d1, d2, swap(d2, "section", 1))
    own_part = call(
        next_down_kernel, rows_full, (scal, own_part, first[5], d2), [smem] + [vmem] * 3,
        limit=16, cost=2,
    )
    second = call(
        functools.partial(second_kernel, seq_len=seq_len),
        kept_out[7:], (scal, own_part, first[5], vec, downs[3]),
        [smem] + [vmem] * 4, [*map(scratch, residuals[7:]), pltpu.SemaphoreType.DMA((3,))],
        out_specs=[hbm] * 3, limit=16, cost=4,
    )
    arrived = hop(second[0], True)
    layer_in = jnp.where(at_first, own_in, arrived)
    ins = (scal, arrived, own_cot, docs, doc_col, vec, attn_w, feed_w, *downs, *first, *second)
    *kept, back_low = call(
        turn_kernel, [*kept_out, rows_low], ins,
        [smem] + [vmem] * 11 + [hbm] * 10,
        [
            *map(scratch, (*residuals, blocks, blocks, rows_low)),
            pltpu.VMEM((slots * HEAD_PAIRS, seq_len, 2 * seq_len), full),
            pltpu.SemaphoreType.DMA((10,)),
        ],
        out_specs=[hbm] * 10 + [vmem], limit=36, cost=25,
        aliases={len(ins) - 10 + i: i for i in range(10)},
    )
    qkv, ctx, n_one, r_one, h_one, act, slope, h_two, n_two, r_two = kept

    kept_left = (by_core(layer_in, h_one), by_core(ctx, h_one), by_core(h_one, h_two))
    sent_left = jnp.stack(
        [by_core(h_one, layer_in), by_core(h_one, ctx), by_core(h_two, h_one)]
    )
    got_left = swap(sent_left, "section", 1)
    act_pairs = act.reshape(2, 2, rows, width)
    act_kept = pick(act_pairs, core)
    act_got = swap(pick(act_pairs, 1 - core), "section", 1)

    masks = masks_of(group_count)
    index = lax.axis_index("dp")
    share = width // group_count
    half = group_count // 2
    bits = jnp.stack([(index // mask) % 2 for mask in masks] + [layer]).astype(jnp.int32)
    scatter = Order(masks)
    turned = masks[1:] + masks[:1]
    gathers = {
        name: Order(turned if name in (3,) else masks) for name in ("near", 0, 1, 2, 3, "far")
    }
    last = len(masks) - 1
    part = struct((half, share, width), low)

    def bit(mask):
        return (index // mask) % 2

    token = [jnp.zeros((8, 128), full)]

    def tie(*arrays):
        *arrays, token[0] = lax.optimization_barrier((*arrays, token[0]))
        return arrays if len(arrays) > 1 else arrays[0]

    db, dpre, dh_two, sums_two = call(
        functools.partial(back_second_kernel, seq_len=seq_len),
        [rows_low, blocks, rows_full, struct((8, width), full)],
        (
            scal, hop(back_low, False), vec, n_two, r_two, own_cot, downs[0], slope, *downs[1:],
            feed_w,
        ),
        [smem, vmem, vmem] + [hbm] * 9,
        (
            *map(scratch, (rows_full, inverse, rows_full, d0, blocks, d0, d0, d0, own_w)),
            pltpu.SemaphoreType.DMA((12,)),
        ),
        limit=58, cost=6,
    )
    keep, send, far = call(
        functools.partial(
            down_gradient, stride=scatter.strides[0], place=0, here=len(masks)
        ),
        [part, part, struct((group_count, share, width), low)],
        (bits, act_kept, act_got, db, swap(db, "section", 1)),
        [smem] + [vmem] * 4, cost=4,
    )
    terms = {"near": [keep]}
    dh_two, send, far = lax.optimization_barrier((dh_two, send, far))
    got = {"near": swap(send, "dp", masks[0])}
    kept_right, sent_right, dh_one, sums_one = call(
        back_first_kernel,
        [blocks, blocks, rows_full, struct((8, width), full)],
        (scal, dh_two, docs, doc_col, vec, n_one, r_one, qkv, dpre, attn_w),
        [smem] + [vmem] * 4 + [hbm] * 5,
        (
            *map(scratch, (rows_full, inverse, residuals[0], blocks, own_w, rows_low, blocks)),
            pltpu.SemaphoreType.DMA((6,)),
        ),
        limit=24, cost=9,
    )
    got_right = [swap(sent_right[k], "section", 1) for k in range(4)]
    kept_grad = by_core(dh_one, dh_two)
    got_grad = swap(by_core(dh_two, dh_one), "section", 1)
    proj_copy, down_copy, updated = [], [], {}

    def begin(k):
        flight.append(k)
        if k == "far":
            blocks = tie(far)
            terms[k] = [take(blocks, bit(masks[0]), scatter.strides[0])]
            send = take(blocks, 1 - bit(masks[0]), scatter.strides[0])
            got[k] = swap(tie(send), "dp", masks[0])
            return
        lhs = 0 if k < 3 else 1
        keep, send = call(
            functools.partial(weight_gradient, stride=scatter.strides[0], place=0),
            [part, part],
            (bits, kept_left[lhs], got_left, kept_right, tie(got_right[k])),
            [
                smem, vmem, pl.BlockSpec((None, rows, width), lambda _: (lhs, 0, 0)),
                pl.BlockSpec((None, rows, width), lambda _: (k, 0, 0)), vmem,
            ],
            grid=(1,),
        )
        terms[k] = [keep]
        got[k] = swap(tie(send), "dp", masks[0])

    def arrive(name, stage):
        terms[name].append(tie(got[name]))
        if stage:
            terms[name][:-1] = [
                take(x, bit(scatter.masks[stage]), scatter.strides[stage])
                for x in terms[name][:-1]
            ]

    def total_of(name):
        return sum(x.astype(full) for x in terms[name])[0]

    def scatter_step(stage):
        def step(name):
            arrive(name, stage)
            mask, stride = scatter.masks[stage + 1], scatter.strides[stage + 1]
            send = sum(take(x, 1 - bit(mask), stride).astype(full) for x in terms[name])
            got[name] = swap(tie(send.astype(low)), "dp", mask)

        return step

    def gather_start(name, payload):
        terms[name] = tie(payload)
        got[name] = swap(terms[name], "dp", gathers[name].masks[last])

    def down_step(name):
        arrive(name, last)
        grad = total_of(name) / group_count
        at = layer if name == "near" else 1 - layer
        held = [
            lax.dynamic_index_in_dim(jnp.swapaxes(x, 1, 2), at, 0, keepdims=False)
            for x in (down_master, down_m, down_v)
        ]
        new = adam_apply(*held, grad, weight_decay)
        updated[name] = (grad, *new)
        gather_start(name, new[0][None].astype(low))

    def proj_step(name):
        arrive(name, last)
        grad = total_of(name) / group_count
        cols = slice(name * width, (name + 1) * width)
        new = adam_apply(
            proj_master[0, :, cols], proj_m[0, :, cols], proj_v[0, :, cols], grad, weight_decay
        )
        updated[name] = (grad, *new)
        gather_start(name, new[0][None].astype(low))

    def woven(name, stage):
        mask, stride = gathers[name].masks[stage], gathers[name].strides[stage]
        return weave(terms[name], tie(got[name]), bit(mask), stride)

    def gather_step(stage):
        def step(name):
            terms[name] = tie(woven(name, stage))
            got[name] = swap(terms[name], "dp", gathers[name].masks[stage - 1])

        return step

    def copy_proj_step(name):
        ins, aliases = (bits, terms[name], tie(got[name])), {}
        if proj_copy:
            ins, aliases = (*ins, proj_copy.pop()), {3: 0}
        spec = pl.BlockSpec((group_count, share, width), lambda _: (0, 0, name))
        held = gathers[name]
        proj_copy.append(
            call(
                functools.partial(
                    copy_columns, stride=held.strides[0],
                    place=held.masks[0].bit_length() - 1,
                ),
                pltpu.HBM((group_count, share, wide), low), ins,
                [smem, vmem, vmem] + [anywhere] * len(aliases), out_specs=spec, aliases=aliases,
                grid=(1,),
            )
        )

    def copy_down_step(name):
        ins, aliases = (bits, terms[name], tie(got[name])), {}
        if down_copy:
            ins, aliases = (*ins, down_copy.pop()), {3: 0}
        held = gathers[name]
        down_copy.append(
            call(
                functools.partial(
                    copy_turned, stride=held.strides[0], place=held.masks[0].bit_length() - 1,
                    here=len(masks), far=int(name == "far"),
                ),
                pltpu.HBM((2, width, width), low), ins,
                [smem, vmem, vmem] + [anywhere] * len(aliases),
                (
                    pltpu.VMEM((group_count, share, width), full), pltpu.VMEM((width, width), low),
                    pltpu.SemaphoreType.DMA(()),
                ),
                out_specs=hbm, aliases=aliases,
            )
        )

    halvings = [scatter_step(stage) for stage in range(last)]
    doublings = [gather_step(stage) for stage in range(last, 0, -1)]
    todo = {
        name: halvings
        + [down_step if name in ("near", "far") else proj_step]
        + doublings
        + [copy_down_step if name in ("near", "far") else copy_proj_step]
        for name in gathers
    }
    flight = ["near"]

    def advance():
        name = flight.pop(0)
        todo[name].pop(0)(name)
        if todo[name]:
            flight.append(name)

    def by_layer(near, far):
        return jnp.where(at_first, jnp.stack([near, far]), jnp.stack([far, near]))

    sums = jnp.concatenate([sums_one[:5], sums_two[:7]], 0)
    sums = sums + swap(sums, "section", 1)
    vector_sums = [sums]

    def vector_step(mask):
        def step(name):
            vector_sums[0] = tie(vector_sums[0] + tie(got[name]))
            if mask:
                got[name] = swap(vector_sums[0], "dp", mask)
            else:
                got[name] = swap(vector_sums[0], "section", 2)

        return step

    def vector_last(name):
        updated[name] = by_layer(vector_sums[0], tie(got[name]))

    todo["vectors"] = [vector_step(mask) for mask in (*masks[1:], 0)] + [vector_last]
    begin(0)
    advance()
    far = swap(tie(far), "section", 2)
    for name in (1, 2, 3, 'far'):
        begin(name)
        if name == 1:
            got["vectors"] = swap(tie(vector_sums[0]), "dp", masks[0])
            flight.append("vectors")
        while flight[0] != name:
            advance()
    while flight:
        advance()

    vec_grad = updated["vectors"] / group_count
    vec_moments = adam_apply(vectors, vec_m, vec_v, vec_grad, 0.0)

    def in_order(kept, got):
        return by_core(jnp.concatenate([kept, got], 0), jnp.concatenate([got, kept], 0))[None]

    return (
        in_order(kept_left[2], got_left[2]),
        in_order(kept_grad, got_grad),
        *[jnp.concatenate([updated[k][i] for k in range(4)], 1)[None] for i in range(4)],
        proj_copy[0].reshape(1, width, wide),
        *[
            jnp.swapaxes(by_layer(updated["near"][i], updated["far"][i]), 1, 2) for i in range(4)
        ],
        down_copy[0],
        vec_grad,
        vec_moments[1],
        vec_moments[2],
    )


def solution(mesh):
    shared = P("section", "dp", None)
    split = P(None, "section", "dp")
    placed = (
        P("dp", None), P("dp", None), P("dp", None), P("dp", None),
        P("section", None, None), shared, shared, shared,
        P(None, "section", None), split, split, split, P(), P(), P(),
    )
    return jax.shard_map(
        shards,
        mesh=mesh,
        in_specs=placed,
        out_specs=(
            shared, shared, shared, shared, shared, shared,
            P("section", None, None), split, split, split, split,
            P(None, "section", None), P(), P(), P(),
        ),
        check_vma=False,
    )
```

```python
import functools
import math

import jax
import jax.numpy as jnp
from jax import lax
from jax.experimental import pallas as pl
from jax.experimental.pallas import tpu as pltpu
from jax.sharding import PartitionSpec as P

HEADS = 12
HEAD_PAIRS = HEADS // 2

norm_eps = 1e-05
beta_one = 0.9
beta_two = 0.98
adam_eps = 1e-06
learn_rate = 0.001
weight_decay = 0.01
adam_step = 100.0

low = jnp.bfloat16
full = jnp.float32

vmem = pl.BlockSpec(memory_space=pltpu.VMEM)
smem = pl.BlockSpec(memory_space=pltpu.SMEM)
anywhere = pl.BlockSpec(memory_space=pl.ANY)
hbm = pl.BlockSpec(memory_space=pltpu.HBM)


def dot(a, b):
    return lax.dot_general(a, b, (((1,), (0,)), ((), ())), preferred_element_type=full)


def dot_right(a, b):
    return lax.dot_general(a, b, (((1,), (1,)), ((), ())), preferred_element_type=full)


def dot_left(a, b):
    return lax.dot_general(a, b, (((0,), (0,)), ((), ())), preferred_element_type=full)


def row_mean(z):
    return jnp.mean(z, -1, keepdims=True)


def norm_rows(z):
    centered = z - row_mean(z)
    inv = lax.rsqrt(row_mean(centered * centered) + norm_eps)
    return centered * inv, inv


def norm_rows_back(upstream, normed, inv, gain):
    scaled = upstream * gain
    return inv * (scaled - row_mean(scaled) - normed * row_mean(scaled * normed))


def live_rows(rows, live_count, seq_len):
    return lax.broadcasted_iota(jnp.int32, (rows, 1), 0) < live_count * seq_len


def column_sum(block):
    return jnp.sum(block, 0, keepdims=True)


def call(kernel, outs, ins, specs, scratch=(), grid=(), out_specs=None, limit=12, cost=0, aliases=None):
    return pl.pallas_call(
        kernel,
        grid=grid,
        out_shape=outs,
        in_specs=specs,
        out_specs=out_specs or jax.tree.map(lambda _: vmem, outs),
        scratch_shapes=list(scratch),
        input_output_aliases=aliases or {},
        compiler_params=pltpu.CompilerParams(vmem_limit_bytes=limit << 20),
        cost_estimate=pl.CostEstimate(flops=cost * 10**9, bytes_accessed=0, transcendentals=0),
    )(*ins)


def pair_masks(seq_len):
    first = lax.broadcasted_iota(jnp.int32, (seq_len, 128), 1) < 64
    return first


def spread_pair(block, first):
    zero = jnp.zeros_like(block)
    return jnp.concatenate([jnp.where(first, block, zero), jnp.where(first, zero, block)], 0)


def pair_probs(q, keys_two, same_doc, scale, seq_len):
    scores = dot_right(q, keys_two) * scale
    parts = []
    for half in range(2):
        part = jnp.where(same_doc, scores[:, half * seq_len : (half + 1) * seq_len], -1e30)
        exponent = jnp.exp(part - jnp.max(part, -1, keepdims=True))
        parts.append(exponent / jnp.sum(exponent, -1, keepdims=True))
    return parts


class Blocks:
    def __init__(self, *refs):
        self.refs = refs

    def __call__(self, k):
        if len(self.refs) > 1:
            return self.refs[k][...]
        (ref,) = self.refs
        width = ref.shape[1] // 4
        return ref[:, k * width : (k + 1) * width]


def attend_forward(
    hidden, doc_row, doc_col, vec, attn, live, qkv_ref, ctx_ref, n_ref, r_ref, h_next,
    probs_ref=None,
):
    rows, width = hidden.shape
    seq_len = doc_row.shape[1]
    scale = (width // HEADS) ** (-0.5)
    for part in range(3):
        block = dot(hidden, attn(part))
        if part == 0:
            block = block + vec[0:1, :]
        if part == 2:
            block = block + vec[1:2, :]
        qkv_ref[:, part * width : (part + 1) * width] = block.astype(low)
    first = pair_masks(seq_len)
    for s in range(rows // seq_len):
        at = slice(s * seq_len, (s + 1) * seq_len)
        same_doc = doc_col[at, :] == doc_row[s : s + 1, :]
        for p in range(HEAD_PAIRS):
            q, k, v = (
                qkv_ref[at, part * width + p * 128 : part * width + (p + 1) * 128]
                for part in range(3)
            )
            probs = pair_probs(q, spread_pair(k, first), same_doc, scale, seq_len)
            if probs_ref is not None:
                probs_ref[s * HEAD_PAIRS + p] = jnp.concatenate(probs, 1)
            probs_low = jnp.concatenate([x.astype(low) for x in probs], 1)
            ctx_ref[at, p * 128 : (p + 1) * 128] = dot(probs_low, spread_pair(v, first)).astype(low)
    z = hidden.astype(full) + (dot(ctx_ref[...], attn(3)) + vec[2:3, :])
    normed, inv = norm_rows(z)
    n_ref[...] = normed
    r_ref[...] = jnp.broadcast_to(inv, r_ref.shape)
    h_next[...] = jnp.where(live, normed * vec[3:4, :] + vec[4:5, :], 0.0).astype(low)


def feed_up(h_ref, vec, feed, act_ref, slope_ref):
    hidden = h_ref[...]
    for k in range(4):
        pre = dot(hidden, feed(k)) + vec[5 + k : 6 + k, :]
        half_cdf = 0.5 * (1.0 + lax.erf(pre * (1.0 / math.sqrt(2.0))))
        act_ref[k] = (pre * half_cdf).astype(low)
        slope_ref[k] = (
            half_cdf + pre * jnp.exp(-0.5 * pre * pre) * (1.0 / math.sqrt(2.0 * math.pi))
        ).astype(slope_ref.dtype)


def feed_down(h_ref, act_ref, section, vec, downs, live, h_next, n_ref, r_ref):
    total = h_ref[...].astype(full) + vec[9:10, :]
    for m in range(4):
        total = total + dot(act_ref[section ^ m], downs(m))
    finish_second(total, vec, live, h_next, n_ref, r_ref)


def finish_second(total, vec, live, h_next, n_ref, r_ref):
    normed, inv = norm_rows(total)
    n_ref[...] = normed
    r_ref[...] = jnp.broadcast_to(inv, r_ref.shape)
    h_next[...] = jnp.where(live, normed * vec[10:11, :] + vec[11:12, :], 0.0).astype(low)


def feed_back(
    upstream, n_ref, r_ref, slope_ref, section, vec, downs, feed, db_ref, dpre_ref, sums, loads=()
):
    width = n_ref.shape[1]
    normed = n_ref[...]
    dz = norm_rows_back(upstream, normed, r_ref[:, :1], vec[10:11, :])
    db = dz.astype(low)
    if db_ref is not None:
        db_ref[...] = db
        sums[4:5, :] = column_sum(db.astype(full))
        sums[5:6, :] = column_sum(upstream * normed)
        sums[6:7, :] = column_sum(upstream)
        sums[7:8, :] = jnp.zeros((1, width), full)
    for m in range(4):
        at = section ^ m
        if loads:
            loads[m].wait()
        dact = dot_right(db, downs(m))
        if m == 0 and loads:
            loads[4].wait()
        dpre_ref[at] = (dact * slope_ref[at].astype(full)).astype(low)
    total = dz
    for k in range(4):
        if loads:
            loads[5 + k].wait()
        dpre = dpre_ref[k]
        if db_ref is not None:
            sums[k : k + 1, :] = column_sum(dpre.astype(full))
        total = total + dot_right(dpre, feed(k))
    return total


def attend_back(
    upstream, n_ref, r_ref, qkv_ref, doc_row, doc_col, vec, attn, dqkvd_ref, dctx_buf, sums,
    loads=(), probs_ref=None,
):
    rows, width = n_ref.shape
    seq_len = doc_row.shape[1]
    scale = (width // HEADS) ** (-0.5)
    normed = n_ref[...]
    dz = norm_rows_back(upstream, normed, r_ref[:, :1], vec[3:4, :])
    da = dz.astype(low)
    dqkvd_ref[3] = da
    if sums is not None:
        sums[2:3, :] = column_sum(da.astype(full))
        sums[3:4, :] = column_sum(upstream * normed)
        sums[4:5, :] = column_sum(upstream)
        sums[5:8, :] = jnp.zeros((3, width), full)
    if loads:
        loads[0].wait()
    dctx_buf[...] = dot_right(da, attn(3)).astype(low)
    if loads:
        loads[1].wait()
    first = pair_masks(seq_len)
    for s in range(rows // seq_len):
        at = slice(s * seq_len, (s + 1) * seq_len)
        same_doc = doc_col[at, :] == doc_row[s : s + 1, :]
        for p in range(HEAD_PAIRS):
            here = slice(p * 128, (p + 1) * 128)
            q, k, v = (
                qkv_ref[at, part * width + p * 128 : part * width + (p + 1) * 128]
                for part in range(3)
            )
            keys_two = spread_pair(k, first)
            dctx = dctx_buf[at, here]
            if probs_ref is None:
                probs = pair_probs(q, keys_two, same_doc, scale, seq_len)
            else:
                both = probs_ref[s * HEAD_PAIRS + p]
                probs = [both[:, :seq_len], both[:, seq_len:]]
            probs_low = jnp.concatenate([x.astype(low) for x in probs], 1)
            dv_two = dot_left(probs_low, dctx)
            dqkvd_ref[2, at, here] = jnp.where(
                first, dv_two[:seq_len, :], dv_two[seq_len:, :]
            ).astype(low)
            dprobs = dot_right(dctx, spread_pair(v, first))
            dscores = []
            for half in range(2):
                part = dprobs[:, half * seq_len : (half + 1) * seq_len]
                inner = jnp.sum(probs[half] * part, -1, keepdims=True)
                dscores.append((probs[half] * (part - inner)).astype(low))
            dscores = jnp.concatenate(dscores, 1)
            dqkvd_ref[0, at, here] = (dot(dscores, keys_two) * scale).astype(low)
            dk_two = dot_left(dscores, q)
            dqkvd_ref[1, at, here] = (
                jnp.where(first, dk_two[:seq_len, :], dk_two[seq_len:, :]) * scale
            ).astype(low)
    total = dz
    if loads:
        loads[2].wait()
    for k in range(3):
        block = dqkvd_ref[k]
        if sums is not None and k != 1:
            sums[k // 2 : k // 2 + 1, :] = column_sum(block.astype(full))
        total = total + dot_right(block, attn(k))
    return total


class Stores:
    def __init__(self, targets, sources, sems):
        self.copies = [
            pltpu.make_async_copy(source, target, sems.at[at])
            for at, (target, source) in enumerate(zip(targets, sources))
        ]

    def __call__(self, which):
        for at in which:
            self.copies[at].start()

    def wait(self):
        for copy in self.copies:
            copy.wait()


def first_kernel(
    scal, h_ref, doc_row, doc_col, vec, attn_ref, feed_ref,
    *refs,
):
    store = Stores(refs[:7], refs[7:14], refs[14])
    qkv_ref, ctx_ref, n_ref, r_ref, h_next, act_ref, slope_ref = refs[7:14]
    live = live_rows(h_ref.shape[0], scal[2], doc_row.shape[1])
    attend_forward(
        h_ref[...], doc_row, doc_col, vec, Blocks(attn_ref), live, qkv_ref, ctx_ref, n_ref, r_ref,
        h_next,
    )
    store(range(5))
    feed_up(h_next, vec, Blocks(feed_ref), act_ref, slope_ref)
    store((5, 6))
    store.wait()


def near_down_kernel(scal, h_ref, act_ref, vec, d0, d1, total):
    total[...] = h_ref[...].astype(full) + vec[9:10, :] + (
        dot(act_ref[scal[1]], d0[...]) + dot(act_ref[scal[1] ^ 1], d1[...])
    )


def next_down_kernel(scal, total_ref, act_ref, block, total):
    total[...] = total_ref[...] + dot(act_ref[scal[1] ^ 2], block[...])


def second_kernel(scal, total_ref, act_ref, vec, d3, *refs, seq_len):
    store = Stores(refs[:3], refs[3:6], refs[6])
    rows = total_ref.shape[0]
    total = total_ref[...] + dot(act_ref[scal[1] ^ 3], d3[...])
    finish_second(total, vec, live_rows(rows, scal[2], seq_len), *refs[3:6])
    store(range(3))
    store.wait()


def turn_kernel(
    scal, h_ref, e_ref, doc_row, doc_col, vec, attn_ref, feed_ref, d0, d1, d2, d3, *refs
):
    low_ref, bufs = refs[20], refs[21:31]
    dpre_buf, dqkvd_buf, dctx_buf, probs_buf, out_sems = refs[31:]
    qkv_ref, ctx_ref, n_one, r_one, h_one, act_ref, slope_ref, h_two, n_two, r_two = bufs
    rows, seq_len = h_ref.shape[0], doc_row.shape[1]

    @pl.when(scal[1] >= 2)
    def _():
        store = Stores(refs[10:20], bufs, out_sems)
        attn, feed, downs = Blocks(attn_ref), Blocks(feed_ref), Blocks(d0, d1, d2, d3)
        live = live_rows(rows, scal[2], seq_len)
        attend_forward(
            h_ref[...], doc_row, doc_col, vec, attn, live, qkv_ref, ctx_ref, n_one, r_one, h_one,
            probs_buf,
        )
        store(range(5))
        feed_up(h_one, vec, feed, act_ref, slope_ref)
        store((5, 6))
        feed_down(h_one, act_ref, scal[1], vec, downs, live, h_two, n_two, r_two)
        store((7, 8, 9))
        upstream = jnp.where(live, e_ref[...], 0.0)
        total = feed_back(
            upstream, n_two, r_two, slope_ref, scal[1], vec, downs, feed, None, dpre_buf, None
        )
        upstream = jnp.where(live, total.astype(low).astype(full), 0.0)
        total = attend_back(
            upstream, n_one, r_one, qkv_ref, doc_row, doc_col, vec, attn, dqkvd_buf, dctx_buf, None,
            probs_ref=probs_buf,
        )
        low_ref[...] = total.astype(low)
        store.wait()


def back_second_kernel(
    scal, low_ref, vec, *refs, seq_len,
):
    sources, (db_ref, dpre_ref, dh_ref, sums) = refs[:9], refs[9:13]
    targets, sems = refs[13:22], refs[22]
    n_ref, r_ref, e_ref, d0, slope_ref, d1, d2, d3, feed_ref = targets
    width = n_ref.shape[1]
    parts = [pl.ds(k * width, width) for k in range(4)]
    loads = Stores(
        (*targets[:8], *[feed_ref.at[:, part] for part in parts]),
        (*sources[:8], *[sources[8].at[:, part] for part in parts]),
        sems,
    )
    loads((0, 1))
    pl.when(scal[1] >= 2)(loads.copies[2].start)
    loads(range(3, 12))
    loads.copies[0].wait()
    loads.copies[1].wait()
    pl.when(scal[1] >= 2)(loads.copies[2].wait)
    waits = [loads.copies[at] for at in (3, 5, 6, 7, 4, 8, 9, 10, 11)]
    upstream = jnp.where(scal[1] < 2, low_ref[...].astype(full), e_ref[...])
    upstream = jnp.where(live_rows(n_ref.shape[0], scal[2], seq_len), upstream, 0.0)
    dh_ref[...] = feed_back(
        upstream, n_ref, r_ref, slope_ref, scal[1], vec, Blocks(d0, d1, d2, d3), Blocks(feed_ref),
        db_ref, dpre_ref, sums, waits,
    )


def back_first_kernel(scal, e_ref, doc_row, doc_col, vec, *refs):
    *sources, attn_hbm = refs[:5]
    kept_ref, sent_ref, dh_ref, sums = refs[5:9]
    n_ref, r_ref, qkv_ref, dpre_ref, attn_ref, dctx_buf, dqkvd_ref, sems = refs[9:]
    width = n_ref.shape[1]
    out_cols, in_cols = pl.ds(3 * width, width), pl.ds(0, 3 * width)
    loads = Stores(
        (n_ref, r_ref, attn_ref.at[:, out_cols], qkv_ref, attn_ref.at[:, in_cols], dpre_ref),
        (*sources[:2], attn_hbm.at[:, out_cols], sources[2], attn_hbm.at[:, in_cols], sources[3]),
        sems,
    )
    loads(range(6))
    live = live_rows(n_ref.shape[0], scal[2], doc_row.shape[1])
    upstream = jnp.where(live, e_ref[...].astype(low).astype(full), 0.0)
    for at in range(2):
        loads.copies[at].wait()
    dh_ref[...] = attend_back(
        upstream, n_ref, r_ref, qkv_ref, doc_row, doc_col, vec, Blocks(attn_ref), dqkvd_ref,
        dctx_buf, sums, loads.copies[2:5],
    )
    loads.copies[5].wait()

    @pl.when(scal[0] == 0)
    def _():
        kept_ref[...] = dqkvd_ref[...]
        sent_ref[...] = dpre_ref[...]

    @pl.when(scal[0] != 0)
    def _():
        kept_ref[...] = dpre_ref[...]
        sent_ref[...] = dqkvd_ref[...]


def split_blocks(total, keep, send, bit, stride):
    half, share, cols = keep.shape
    blocks = total.reshape(2 * half, share, cols)
    for i in range(half):
        base = (i // stride) * 2 * stride + i % stride

        @pl.when(bit == 0)
        def _():
            keep[i] = blocks[base].astype(low)
            send[i] = blocks[base + stride].astype(low)

        @pl.when(bit != 0)
        def _():
            keep[i] = blocks[base + stride].astype(low)
            send[i] = blocks[base].astype(low)


def down_gradient(
    bits, act_own, act_other, db_own, db_other, keep, send, far, *, stride, place, here
):
    t = bits[here]
    total = dot_left(db_own[...], act_own[1 - t]) + dot_left(db_other[...], act_other[1 - t])
    far[...] = total.reshape(far.shape).astype(low)
    total = dot_left(db_own[...], act_own[t]) + dot_left(db_other[...], act_other[t])
    split_blocks(total, keep, send, bits[place], stride)


def weight_gradient(
    bits, left_own, left_other, right_own, right_other, keep, send, *, stride, place
):
    total = dot_left(left_own[...], right_own[...]) + dot_left(left_other[...], right_other[...])
    split_blocks(total, keep, send, bits[place], stride)


def adam_apply(weight_now, first_moment, second_moment, gradient, decay_rate):
    first_new = beta_one * first_moment + (1.0 - beta_one) * gradient
    second_new = beta_two * second_moment + (1.0 - beta_two) * gradient * gradient
    update = (
        first_new
        / (1.0 - beta_one**adam_step)
        / (jnp.sqrt(second_new / (1.0 - beta_two**adam_step)) + adam_eps)
    )
    return (weight_now - learn_rate * (update + decay_rate * weight_now), first_new, second_new)


def copy_columns(bits, keep, got, *refs, stride, place):
    out = refs[-1]
    bit = bits[place]
    for i in range(keep.shape[0]):
        base = (i // stride) * 2 * stride + i % stride
        out[base + bit * stride] = keep[i]
        out[base + (1 - bit) * stride] = got[i]


def copy_turned(bits, keep, got, *refs, stride, place, here, far):
    out, buf, turned, sem = refs[-4:]
    bit = bits[place]
    for i in range(keep.shape[0]):
        base = (i // stride) * 2 * stride + i % stride
        buf[base + bit * stride] = keep[i].astype(full)
        buf[base + (1 - bit) * stride] = got[i].astype(full)
    count, share, cols = buf.shape
    turned[...] = buf[...].reshape(count * share, cols).T.astype(low)
    copy = pltpu.make_async_copy(turned, out.at[bits[here] ^ far], sem)
    copy.start()
    copy.wait()


def swap(block, axis, mask):
    return lax.ppermute(block, axis, [(i, i ^ mask) for i in range(lax.axis_size(axis))])


def masks_of(count):
    return [1 << b for b in range(count.bit_length() - 1)]


def pick(block, at):
    return lax.dynamic_index_in_dim(block, at, 1, keepdims=False)


def struct(dims, kind):
    return jax.ShapeDtypeStruct(dims, kind)


class Order:
    def __init__(self, masks):
        self.masks = masks
        left = sorted(masks)
        self.strides = []
        for mask in masks:
            self.strides.append(1 << left.index(mask))
            left.remove(mask)


def take(blocks, bit, stride):
    rest = blocks.shape[1:]
    blocks = blocks.reshape(-1, 2, stride, *rest)
    return lax.dynamic_index_in_dim(blocks, bit, 1, keepdims=False).reshape(-1, *rest)


def weave(own, got, bit, stride):
    rest = own.shape[1:]
    own, got = own.reshape(-1, 1, stride, *rest), got.reshape(-1, 1, stride, *rest)
    both = jnp.where(
        bit == 0, jnp.concatenate([own, got], 1), jnp.concatenate([got, own], 1)
    )
    return both.reshape(-1, *rest)


def shards(
    hidden_in, out_grad, seq_counts, segment_ids, proj, proj_master, proj_m, proj_v,
    down, down_master, down_m, down_v, vectors, vec_m, vec_v,
):
    group_count = lax.axis_size("dp")
    section = lax.axis_index("section")
    core, layer = section % 2, section // 2
    width = hidden_in.shape[1]
    seq_len = segment_ids.shape[1]
    slots = segment_ids.shape[0] // 2
    rows = slots * seq_len
    wide = proj.shape[2]
    at_first = layer == 0

    own_w = proj[0]
    other_w = swap(own_w, "section", 1)
    crossing = lax.dynamic_index_in_dim(down, 1 - layer, 0, keepdims=False)
    d2 = swap(crossing, "section", 2)
    whole_down, other_w = lax.optimization_barrier((down, other_w))
    d0 = lax.dynamic_index_in_dim(whole_down, layer, 0, keepdims=False)
    d1 = swap(d0, "section", 1)
    vec = lax.dynamic_index_in_dim(vectors, layer, 0, keepdims=False)

    own_in = lax.dynamic_slice_in_dim(hidden_in, core * rows, rows, 0)
    own_cot = lax.dynamic_slice_in_dim(out_grad, core * rows, rows, 0)
    docs = lax.dynamic_slice_in_dim(segment_ids, core * slots, slots, 0)
    doc_col = docs.reshape(rows, 1)
    live_count = lax.dynamic_index_in_dim(seq_counts[0], core, 0, keepdims=False)
    scal = jnp.stack([core, section, live_count]).astype(jnp.int32)

    def by_core(at_zero, at_one):
        return jnp.where(core == 0, at_zero, at_one)

    attn_w, feed_w = by_core(own_w, other_w), by_core(other_w, own_w)
    rows_low, rows_full = struct((rows, width), low), struct((rows, width), full)
    blocks, inverse = struct((4, rows, width), low), struct((rows, 128), full)
    residuals = [
        struct((rows, 3 * width), low), rows_low, rows_full, inverse, rows_low, blocks, blocks,
        rows_low, rows_full, inverse,
    ]

    kept_out = [pltpu.HBM(x.shape, x.dtype) for x in residuals]

    def scratch(shape):
        return pltpu.VMEM(shape.shape, shape.dtype)

    def hop(block, towards):
        route = [(0, 2), (1, 3)] if towards else [(2, 0), (3, 1)]
        return lax.ppermute(block, "section", route)

    first = call(
        first_kernel, kept_out[:7], (scal, own_in, docs, doc_col, vec, attn_w, feed_w),
        [smem] + [vmem] * 6, [*map(scratch, residuals[:7]), pltpu.SemaphoreType.DMA((7,))],
        out_specs=[hbm] * 7, limit=24, cost=6,
    )
    own_part = call(
        near_down_kernel, rows_full, (scal, first[4], first[5], vec, d0, d1), [smem] + [vmem] * 5,
        limit=16, cost=2,
    )
    d2, own_part = lax.optimization_barrier((d2, own_part))
    downs = (d0, d1, d2, swap(d2, "section", 1))
    own_part = call(
        next_down_kernel, rows_full, (scal, own_part, first[5], d2), [smem] + [vmem] * 3,
        limit=16, cost=2,
    )
    second = call(
        functools.partial(second_kernel, seq_len=seq_len),
        kept_out[7:], (scal, own_part, first[5], vec, downs[3]),
        [smem] + [vmem] * 4, [*map(scratch, residuals[7:]), pltpu.SemaphoreType.DMA((3,))],
        out_specs=[hbm] * 3, limit=16, cost=4,
    )
    arrived = hop(second[0], True)
    layer_in = jnp.where(at_first, own_in, arrived)
    ins = (scal, arrived, own_cot, docs, doc_col, vec, attn_w, feed_w, *downs, *first, *second)
    *kept, back_low = call(
        turn_kernel, [*kept_out, rows_low], ins,
        [smem] + [vmem] * 11 + [hbm] * 10,
        [
            *map(scratch, (*residuals, blocks, blocks, rows_low)),
            pltpu.VMEM((slots * HEAD_PAIRS, seq_len, 2 * seq_len), full),
            pltpu.SemaphoreType.DMA((10,)),
        ],
        out_specs=[hbm] * 10 + [vmem], limit=44, cost=25,
        aliases={len(ins) - 10 + i: i for i in range(10)},
    )
    qkv, ctx, n_one, r_one, h_one, act, slope, h_two, n_two, r_two = kept

    kept_left = (by_core(layer_in, h_one), by_core(ctx, h_one), by_core(h_one, h_two))
    sent_left = jnp.stack(
        [by_core(h_one, layer_in), by_core(h_one, ctx), by_core(h_two, h_one)]
    )
    got_left = swap(sent_left, "section", 1)
    act_pairs = act.reshape(2, 2, rows, width)
    act_kept = pick(act_pairs, core)
    act_got = swap(pick(act_pairs, 1 - core), "section", 1)

    masks = masks_of(group_count)
    index = lax.axis_index("dp")
    share = width // group_count
    half = group_count // 2
    bits = jnp.stack([(index // mask) % 2 for mask in masks] + [layer]).astype(jnp.int32)
    scatter = Order(masks)
    turned = masks[1:] + masks[:1]
    gathers = {
        name: Order(turned if name in (3,) else masks) for name in ("near", 0, 1, 2, 3, "far")
    }
    last = len(masks) - 1
    part = struct((half, share, width), low)

    def bit(mask):
        return (index // mask) % 2

    token = [jnp.zeros((8, 128), full)]

    def tie(*arrays):
        *arrays, token[0] = lax.optimization_barrier((*arrays, token[0]))
        return arrays if len(arrays) > 1 else arrays[0]

    db, dpre, dh_two, sums_two = call(
        functools.partial(back_second_kernel, seq_len=seq_len),
        [rows_low, blocks, rows_full, struct((8, width), full)],
        (
            scal, hop(back_low, False), vec, n_two, r_two, own_cot, downs[0], slope, *downs[1:],
            feed_w,
        ),
        [smem, vmem, vmem] + [hbm] * 9,
        (
            *map(scratch, (rows_full, inverse, rows_full, d0, blocks, d0, d0, d0, own_w)),
            pltpu.SemaphoreType.DMA((12,)),
        ),
        limit=58, cost=6,
    )
    keep, send, far = call(
        functools.partial(
            down_gradient, stride=scatter.strides[0], place=0, here=len(masks)
        ),
        [part, part, struct((group_count, share, width), low)],
        (bits, act_kept, act_got, db, swap(db, "section", 1)),
        [smem] + [vmem] * 4, cost=4,
    )
    terms = {"near": [keep]}
    dh_two, send, far = lax.optimization_barrier((dh_two, send, far))
    got = {"near": swap(send, "dp", masks[0])}
    kept_right, sent_right, dh_one, sums_one = call(
        back_first_kernel,
        [blocks, blocks, rows_full, struct((8, width), full)],
        (scal, dh_two, docs, doc_col, vec, n_one, r_one, qkv, dpre, attn_w),
        [smem] + [vmem] * 4 + [hbm] * 5,
        (
            *map(scratch, (rows_full, inverse, residuals[0], blocks, own_w, rows_low, blocks)),
            pltpu.SemaphoreType.DMA((6,)),
        ),
        limit=24, cost=9,
    )
    got_right = [swap(sent_right[k], "section", 1) for k in range(4)]
    kept_grad = by_core(dh_one, dh_two)
    got_grad = swap(by_core(dh_two, dh_one), "section", 1)
    proj_copy, down_copy, updated = [], [], {}

    def begin(k):
        flight.append(k)
        if k == "far":
            blocks = tie(far)
            terms[k] = [take(blocks, bit(masks[0]), scatter.strides[0])]
            send = take(blocks, 1 - bit(masks[0]), scatter.strides[0])
            got[k] = swap(tie(send), "dp", masks[0])
            return
        lhs = 0 if k < 3 else 1
        keep, send = call(
            functools.partial(weight_gradient, stride=scatter.strides[0], place=0),
            [part, part],
            (bits, kept_left[lhs], got_left, kept_right, tie(got_right[k])),
            [
                smem, vmem, pl.BlockSpec((None, rows, width), lambda _: (lhs, 0, 0)),
                pl.BlockSpec((None, rows, width), lambda _: (k, 0, 0)), vmem,
            ],
            grid=(1,),
        )
        terms[k] = [keep]
        got[k] = swap(tie(send), "dp", masks[0])

    def arrive(name, stage):
        terms[name].append(tie(got[name]))
        if stage:
            terms[name][:-1] = [
                take(x, bit(scatter.masks[stage]), scatter.strides[stage])
                for x in terms[name][:-1]
            ]

    def total_of(name):
        return sum(x.astype(full) for x in terms[name])[0]

    def scatter_step(stage):
        def step(name):
            arrive(name, stage)
            mask, stride = scatter.masks[stage + 1], scatter.strides[stage + 1]
            send = sum(take(x, 1 - bit(mask), stride).astype(full) for x in terms[name])
            got[name] = swap(tie(send.astype(low)), "dp", mask)

        return step

    def gather_start(name, payload):
        terms[name] = tie(payload)
        got[name] = swap(terms[name], "dp", gathers[name].masks[last])

    def down_step(name):
        arrive(name, last)
        grad = total_of(name) / group_count
        at = layer if name == "near" else 1 - layer
        held = [
            lax.dynamic_index_in_dim(jnp.swapaxes(x, 1, 2), at, 0, keepdims=False)
            for x in (down_master, down_m, down_v)
        ]
        new = adam_apply(*held, grad, weight_decay)
        updated[name] = (grad, *new)
        gather_start(name, new[0][None].astype(low))

    def proj_step(name):
        arrive(name, last)
        grad = total_of(name) / group_count
        cols = slice(name * width, (name + 1) * width)
        new = adam_apply(
            proj_master[0, :, cols], proj_m[0, :, cols], proj_v[0, :, cols], grad, weight_decay
        )
        updated[name] = (grad, *new)
        gather_start(name, new[0][None].astype(low))

    def woven(name, stage):
        mask, stride = gathers[name].masks[stage], gathers[name].strides[stage]
        return weave(terms[name], tie(got[name]), bit(mask), stride)

    def gather_step(stage):
        def step(name):
            terms[name] = tie(woven(name, stage))
            got[name] = swap(terms[name], "dp", gathers[name].masks[stage - 1])

        return step

    def copy_proj_step(name):
        ins, aliases = (bits, terms[name], tie(got[name])), {}
        if proj_copy:
            ins, aliases = (*ins, proj_copy.pop()), {3: 0}
        spec = pl.BlockSpec((group_count, share, width), lambda _: (0, 0, name))
        held = gathers[name]
        proj_copy.append(
            call(
                functools.partial(
                    copy_columns, stride=held.strides[0],
                    place=held.masks[0].bit_length() - 1,
                ),
                pltpu.HBM((group_count, share, wide), low), ins,
                [smem, vmem, vmem] + [anywhere] * len(aliases), out_specs=spec, aliases=aliases,
                grid=(1,),
            )
        )

    def copy_down_step(name):
        ins, aliases = (bits, terms[name], tie(got[name])), {}
        if down_copy:
            ins, aliases = (*ins, down_copy.pop()), {3: 0}
        held = gathers[name]
        down_copy.append(
            call(
                functools.partial(
                    copy_turned, stride=held.strides[0], place=held.masks[0].bit_length() - 1,
                    here=len(masks), far=int(name == "far"),
                ),
                pltpu.HBM((2, width, width), low), ins,
                [smem, vmem, vmem] + [anywhere] * len(aliases),
                (
                    pltpu.VMEM((group_count, share, width), full), pltpu.VMEM((width, width), low),
                    pltpu.SemaphoreType.DMA(()),
                ),
                out_specs=hbm, aliases=aliases,
            )
        )

    halvings = [scatter_step(stage) for stage in range(last)]
    doublings = [gather_step(stage) for stage in range(last, 0, -1)]
    todo = {
        name: halvings
        + [down_step if name in ("near", "far") else proj_step]
        + doublings
        + [copy_down_step if name in ("near", "far") else copy_proj_step]
        for name in gathers
    }
    flight = ["near"]

    def advance():
        name = flight.pop(0)
        todo[name].pop(0)(name)
        if todo[name]:
            flight.append(name)

    def by_layer(near, far):
        return jnp.where(at_first, jnp.stack([near, far]), jnp.stack([far, near]))

    sums = jnp.concatenate([sums_one[:5], sums_two[:7]], 0)
    sums = sums + swap(sums, "section", 1)
    vector_sums = [sums]

    def vector_step(mask):
        def step(name):
            vector_sums[0] = tie(vector_sums[0] + tie(got[name]))
            if mask:
                got[name] = swap(vector_sums[0], "dp", mask)
            else:
                got[name] = swap(vector_sums[0], "section", 2)

        return step

    def vector_last(name):
        updated[name] = by_layer(vector_sums[0], tie(got[name]))

    todo["vectors"] = [vector_step(mask) for mask in (*masks[1:], 0)] + [vector_last]
    begin(0)
    advance()
    far = swap(tie(far), "section", 2)
    for name in (1, 2, 3, 'far'):
        begin(name)
        if name == 1:
            got["vectors"] = swap(tie(vector_sums[0]), "dp", masks[0])
            flight.append("vectors")
        while flight[0] != name:
            advance()
    while flight:
        advance()

    vec_grad = updated["vectors"] / group_count
    vec_moments = adam_apply(vectors, vec_m, vec_v, vec_grad, 0.0)

    def in_order(kept, got):
        return by_core(jnp.concatenate([kept, got], 0), jnp.concatenate([got, kept], 0))[None]

    return (
        in_order(kept_left[2], got_left[2]),
        in_order(kept_grad, got_grad),
        *[jnp.concatenate([updated[k][i] for k in range(4)], 1)[None] for i in range(4)],
        proj_copy[0].reshape(1, width, wide),
        *[
            jnp.swapaxes(by_layer(updated["near"][i], updated["far"][i]), 1, 2) for i in range(4)
        ],
        down_copy[0],
        vec_grad,
        vec_moments[1],
        vec_moments[2],
    )


def solution(mesh):
    shared = P("section", "dp", None)
    split = P(None, "section", "dp")
    placed = (
        P("dp", None), P("dp", None), P("dp", None), P("dp", None),
        P("section", None, None), shared, shared, shared,
        P(None, "section", None), split, split, split, P(), P(), P(),
    )
    return jax.shard_map(
        shards,
        mesh=mesh,
        in_specs=placed,
        out_specs=(
            shared, shared, shared, shared, shared, shared,
            P("section", None, None), split, split, split, split,
            P(None, "section", None), P(), P(), P(),
        ),
        check_vma=False,
    )
```

```python
import functools
import math

import jax
import jax.numpy as jnp
from jax import lax
from jax.experimental import pallas as pl
from jax.experimental.pallas import tpu as pltpu
from jax.sharding import PartitionSpec as P

HEADS = 12
HEAD_PAIRS = HEADS // 2

norm_eps = 1e-05
beta_one = 0.9
beta_two = 0.98
adam_eps = 1e-06
learn_rate = 0.001
weight_decay = 0.01
adam_step = 100.0

low = jnp.bfloat16
full = jnp.float32

vmem = pl.BlockSpec(memory_space=pltpu.VMEM)
smem = pl.BlockSpec(memory_space=pltpu.SMEM)
anywhere = pl.BlockSpec(memory_space=pl.ANY)
hbm = pl.BlockSpec(memory_space=pltpu.HBM)


def dot(a, b):
    return lax.dot_general(a, b, (((1,), (0,)), ((), ())), preferred_element_type=full)


def dot_right(a, b):
    return lax.dot_general(a, b, (((1,), (1,)), ((), ())), preferred_element_type=full)


def dot_left(a, b):
    return lax.dot_general(a, b, (((0,), (0,)), ((), ())), preferred_element_type=full)


def row_mean(z):
    return jnp.mean(z, -1, keepdims=True)


def norm_rows(z):
    centered = z - row_mean(z)
    inv = lax.rsqrt(row_mean(centered * centered) + norm_eps)
    return centered * inv, inv


def norm_rows_back(upstream, normed, inv, gain):
    scaled = upstream * gain
    return inv * (scaled - row_mean(scaled) - normed * row_mean(scaled * normed))


def live_rows(rows, live_count, seq_len):
    return lax.broadcasted_iota(jnp.int32, (rows, 1), 0) < live_count * seq_len


def column_sum(block):
    return jnp.sum(block, 0, keepdims=True)


def call(kernel, outs, ins, specs, scratch=(), grid=(), out_specs=None, limit=12, cost=0, aliases=None):
    return pl.pallas_call(
        kernel,
        grid=grid,
        out_shape=outs,
        in_specs=specs,
        out_specs=out_specs or jax.tree.map(lambda _: vmem, outs),
        scratch_shapes=list(scratch),
        input_output_aliases=aliases or {},
        compiler_params=pltpu.CompilerParams(vmem_limit_bytes=limit << 20),
        cost_estimate=pl.CostEstimate(flops=cost * 10**9, bytes_accessed=0, transcendentals=0),
    )(*ins)


def pair_masks(seq_len):
    first = lax.broadcasted_iota(jnp.int32, (seq_len, 128), 1) < 64
    return first


def spread_pair(block, first):
    zero = jnp.zeros_like(block)
    return jnp.concatenate([jnp.where(first, block, zero), jnp.where(first, zero, block)], 0)


def pair_probs(q, keys_two, same_doc, scale, seq_len):
    scores = dot_right(q, keys_two) * scale
    parts = []
    for half in range(2):
        part = jnp.where(same_doc, scores[:, half * seq_len : (half + 1) * seq_len], -1e30)
        exponent = jnp.exp(part - jnp.max(part, -1, keepdims=True))
        parts.append(exponent / jnp.sum(exponent, -1, keepdims=True))
    return parts


class Blocks:
    def __init__(self, *refs):
        self.refs = refs

    def __call__(self, k):
        if len(self.refs) > 1:
            return self.refs[k][...]
        (ref,) = self.refs
        width = ref.shape[1] // 4
        return ref[:, k * width : (k + 1) * width]


def attend_forward(
    hidden, doc_row, doc_col, vec, attn, live, qkv_ref, ctx_ref, n_ref, r_ref, h_next,
    probs_ref=None,
):
    rows, width = hidden.shape
    seq_len = doc_row.shape[1]
    scale = (width // HEADS) ** (-0.5)
    for part in range(3):
        block = dot(hidden, attn(part))
        if part == 0:
            block = block + vec[0:1, :]
        if part == 2:
            block = block + vec[1:2, :]
        qkv_ref[:, part * width : (part + 1) * width] = block.astype(low)
    first = pair_masks(seq_len)
    for s in range(rows // seq_len):
        at = slice(s * seq_len, (s + 1) * seq_len)
        same_doc = doc_col[at, :] == doc_row[s : s + 1, :]
        for p in range(HEAD_PAIRS):
            q, k, v = (
                qkv_ref[at, part * width + p * 128 : part * width + (p + 1) * 128]
                for part in range(3)
            )
            probs = pair_probs(q, spread_pair(k, first), same_doc, scale, seq_len)
            if probs_ref is not None:
                probs_ref[s * HEAD_PAIRS + p] = jnp.concatenate(probs, 1)
            probs_low = jnp.concatenate([x.astype(low) for x in probs], 1)
            ctx_ref[at, p * 128 : (p + 1) * 128] = dot(probs_low, spread_pair(v, first)).astype(low)
    z = hidden.astype(full) + (dot(ctx_ref[...], attn(3)) + vec[2:3, :])
    normed, inv = norm_rows(z)
    n_ref[...] = normed
    r_ref[...] = jnp.broadcast_to(inv, r_ref.shape)
    h_next[...] = jnp.where(live, normed * vec[3:4, :] + vec[4:5, :], 0.0).astype(low)


def feed_up(h_ref, vec, feed, act_ref, slope_ref):
    hidden = h_ref[...]
    for k in range(4):
        pre = dot(hidden, feed(k)) + vec[5 + k : 6 + k, :]
        half_cdf = 0.5 * (1.0 + lax.erf(pre * (1.0 / math.sqrt(2.0))))
        act_ref[k] = (pre * half_cdf).astype(low)
        slope_ref[k] = (
            half_cdf + pre * jnp.exp(-0.5 * pre * pre) * (1.0 / math.sqrt(2.0 * math.pi))
        ).astype(slope_ref.dtype)


def feed_down(h_ref, act_ref, section, vec, downs, live, h_next, n_ref, r_ref):
    total = h_ref[...].astype(full) + vec[9:10, :]
    for m in range(4):
        total = total + dot(act_ref[section ^ m], downs(m))
    finish_second(total, vec, live, h_next, n_ref, r_ref)


def finish_second(total, vec, live, h_next, n_ref, r_ref):
    normed, inv = norm_rows(total)
    n_ref[...] = normed
    r_ref[...] = jnp.broadcast_to(inv, r_ref.shape)
    h_next[...] = jnp.where(live, normed * vec[10:11, :] + vec[11:12, :], 0.0).astype(low)


def feed_back(
    upstream, n_ref, r_ref, slope_ref, section, vec, downs, feed, db_ref, dpre_ref, sums, loads=()
):
    width = n_ref.shape[1]
    normed = n_ref[...]
    dz = norm_rows_back(upstream, normed, r_ref[:, :1], vec[10:11, :])
    db = dz.astype(low)
    if db_ref is not None:
        db_ref[...] = db
        sums[4:5, :] = column_sum(db.astype(full))
        sums[5:6, :] = column_sum(upstream * normed)
        sums[6:7, :] = column_sum(upstream)
        sums[7:8, :] = jnp.zeros((1, width), full)
    for m in range(4):
        at = section ^ m
        if loads:
            loads[m].wait()
        dact = dot_right(db, downs(m))
        if m == 0 and loads:
            loads[4].wait()
        dpre_ref[at] = (dact * slope_ref[at].astype(full)).astype(low)
    total = dz
    for k in range(4):
        if loads:
            loads[5 + k].wait()
        dpre = dpre_ref[k]
        if db_ref is not None:
            sums[k : k + 1, :] = column_sum(dpre.astype(full))
        total = total + dot_right(dpre, feed(k))
    return total


def attend_back(
    upstream, n_ref, r_ref, qkv_ref, doc_row, doc_col, vec, attn, dqkvd_ref, dctx_buf, sums,
    loads=(), probs_ref=None,
):
    rows, width = n_ref.shape
    seq_len = doc_row.shape[1]
    scale = (width // HEADS) ** (-0.5)
    normed = n_ref[...]
    dz = norm_rows_back(upstream, normed, r_ref[:, :1], vec[3:4, :])
    da = dz.astype(low)
    dqkvd_ref[3] = da
    if sums is not None:
        sums[2:3, :] = column_sum(da.astype(full))
        sums[3:4, :] = column_sum(upstream * normed)
        sums[4:5, :] = column_sum(upstream)
        sums[5:8, :] = jnp.zeros((3, width), full)
    if loads:
        loads[0].wait()
    dctx_buf[...] = dot_right(da, attn(3)).astype(low)
    if loads:
        loads[1].wait()
    first = pair_masks(seq_len)
    for s in range(rows // seq_len):
        at = slice(s * seq_len, (s + 1) * seq_len)
        same_doc = doc_col[at, :] == doc_row[s : s + 1, :]
        for p in range(HEAD_PAIRS):
            here = slice(p * 128, (p + 1) * 128)
            q, k, v = (
                qkv_ref[at, part * width + p * 128 : part * width + (p + 1) * 128]
                for part in range(3)
            )
            keys_two = spread_pair(k, first)
            dctx = dctx_buf[at, here]
            if probs_ref is None:
                probs = pair_probs(q, keys_two, same_doc, scale, seq_len)
            else:
                both = probs_ref[s * HEAD_PAIRS + p]
                probs = [both[:, :seq_len], both[:, seq_len:]]
            probs_low = jnp.concatenate([x.astype(low) for x in probs], 1)
            dv_two = dot_left(probs_low, dctx)
            dqkvd_ref[2, at, here] = jnp.where(
                first, dv_two[:seq_len, :], dv_two[seq_len:, :]
            ).astype(low)
            dprobs = dot_right(dctx, spread_pair(v, first))
            dscores = []
            for half in range(2):
                part = dprobs[:, half * seq_len : (half + 1) * seq_len]
                inner = jnp.sum(probs[half] * part, -1, keepdims=True)
                dscores.append((probs[half] * (part - inner)).astype(low))
            dscores = jnp.concatenate(dscores, 1)
            dqkvd_ref[0, at, here] = (dot(dscores, keys_two) * scale).astype(low)
            dk_two = dot_left(dscores, q)
            dqkvd_ref[1, at, here] = (
                jnp.where(first, dk_two[:seq_len, :], dk_two[seq_len:, :]) * scale
            ).astype(low)
    total = dz
    if loads:
        loads[2].wait()
    for k in range(3):
        block = dqkvd_ref[k]
        if sums is not None and k != 1:
            sums[k // 2 : k // 2 + 1, :] = column_sum(block.astype(full))
        total = total + dot_right(block, attn(k))
    return total


class Stores:
    def __init__(self, targets, sources, sems):
        self.copies = [
            pltpu.make_async_copy(source, target, sems.at[at])
            for at, (target, source) in enumerate(zip(targets, sources))
        ]

    def __call__(self, which):
        for at in which:
            self.copies[at].start()

    def wait(self):
        for copy in self.copies:
            copy.wait()


def first_kernel(
    scal, h_ref, doc_row, doc_col, vec, attn_ref, feed_ref,
    *refs,
):
    store = Stores(refs[:7], refs[7:14], refs[14])
    qkv_ref, ctx_ref, n_ref, r_ref, h_next, act_ref, slope_ref = refs[7:14]
    live = live_rows(h_ref.shape[0], scal[2], doc_row.shape[1])
    attend_forward(
        h_ref[...], doc_row, doc_col, vec, Blocks(attn_ref), live, qkv_ref, ctx_ref, n_ref, r_ref,
        h_next,
    )
    store(range(5))
    feed_up(h_next, vec, Blocks(feed_ref), act_ref, slope_ref)
    store((5, 6))
    store.wait()


def near_down_kernel(scal, h_ref, act_ref, vec, d0, d1, total):
    total[...] = h_ref[...].astype(full) + vec[9:10, :] + (
        dot(act_ref[scal[1]], d0[...]) + dot(act_ref[scal[1] ^ 1], d1[...])
    )


def next_down_kernel(scal, total_ref, act_ref, block, total):
    total[...] = total_ref[...] + dot(act_ref[scal[1] ^ 2], block[...])


def second_kernel(scal, total_ref, act_ref, vec, d3, *refs, seq_len):
    store = Stores(refs[:3], refs[3:6], refs[6])
    rows = total_ref.shape[0]
    total = total_ref[...] + dot(act_ref[scal[1] ^ 3], d3[...])
    finish_second(total, vec, live_rows(rows, scal[2], seq_len), *refs[3:6])
    store(range(3))
    store.wait()


def turn_kernel(
    scal, h_ref, e_ref, doc_row, doc_col, vec, attn_ref, feed_ref, d0, d1, d2, d3, *refs
):
    low_ref, bufs = refs[20], refs[21:31]
    dpre_buf, dqkvd_buf, dctx_buf, probs_buf, out_sems = refs[31:]
    qkv_ref, ctx_ref, n_one, r_one, h_one, act_ref, slope_ref, h_two, n_two, r_two = bufs
    rows, seq_len = h_ref.shape[0], doc_row.shape[1]

    @pl.when(scal[1] >= 2)
    def _():
        store = Stores(refs[10:20], bufs, out_sems)
        attn, feed, downs = Blocks(attn_ref), Blocks(feed_ref), Blocks(d0, d1, d2, d3)
        live = live_rows(rows, scal[2], seq_len)
        attend_forward(
            h_ref[...], doc_row, doc_col, vec, attn, live, qkv_ref, ctx_ref, n_one, r_one, h_one,
            probs_buf,
        )
        store(range(5))
        feed_up(h_one, vec, feed, act_ref, slope_ref)
        store((5, 6))
        feed_down(h_one, act_ref, scal[1], vec, downs, live, h_two, n_two, r_two)
        store((7, 8, 9))
        upstream = jnp.where(live, e_ref[...], 0.0)
        total = feed_back(
            upstream, n_two, r_two, slope_ref, scal[1], vec, downs, feed, None, dpre_buf, None
        )
        upstream = jnp.where(live, total.astype(low).astype(full), 0.0)
        total = attend_back(
            upstream, n_one, r_one, qkv_ref, doc_row, doc_col, vec, attn, dqkvd_buf, dctx_buf, None,
            probs_ref=probs_buf,
        )
        low_ref[...] = total.astype(low)
        store.wait()


def back_second_kernel(
    scal, low_ref, vec, *refs, seq_len,
):
    sources, (db_ref, dpre_ref, dh_ref, sums) = refs[:9], refs[9:13]
    targets, sems = refs[13:22], refs[22]
    n_ref, r_ref, e_ref, d0, slope_ref, d1, d2, d3, feed_ref = targets
    width = n_ref.shape[1]
    parts = [pl.ds(k * width, width) for k in range(4)]
    loads = Stores(
        (*targets[:8], *[feed_ref.at[:, part] for part in parts]),
        (*sources[:8], *[sources[8].at[:, part] for part in parts]),
        sems,
    )
    loads((0, 1))
    pl.when(scal[1] >= 2)(loads.copies[2].start)
    loads(range(3, 6))
    loads.copies[0].wait()
    loads.copies[1].wait()
    loads(range(6, 12))
    pl.when(scal[1] >= 2)(loads.copies[2].wait)
    waits = [loads.copies[at] for at in (3, 5, 6, 7, 4, 8, 9, 10, 11)]
    upstream = jnp.where(scal[1] < 2, low_ref[...].astype(full), e_ref[...])
    upstream = jnp.where(live_rows(n_ref.shape[0], scal[2], seq_len), upstream, 0.0)
    dh_ref[...] = feed_back(
        upstream, n_ref, r_ref, slope_ref, scal[1], vec, Blocks(d0, d1, d2, d3), Blocks(feed_ref),
        db_ref, dpre_ref, sums, waits,
    )


def back_first_kernel(scal, e_ref, doc_row, doc_col, vec, *refs):
    *sources, attn_hbm = refs[:5]
    kept_ref, sent_ref, dh_ref, sums = refs[5:9]
    n_ref, r_ref, qkv_ref, dpre_ref, attn_ref, dctx_buf, dqkvd_ref, sems = refs[9:]
    width = n_ref.shape[1]
    out_cols, in_cols = pl.ds(3 * width, width), pl.ds(0, 3 * width)
    loads = Stores(
        (n_ref, r_ref, attn_ref.at[:, out_cols], qkv_ref, attn_ref.at[:, in_cols], dpre_ref),
        (*sources[:2], attn_hbm.at[:, out_cols], sources[2], attn_hbm.at[:, in_cols], sources[3]),
        sems,
    )
    loads(range(4))
    live = live_rows(n_ref.shape[0], scal[2], doc_row.shape[1])
    upstream = jnp.where(live, e_ref[...].astype(low).astype(full), 0.0)
    for at in range(2):
        loads.copies[at].wait()
    loads((4, 5))
    dh_ref[...] = attend_back(
        upstream, n_ref, r_ref, qkv_ref, doc_row, doc_col, vec, Blocks(attn_ref), dqkvd_ref,
        dctx_buf, sums, loads.copies[2:5],
    )
    loads.copies[5].wait()

    @pl.when(scal[0] == 0)
    def _():
        kept_ref[...] = dqkvd_ref[...]
        sent_ref[...] = dpre_ref[...]

    @pl.when(scal[0] != 0)
    def _():
        kept_ref[...] = dpre_ref[...]
        sent_ref[...] = dqkvd_ref[...]


def split_blocks(total, keep, send, bit, stride):
    half, share, cols = keep.shape
    blocks = total.reshape(2 * half, share, cols)
    for i in range(half):
        base = (i // stride) * 2 * stride + i % stride

        @pl.when(bit == 0)
        def _():
            keep[i] = blocks[base].astype(low)
            send[i] = blocks[base + stride].astype(low)

        @pl.when(bit != 0)
        def _():
            keep[i] = blocks[base + stride].astype(low)
            send[i] = blocks[base].astype(low)


def down_gradient(
    bits, act_own, act_other, db_own, db_other, keep, send, far, *, stride, place, here
):
    t = bits[here]
    total = dot_left(db_own[...], act_own[1 - t]) + dot_left(db_other[...], act_other[1 - t])
    far[...] = total.reshape(far.shape).astype(low)
    total = dot_left(db_own[...], act_own[t]) + dot_left(db_other[...], act_other[t])
    split_blocks(total, keep, send, bits[place], stride)


def weight_gradient(
    bits, left_own, left_other, right_own, right_other, keep, send, *, stride, place
):
    total = dot_left(left_own[...], right_own[...]) + dot_left(left_other[...], right_other[...])
    split_blocks(total, keep, send, bits[place], stride)


def adam_apply(weight_now, first_moment, second_moment, gradient, decay_rate):
    first_new = beta_one * first_moment + (1.0 - beta_one) * gradient
    second_new = beta_two * second_moment + (1.0 - beta_two) * gradient * gradient
    update = (
        first_new
        / (1.0 - beta_one**adam_step)
        / (jnp.sqrt(second_new / (1.0 - beta_two**adam_step)) + adam_eps)
    )
    return (weight_now - learn_rate * (update + decay_rate * weight_now), first_new, second_new)


def copy_columns(bits, keep, got, *refs, stride, place):
    out = refs[-1]
    bit = bits[place]
    for i in range(keep.shape[0]):
        base = (i // stride) * 2 * stride + i % stride
        out[base + bit * stride] = keep[i]
        out[base + (1 - bit) * stride] = got[i]


def copy_turned(bits, keep, got, *refs, stride, place, here, far):
    out, buf, turned, sem = refs[-4:]
    bit = bits[place]
    for i in range(keep.shape[0]):
        base = (i // stride) * 2 * stride + i % stride
        buf[base + bit * stride] = keep[i].astype(full)
        buf[base + (1 - bit) * stride] = got[i].astype(full)
    count, share, cols = buf.shape
    turned[...] = buf[...].reshape(count * share, cols).T.astype(low)
    copy = pltpu.make_async_copy(turned, out.at[bits[here] ^ far], sem)
    copy.start()
    copy.wait()


def swap(block, axis, mask):
    return lax.ppermute(block, axis, [(i, i ^ mask) for i in range(lax.axis_size(axis))])


def masks_of(count):
    return [1 << b for b in range(count.bit_length() - 1)]


def pick(block, at):
    return lax.dynamic_index_in_dim(block, at, 1, keepdims=False)


def struct(dims, kind):
    return jax.ShapeDtypeStruct(dims, kind)


class Order:
    def __init__(self, masks):
        self.masks = masks
        left = sorted(masks)
        self.strides = []
        for mask in masks:
            self.strides.append(1 << left.index(mask))
            left.remove(mask)


def take(blocks, bit, stride):
    rest = blocks.shape[1:]
    blocks = blocks.reshape(-1, 2, stride, *rest)
    return lax.dynamic_index_in_dim(blocks, bit, 1, keepdims=False).reshape(-1, *rest)


def weave(own, got, bit, stride):
    rest = own.shape[1:]
    own, got = own.reshape(-1, 1, stride, *rest), got.reshape(-1, 1, stride, *rest)
    both = jnp.where(
        bit == 0, jnp.concatenate([own, got], 1), jnp.concatenate([got, own], 1)
    )
    return both.reshape(-1, *rest)


def shards(
    hidden_in, out_grad, seq_counts, segment_ids, proj, proj_master, proj_m, proj_v,
    down, down_master, down_m, down_v, vectors, vec_m, vec_v,
):
    group_count = lax.axis_size("dp")
    section = lax.axis_index("section")
    core, layer = section % 2, section // 2
    width = hidden_in.shape[1]
    seq_len = segment_ids.shape[1]
    slots = segment_ids.shape[0] // 2
    rows = slots * seq_len
    wide = proj.shape[2]
    at_first = layer == 0

    own_w = proj[0]
    other_w = swap(own_w, "section", 1)
    crossing = lax.dynamic_index_in_dim(down, 1 - layer, 0, keepdims=False)
    d2 = swap(crossing, "section", 2)
    whole_down, other_w = lax.optimization_barrier((down, other_w))
    d0 = lax.dynamic_index_in_dim(whole_down, layer, 0, keepdims=False)
    d1 = swap(d0, "section", 1)
    vec = lax.dynamic_index_in_dim(vectors, layer, 0, keepdims=False)

    own_in = lax.dynamic_slice_in_dim(hidden_in, core * rows, rows, 0)
    own_cot = lax.dynamic_slice_in_dim(out_grad, core * rows, rows, 0)
    docs = lax.dynamic_slice_in_dim(segment_ids, core * slots, slots, 0)
    doc_col = docs.reshape(rows, 1)
    live_count = lax.dynamic_index_in_dim(seq_counts[0], core, 0, keepdims=False)
    scal = jnp.stack([core, section, live_count]).astype(jnp.int32)

    def by_core(at_zero, at_one):
        return jnp.where(core == 0, at_zero, at_one)

    attn_w, feed_w = by_core(own_w, other_w), by_core(other_w, own_w)
    rows_low, rows_full = struct((rows, width), low), struct((rows, width), full)
    blocks, inverse = struct((4, rows, width), low), struct((rows, 128), full)
    residuals = [
        struct((rows, 3 * width), low), rows_low, rows_full, inverse, rows_low, blocks, blocks,
        rows_low, rows_full, inverse,
    ]

    kept_out = [pltpu.HBM(x.shape, x.dtype) for x in residuals]

    def scratch(shape):
        return pltpu.VMEM(shape.shape, shape.dtype)

    def hop(block, towards):
        route = [(0, 2), (1, 3)] if towards else [(2, 0), (3, 1)]
        return lax.ppermute(block, "section", route)

    first = call(
        first_kernel, kept_out[:7], (scal, own_in, docs, doc_col, vec, attn_w, feed_w),
        [smem] + [vmem] * 6, [*map(scratch, residuals[:7]), pltpu.SemaphoreType.DMA((7,))],
        out_specs=[hbm] * 7, limit=24, cost=6,
    )
    own_part = call(
        near_down_kernel, rows_full, (scal, first[4], first[5], vec, d0, d1), [smem] + [vmem] * 5,
        limit=16, cost=2,
    )
    d2, own_part = lax.optimization_barrier((d2, own_part))
    downs = (d0, d1, d2, swap(d2, "section", 1))
    own_part = call(
        next_down_kernel, rows_full, (scal, own_part, first[5], d2), [smem] + [vmem] * 3,
        limit=16, cost=2,
    )
    second = call(
        functools.partial(second_kernel, seq_len=seq_len),
        kept_out[7:], (scal, own_part, first[5], vec, downs[3]),
        [smem] + [vmem] * 4, [*map(scratch, residuals[7:]), pltpu.SemaphoreType.DMA((3,))],
        out_specs=[hbm] * 3, limit=16, cost=4,
    )
    arrived = hop(second[0], True)
    layer_in = jnp.where(at_first, own_in, arrived)
    ins = (scal, arrived, own_cot, docs, doc_col, vec, attn_w, feed_w, *downs, *first, *second)
    *kept, back_low = call(
        turn_kernel, [*kept_out, rows_low], ins,
        [smem] + [vmem] * 11 + [hbm] * 10,
        [
            *map(scratch, (*residuals, blocks, blocks, rows_low)),
            pltpu.VMEM((slots * HEAD_PAIRS, seq_len, 2 * seq_len), full),
            pltpu.SemaphoreType.DMA((10,)),
        ],
        out_specs=[hbm] * 10 + [vmem], limit=44, cost=25,
        aliases={len(ins) - 10 + i: i for i in range(10)},
    )
    qkv, ctx, n_one, r_one, h_one, act, slope, h_two, n_two, r_two = kept

    kept_left = (by_core(layer_in, h_one), by_core(ctx, h_one), by_core(h_one, h_two))
    sent_left = jnp.stack(
        [by_core(h_one, layer_in), by_core(h_one, ctx), by_core(h_two, h_one)]
    )
    got_left = swap(sent_left, "section", 1)
    act_pairs = act.reshape(2, 2, rows, width)
    act_kept = pick(act_pairs, core)
    act_got = swap(pick(act_pairs, 1 - core), "section", 1)

    masks = masks_of(group_count)
    index = lax.axis_index("dp")
    share = width // group_count
    half = group_count // 2
    bits = jnp.stack([(index // mask) % 2 for mask in masks] + [layer]).astype(jnp.int32)
    scatter = Order(masks)
    turned = masks[1:] + masks[:1]
    gathers = {
        name: Order(turned if name in (3,) else masks) for name in ("near", 0, 1, 2, 3, "far")
    }
    last = len(masks) - 1
    part = struct((half, share, width), low)

    def bit(mask):
        return (index // mask) % 2

    token = [jnp.zeros((8, 128), full)]

    def tie(*arrays):
        *arrays, token[0] = lax.optimization_barrier((*arrays, token[0]))
        return arrays if len(arrays) > 1 else arrays[0]

    db, dpre, dh_two, sums_two = call(
        functools.partial(back_second_kernel, seq_len=seq_len),
        [rows_low, blocks, rows_full, struct((8, width), full)],
        (
            scal, hop(back_low, False), vec, n_two, r_two, own_cot, downs[0], slope, *downs[1:],
            feed_w,
        ),
        [smem, vmem, vmem] + [hbm] * 9,
        (
            *map(scratch, (rows_full, inverse, rows_full, d0, blocks, d0, d0, d0, own_w)),
            pltpu.SemaphoreType.DMA((12,)),
        ),
        limit=58, cost=6,
    )
    keep, send, far = call(
        functools.partial(
            down_gradient, stride=scatter.strides[0], place=0, here=len(masks)
        ),
        [part, part, struct((group_count, share, width), low)],
        (bits, act_kept, act_got, db, swap(db, "section", 1)),
        [smem] + [vmem] * 4, cost=4,
    )
    terms = {"near": [keep]}
    dh_two, send, far = lax.optimization_barrier((dh_two, send, far))
    got = {"near": swap(send, "dp", masks[0])}
    kept_right, sent_right, dh_one, sums_one = call(
        back_first_kernel,
        [blocks, blocks, rows_full, struct((8, width), full)],
        (scal, dh_two, docs, doc_col, vec, n_one, r_one, qkv, dpre, attn_w),
        [smem] + [vmem] * 4 + [hbm] * 5,
        (
            *map(scratch, (rows_full, inverse, residuals[0], blocks, own_w, rows_low, blocks)),
            pltpu.SemaphoreType.DMA((6,)),
        ),
        limit=24, cost=9,
    )
    got_right = [swap(sent_right[k], "section", 1) for k in range(4)]
    kept_grad = by_core(dh_one, dh_two)
    got_grad = swap(by_core(dh_two, dh_one), "section", 1)
    proj_copy, down_copy, updated = [], [], {}

    def begin(k):
        flight.append(k)
        if k == "far":
            blocks = tie(far)
            terms[k] = [take(blocks, bit(masks[0]), scatter.strides[0])]
            send = take(blocks, 1 - bit(masks[0]), scatter.strides[0])
            got[k] = swap(tie(send), "dp", masks[0])
            return
        lhs = 0 if k < 3 else 1
        keep, send = call(
            functools.partial(weight_gradient, stride=scatter.strides[0], place=0),
            [part, part],
            (bits, kept_left[lhs], got_left, kept_right, tie(got_right[k])),
            [
                smem, vmem, pl.BlockSpec((None, rows, width), lambda _: (lhs, 0, 0)),
                pl.BlockSpec((None, rows, width), lambda _: (k, 0, 0)), vmem,
            ],
            grid=(1,),
        )
        terms[k] = [keep]
        got[k] = swap(tie(send), "dp", masks[0])

    def arrive(name, stage):
        terms[name].append(tie(got[name]))
        if stage:
            terms[name][:-1] = [
                take(x, bit(scatter.masks[stage]), scatter.strides[stage])
                for x in terms[name][:-1]
            ]

    def total_of(name):
        return sum(x.astype(full) for x in terms[name])[0]

    def scatter_step(stage):
        def step(name):
            arrive(name, stage)
            mask, stride = scatter.masks[stage + 1], scatter.strides[stage + 1]
            send = sum(take(x, 1 - bit(mask), stride).astype(full) for x in terms[name])
            got[name] = swap(tie(send.astype(low)), "dp", mask)

        return step

    def gather_start(name, payload):
        terms[name] = tie(payload)
        got[name] = swap(terms[name], "dp", gathers[name].masks[last])

    def down_step(name):
        arrive(name, last)
        grad = total_of(name) / group_count
        at = layer if name == "near" else 1 - layer
        held = [
            lax.dynamic_index_in_dim(jnp.swapaxes(x, 1, 2), at, 0, keepdims=False)
            for x in (down_master, down_m, down_v)
        ]
        new = adam_apply(*held, grad, weight_decay)
        updated[name] = (grad, *new)
        gather_start(name, new[0][None].astype(low))

    def proj_step(name):
        arrive(name, last)
        grad = total_of(name) / group_count
        cols = slice(name * width, (name + 1) * width)
        new = adam_apply(
            proj_master[0, :, cols], proj_m[0, :, cols], proj_v[0, :, cols], grad, weight_decay
        )
        updated[name] = (grad, *new)
        gather_start(name, new[0][None].astype(low))

    def woven(name, stage):
        mask, stride = gathers[name].masks[stage], gathers[name].strides[stage]
        return weave(terms[name], tie(got[name]), bit(mask), stride)

    def gather_step(stage):
        def step(name):
            terms[name] = tie(woven(name, stage))
            got[name] = swap(terms[name], "dp", gathers[name].masks[stage - 1])

        return step

    def copy_proj_step(name):
        ins, aliases = (bits, terms[name], tie(got[name])), {}
        if proj_copy:
            ins, aliases = (*ins, proj_copy.pop()), {3: 0}
        spec = pl.BlockSpec((group_count, share, width), lambda _: (0, 0, name))
        held = gathers[name]
        proj_copy.append(
            call(
                functools.partial(
                    copy_columns, stride=held.strides[0],
                    place=held.masks[0].bit_length() - 1,
                ),
                pltpu.HBM((group_count, share, wide), low), ins,
                [smem, vmem, vmem] + [anywhere] * len(aliases), out_specs=spec, aliases=aliases,
                grid=(1,),
            )
        )

    def copy_down_step(name):
        ins, aliases = (bits, terms[name], tie(got[name])), {}
        if down_copy:
            ins, aliases = (*ins, down_copy.pop()), {3: 0}
        held = gathers[name]
        down_copy.append(
            call(
                functools.partial(
                    copy_turned, stride=held.strides[0], place=held.masks[0].bit_length() - 1,
                    here=len(masks), far=int(name == "far"),
                ),
                pltpu.HBM((2, width, width), low), ins,
                [smem, vmem, vmem] + [anywhere] * len(aliases),
                (
                    pltpu.VMEM((group_count, share, width), full), pltpu.VMEM((width, width), low),
                    pltpu.SemaphoreType.DMA(()),
                ),
                out_specs=hbm, aliases=aliases,
            )
        )

    halvings = [scatter_step(stage) for stage in range(last)]
    doublings = [gather_step(stage) for stage in range(last, 0, -1)]
    todo = {
        name: halvings
        + [down_step if name in ("near", "far") else proj_step]
        + doublings
        + [copy_down_step if name in ("near", "far") else copy_proj_step]
        for name in gathers
    }
    flight = ["near"]

    def advance():
        name = flight.pop(0)
        todo[name].pop(0)(name)
        if todo[name]:
            flight.append(name)

    def by_layer(near, far):
        return jnp.where(at_first, jnp.stack([near, far]), jnp.stack([far, near]))

    sums = jnp.concatenate([sums_one[:5], sums_two[:7]], 0)
    sums = sums + swap(sums, "section", 1)
    vector_sums = [sums]

    def vector_step(mask):
        def step(name):
            vector_sums[0] = tie(vector_sums[0] + tie(got[name]))
            if mask:
                got[name] = swap(vector_sums[0], "dp", mask)
            else:
                got[name] = swap(vector_sums[0], "section", 2)

        return step

    def vector_last(name):
        updated[name] = by_layer(vector_sums[0], tie(got[name]))

    todo["vectors"] = [vector_step(mask) for mask in (*masks[1:], 0)] + [vector_last]
    begin(0)
    advance()
    far = swap(tie(far), "section", 2)
    for name in (1, 2, 3, 'far'):
        begin(name)
        if name == 1:
            got["vectors"] = swap(tie(vector_sums[0]), "dp", masks[0])
            flight.append("vectors")
        while flight[0] != name:
            advance()
    while flight:
        advance()

    vec_grad = updated["vectors"] / group_count
    vec_moments = adam_apply(vectors, vec_m, vec_v, vec_grad, 0.0)

    def in_order(kept, got):
        return by_core(jnp.concatenate([kept, got], 0), jnp.concatenate([got, kept], 0))[None]

    return (
        in_order(kept_left[2], got_left[2]),
        in_order(kept_grad, got_grad),
        *[jnp.concatenate([updated[k][i] for k in range(4)], 1)[None] for i in range(4)],
        proj_copy[0].reshape(1, width, wide),
        *[
            jnp.swapaxes(by_layer(updated["near"][i], updated["far"][i]), 1, 2) for i in range(4)
        ],
        down_copy[0],
        vec_grad,
        vec_moments[1],
        vec_moments[2],
    )


def solution(mesh):
    shared = P("section", "dp", None)
    split = P(None, "section", "dp")
    placed = (
        P("dp", None), P("dp", None), P("dp", None), P("dp", None),
        P("section", None, None), shared, shared, shared,
        P(None, "section", None), split, split, split, P(), P(), P(),
    )
    return jax.shard_map(
        shards,
        mesh=mesh,
        in_specs=placed,
        out_specs=(
            shared, shared, shared, shared, shared, shared,
            P("section", None, None), split, split, split, split,
            P(None, "section", None), P(), P(), P(),
        ),
        check_vma=False,
    )
```
